32 devices in a mesh: dp: 8 (over y, x, core), mp: 4 (over z).
Axes of the slice: x: 2, y: 2, z: 4, core: 2. Of those that a mesh axis runs over, the one named last changes fastest.
Arguments:
- block_input: float32 [16384, 1024], P(('dp', 'mp')), may hold values from -6 to 6
- lengths: int32 [8], P('dp'), may hold values from 1537 to 2048, as said below
- mixer_gain: float32 [1024], replicated, may hold values from 0.5 to 1.5
- mixer_shift: float32 [1024], replicated, may hold values from -1.25 to 1.25
- input_weight: bfloat16 [1024, 3, 1024], P(None, None, 'mp'), may hold values from -0.1875 to 0.1875
- input_bias: float32 [3, 1024], P(None, 'mp'), may hold values from -1.25 to 1.25
- conv_weight: float32 [3, 3, 1024], P(None, None, 'mp'), may hold values from -3.5 to 3.5
- conv_bias: float32 [3, 1024], P(None, 'mp'), may hold values from -1.25 to 1.25
- enter_weight: float32 [33, 64], replicated, may hold values from -3.5 to 3.5
- enter_bias: float32 [64], replicated, may hold values from -3.140625 to 3.140625
- middle_weight: float32 [64, 64], replicated, may hold values from -1.5 to 1.5
- middle_bias: float32 [64], replicated, may hold values from -3.140625 to 3.140625
- inner_weight: float32 [64, 64], replicated, may hold values from -1.5 to 1.5
- inner_bias: float32 [64], replicated, may hold values from -3.140625 to 3.140625
- frequency: float32 [64], replicated, may hold values from 0.5 to 1.5
- filter_weight: float32 [64, 1024], P(None, 'mp'), may hold values from -0.015625 to 0.015625
- skip_scale: float32 [1024], P('mp'), may hold values from -6 to 6
- output_weight: bfloat16 [1024, 1024], P('mp'), may hold values from -0.1875 to 0.1875
- output_bias: float32 [1024], replicated, may hold values from -1.25 to 1.25
- feed_gain: float32 [1024], replicated, may hold values from 0.5 to 1.5
- feed_shift: float32 [1024], replicated, may hold values from -1.25 to 1.25
- expand_weight: bfloat16 [1024, 4096], P(None, 'mp'), may hold values from -0.1875 to 0.1875
- expand_bias: float32 [4096], P('mp'), may hold values from -1.25 to 1.25
- reduce_weight: bfloat16 [4096, 1024], P('mp'), may hold values from -0.09375 to 0.09375
- reduce_bias: float32 [1024], replicated, may hold values from -1.25 to 1.25
- cotangent: float32 [16384, 1024], P(('dp', 'mp')), may hold values from -6 to 6
Outputs:
- result: float32 [16384, 1024], P(('dp', 'mp'))
- input_grad: float32 [16384, 1024], P(('dp', 'mp'))
- mixer_gain_grad: float32 [1024], replicated
- mixer_shift_grad: float32 [1024], replicated
- input_weight_grad: float32 [1024, 3, 1024], P(None, None, 'mp')
- input_bias_grad: float32 [3, 1024], P(None, 'mp')
- conv_weight_grad: float32 [3, 3, 1024], P(None, None, 'mp')
- conv_bias_grad: float32 [3, 1024], P(None, 'mp')
- enter_weight_grad: float32 [33, 64], replicated
- enter_bias_grad: float32 [64], replicated
- middle_weight_grad: float32 [64, 64], replicated
- middle_bias_grad: float32 [64], replicated
- inner_weight_grad: float32 [64, 64], replicated
- inner_bias_grad: float32 [64], replicated
- frequency_grad: float32 [64], replicated
- filter_weight_grad: float32 [64, 1024], P(None, 'mp')
- skip_scale_grad: float32 [1024], P('mp')
- output_weight_grad: float32 [1024, 1024], P('mp')
- output_bias_grad: float32 [1024], replicated
- feed_gain_grad: float32 [1024], replicated
- feed_shift_grad: float32 [1024], replicated
- expand_weight_grad: float32 [1024, 4096], P(None, 'mp')
- expand_bias_grad: float32 [4096], P('mp')
- reduce_weight_grad: float32 [4096, 1024], P('mp')
- reduce_bias_grad: float32 [1024], replicated
The draws below stay inside these ranges and needn't reach their ends.
Inputs may be any that keep to these rules, and one draw needn't show every extreme that they name: `lengths`: each sequence uses more than three quarters of its 2048 slots; in every draw some sequence uses all of them.
All inputs are finite; a program needn't handle non-finite values.
Results may differ from the reference program's by a relative error of at most 0.017.
Values may be sent and summed in bfloat16 or wider, within the bound.
No kernel may reach another device: no remote copies, remote signals or barrier semaphores. Data moves between devices by JAX's collectives and lax.ppermute only.
A program may use at most 192 MiB of HBM per device.

```python
import math
import jax
import jax.numpy as jnp
from jax import lax

D = 1024
FF = 4096
ORDER = 64
EMB = 33
SEQ_LEN = 2048
TOKENS = 16384
N_DP = 8


def draw_lengths(key, part):
    key = jax.random.fold_in(key, 11)
    key_cut, key_full = jax.random.split(key)
    length_cuts = jax.random.randint(key_cut, (N_DP,), 0, SEQ_LEN // 4)
    whole_group = jax.random.randint(key_full, (), 0, N_DP)
    length_cuts = jnp.where(jnp.arange(N_DP) == whole_group, 0, length_cuts)
    return (SEQ_LEN - length_cuts).astype(jnp.int32)


def shard_levels(rng, extent, pieces, low, high):
    level = 1.0
    for position, parts in pieces:
        steps = jax.random.uniform(jax.random.fold_in(jax.random.fold_in(rng, 6), position), (parts,), jnp.float32, low / len(pieces), high / len(pieces))
        level = level * jnp.repeat(jnp.exp(steps), extent[position] // parts).reshape((-1,) + (1,) * (len(extent) - 1 - position))
    return level


def normal_values(key, extent, width, bound, cuts=(), held_as=jnp.bfloat16):
    array = jax.random.normal(key, extent, jnp.float32) * width
    if len(cuts) > 0:
        array = shard_levels(key, extent, cuts, -0.22, 0.18) * array
    return jnp.clip(array, min=-bound, max=bound).astype(held_as)


def setup_inputs(seed: int = 0) -> dict:
    key_list = jax.random.split(jax.random.key(seed), 27)
    block_input = normal_values(key_list[0], (TOKENS, D), 1.0, 6.0, ((0, 32),), jnp.float32)
    lengths = draw_lengths(jax.random.fold_in(key_list[26], 71), 0)
    mixer_gain = jnp.clip(1.0 + 0.1 * jax.random.normal(key_list[2], (D,), jnp.float32), 0.5, 1.5)
    mixer_shift = normal_values(key_list[3], (D,), 0.2, 1.25, (), jnp.float32)
    input_weight = normal_values(key_list[4], (D, 3, D), D ** -0.5, 0.1875, ((2, 4),))
    input_bias = normal_values(key_list[5], (3, D), 0.2, 1.25, ((1, 4),), jnp.float32)
    conv_weight = normal_values(key_list[6], (3, 3, D), 3 ** -0.5, 3.5, ((2, 4),), jnp.float32)
    conv_bias = normal_values(key_list[7], (3, D), 0.2, 1.25, ((1, 4),), jnp.float32)
    enter_weight = normal_values(key_list[8], (EMB, ORDER), 3 ** -0.5, 3.5, (), jnp.float32)
    enter_bias = jnp.clip(jax.random.uniform(key_list[9], (ORDER,), jnp.float32, -3.140625, 3.140625), -3.140625, 3.140625)
    middle_weight = normal_values(key_list[10], (ORDER, ORDER), (ORDER // 4) ** -0.5, 1.5, (), jnp.float32)
    middle_bias = jnp.clip(jax.random.uniform(key_list[11], (ORDER,), jnp.float32, -3.140625, 3.140625), -3.140625, 3.140625)
    inner_weight = normal_values(key_list[12], (ORDER, ORDER), (ORDER // 4) ** -0.5, 1.5, (), jnp.float32)
    inner_bias = jnp.clip(jax.random.uniform(key_list[13], (ORDER,), jnp.float32, -3.140625, 3.140625), -3.140625, 3.140625)
    frequency = jnp.clip(1.0 + 0.1 * jax.random.normal(key_list[14], (ORDER,), jnp.float32), 0.5, 1.5)
    filter_weight = normal_values(key_list[15], (ORDER, D), (ORDER * SEQ_LEN) ** -0.5, 0.015625, ((1, 4),), jnp.float32)
    skip_scale = normal_values(key_list[16], (D,), 1.0, 6.0, ((0, 4),), jnp.float32)
    output_weight = normal_values(key_list[17], (D, D), D ** -0.5, 0.1875, ((0, 4),))
    output_bias = normal_values(key_list[18], (D,), 0.2, 1.25, (), jnp.float32)
    feed_gain = jnp.clip(1.0 + 0.1 * jax.random.normal(key_list[19], (D,), jnp.float32), 0.5, 1.5)
    feed_shift = normal_values(key_list[20], (D,), 0.2, 1.25, (), jnp.float32)
    expand_weight = normal_values(key_list[21], (D, FF), D ** -0.5, 0.1875, ((1, 4),))
    expand_bias = normal_values(key_list[22], (FF,), 0.2, 1.25, ((0, 4),), jnp.float32)
    reduce_weight = normal_values(key_list[23], (FF, D), FF ** -0.5, 0.09375, ((0, 4),))
    reduce_bias = normal_values(key_list[24], (D,), 0.2, 1.25, (), jnp.float32)
    cotangent = normal_values(key_list[25], (TOKENS, D), 1.0, 6.0, ((0, 32),), jnp.float32)
    return dict(block_input=block_input, lengths=lengths, mixer_gain=mixer_gain, mixer_shift=mixer_shift, input_weight=input_weight, input_bias=input_bias, conv_weight=conv_weight, conv_bias=conv_bias, enter_weight=enter_weight, enter_bias=enter_bias, middle_weight=middle_weight, middle_bias=middle_bias, inner_weight=inner_weight, inner_bias=inner_bias, frequency=frequency, filter_weight=filter_weight, skip_scale=skip_scale, output_weight=output_weight, output_bias=output_bias, feed_gain=feed_gain, feed_shift=feed_shift, expand_weight=expand_weight, expand_bias=expand_bias, reduce_weight=reduce_weight, reduce_bias=reduce_bias, cotangent=cotangent)


HIGHEST_MODE = lax.Precision.HIGHEST
EPSILON = 1e-05

@jax.custom_vjp
def low(v):
    return lax.optimization_barrier(v.astype(jnp.bfloat16)).astype(jnp.float32)

@jax.custom_vjp
def low_back(v):
    return v

def low_keep(v):
    return (low(v), None)

def low_pass(kept, grad):
    return (grad,)

def back_keep(v):
    return (v, None)

def back_low(kept, grad):
    return (low(grad),)
low.defvjp(low_keep, low_pass)
low_back.defvjp(back_keep, back_low)

def layer_norm(values_in, gain, shift):
    row_mean = lax.optimization_barrier(jnp.mean(values_in, axis=-1, keepdims=True))
    centred = values_in - row_mean
    variance = lax.optimization_barrier(jnp.mean(centred * centred, axis=-1, keepdims=True))
    return centred * lax.rsqrt(variance + EPSILON) * gain + shift

def short_conv(projected, conv_weight, conv_bias):
    one_back = jnp.pad(projected, ((1, 0), (0, 0), (0, 0)))[:-1]
    two_back = jnp.pad(projected, ((2, 0), (0, 0), (0, 0)))[:-2]
    return conv_weight[0] * projected + conv_weight[1] * one_back + conv_weight[2] * two_back + conv_bias

def position_features(total, emb_count):
    place = jnp.arange(total, dtype=jnp.float32)
    time_grid = place / (total - 1)
    bands = (emb_count - 1) // 2
    freq_grid = 0.0001 + jnp.arange(bands, dtype=jnp.float32) * ((bands - 1 - 0.0001) / (bands - 1))
    angles = 2.0 * math.pi / total * place[:, None] * freq_grid[None, :]
    return (jnp.concatenate([time_grid[:, None], jnp.cos(angles), -jnp.sin(angles)], axis=1), time_grid)

def decay_table(time_grid, channel_ids, channel_total):
    slowest = math.log(0.01) / 1.5
    fastest = math.log(0.01) / 0.3
    rates = jnp.abs(slowest + (fastest - slowest) * channel_ids.astype(jnp.float32) / (channel_total - 1))
    return jnp.exp(-time_grid[:, None] * rates[None, :])

def filter_bank(filter_weights, features, decay_rows):
    enter_weight, enter_bias, middle_weight, middle_bias, inner_weight, inner_bias, frequency, filter_weight = filter_weights
    hidden = jnp.sin(frequency * (jnp.dot(features, enter_weight, precision=HIGHEST_MODE) + enter_bias))
    hidden = jnp.sin(frequency * (jnp.dot(hidden, middle_weight, precision=HIGHEST_MODE) + middle_bias))
    hidden = jnp.sin(frequency * (jnp.dot(hidden, inner_weight, precision=HIGHEST_MODE) + inner_bias))
    return jnp.dot(hidden, filter_weight, precision=HIGHEST_MODE) * decay_rows

def long_conv(signal, filter_taps):
    total = 2 * signal.shape[0]
    spectrum = jnp.fft.rfft(signal, n=total, axis=0) * jnp.fft.rfft(filter_taps, n=total, axis=0)
    return jnp.fft.irfft(spectrum, n=total, axis=0)[:signal.shape[0]]

def mat_product(left, right):
    return jnp.dot(left, right, precision=HIGHEST_MODE, preferred_element_type=jnp.float32)

def layer(weights, group_rows, row_mask, features, decay_rows):
    mixer_gain, mixer_shift, input_weight, input_bias, conv_weight, conv_bias, enter_weight, enter_bias, middle_weight, middle_bias, inner_weight, inner_bias, frequency, filter_weight, skip_scale, output_weight, output_bias, feed_gain, feed_shift, expand_weight, expand_bias, reduce_weight, reduce_bias = weights
    length = group_rows.shape[0]
    feature_count = group_rows.shape[1]
    mixer_normed = low(layer_norm(group_rows, mixer_gain, mixer_shift))
    flat_weight = input_weight.reshape(feature_count, 3 * feature_count)
    projected = low_back(mat_product(mixer_normed, flat_weight).reshape(length, 3, feature_count) + input_bias)
    mixed_in = short_conv(projected, conv_weight, conv_bias)
    conv_input = low(mixed_in[:, 1] * mixed_in[:, 0])
    filter_weights = (enter_weight, enter_bias, middle_weight, middle_bias, inner_weight, inner_bias, frequency, filter_weight)
    taps_low = low(filter_bank(filter_weights, features, decay_rows))
    conv_out = low_back(long_conv(conv_input, taps_low) + skip_scale * conv_input)
    gated = low(row_mask * mixed_in[:, 2] * conv_out)
    hidden_res = group_rows + low_back(mat_product(gated, output_weight)) + output_bias
    feed_normed = low(layer_norm(hidden_res, feed_gain, feed_shift))
    pre_act = low_back(mat_product(feed_normed, expand_weight) + expand_bias)
    activated = low(jax.nn.gelu(pre_act, approximate=True))
    return hidden_res + low_back(mat_product(activated, reduce_weight)) + reduce_bias

def reference(block_input, lengths, mixer_gain, mixer_shift, input_weight, input_bias, conv_weight, conv_bias, enter_weight, enter_bias, middle_weight, middle_bias, inner_weight, inner_bias, frequency, filter_weight, skip_scale, output_weight, output_bias, feed_gain, feed_shift, expand_weight, expand_bias, reduce_weight, reduce_bias, cotangent):
    weights = tuple((weight_item.astype(jnp.float32) for weight_item in (mixer_gain, mixer_shift, input_weight, input_bias, conv_weight, conv_bias, enter_weight, enter_bias, middle_weight, middle_bias, inner_weight, inner_bias, frequency, filter_weight, skip_scale, output_weight, output_bias, feed_gain, feed_shift, expand_weight, expand_bias, reduce_weight, reduce_bias)))
    features, time_grid = position_features(SEQ_LEN, EMB)
    decay_rows = decay_table(time_grid, jnp.arange(D, dtype=jnp.int32), D)
    positions = jnp.arange(SEQ_LEN, dtype=jnp.int32)
    group_inputs = block_input.astype(jnp.float32).reshape(N_DP, SEQ_LEN, D)
    group_grads = cotangent.astype(jnp.float32).reshape(N_DP, SEQ_LEN, D)

    def group_step(totals, inputs):
        group_rows, grad_rows, seq_length = inputs
        row_mask = (positions < seq_length).astype(jnp.float32)[:, None]

        def forward(weight_set, rows_in):
            return layer(weight_set, rows_in, row_mask, features, decay_rows)
        group_out, backward = jax.vjp(forward, weights, group_rows)
        weight_grads, row_grad = backward(grad_rows)
        totals = jax.tree.map(lambda first_term, second_term: first_term + second_term, totals, weight_grads)
        return (totals, (group_out, row_grad))
    zero_grads = jax.tree.map(jnp.zeros_like, weights)
    totals, (outputs, row_grads) = lax.scan(group_step, zero_grads, (group_inputs, group_grads, lengths))
    return (outputs.reshape(TOKENS, D), row_grads.reshape(TOKENS, D), totals[0], totals[1], totals[2], totals[3], totals[4], totals[5], totals[6], totals[7], totals[8], totals[9], totals[10], totals[11], totals[12], totals[13], totals[14], totals[15], totals[16], totals[17], totals[18], totals[19], totals[20], totals[21], totals[22])
```

```python
import functools
import math

import jax
import jax.numpy as jnp
import ml_dtypes
import numpy as np
from jax import lax
from jax.experimental import pallas as pl
from jax.experimental.pallas import tpu as pltpu
from jax.sharding import PartitionSpec as P

HIGHEST_MODE = lax.Precision.HIGHEST
EPSILON = 1e-05
FIRST_FACTOR = 64
CHUNK = 16
F32 = jnp.float32
BF16 = jnp.bfloat16
VMEM_SPEC = pl.BlockSpec(memory_space=pltpu.VMEM)


def norm_parts(values_in):
    centred = values_in - jnp.mean(values_in, axis=-1, keepdims=True)
    variance = jnp.mean(centred * centred, axis=-1, keepdims=True)
    scale = lax.rsqrt(variance + EPSILON)
    return centred * scale, scale


def norm_back(normal, scale, gain, grad):
    inner = grad * gain
    part = scale * (
        inner
        - jnp.mean(inner, axis=-1, keepdims=True)
        - normal * jnp.mean(inner * normal, axis=-1, keepdims=True)
    )
    return part, jnp.sum(grad * normal, axis=0), jnp.sum(grad, axis=0)


def delayed(values_in, count):
    if count == 0:
        return values_in
    return jnp.pad(values_in, ((count, 0), (0, 0)))[:-count]


def advanced(values_in, count):
    if count == 0:
        return values_in
    return jnp.pad(values_in, ((0, count), (0, 0)))[count:]


def position_features(total, emb_count):
    place = jnp.arange(total, dtype=F32)
    time_grid = place / (total - 1)
    bands = (emb_count - 1) // 2
    freq_grid = 0.0001 + jnp.arange(bands, dtype=F32) * ((bands - 1 - 0.0001) / (bands - 1))
    angles = 2.0 * math.pi / total * place[:, None] * freq_grid[None, :]
    return (
        jnp.concatenate([time_grid[:, None], jnp.cos(angles), -jnp.sin(angles)], axis=1),
        time_grid,
    )


def decay_table(time_grid, channel_ids, channel_total):
    slowest = math.log(0.01) / 1.5
    fastest = math.log(0.01) / 0.3
    rates = jnp.abs(slowest + (fastest - slowest) * channel_ids.astype(F32) / (channel_total - 1))
    return jnp.exp(-time_grid[:, None] * rates[None, :])


def filter_bank(filter_weights, features, decay_rows):
    (
        enter_weight,
        enter_bias,
        middle_weight,
        middle_bias,
        inner_weight,
        inner_bias,
        frequency,
        filter_weight,
    ) = filter_weights
    hidden = jnp.sin(
        frequency * (jnp.dot(features, enter_weight, precision=HIGHEST_MODE) + enter_bias)
    )
    hidden = jnp.sin(
        frequency * (jnp.dot(hidden, middle_weight, precision=HIGHEST_MODE) + middle_bias)
    )
    hidden = jnp.sin(
        frequency * (jnp.dot(hidden, inner_weight, precision=HIGHEST_MODE) + inner_bias)
    )
    return jnp.dot(hidden, filter_weight, precision=HIGHEST_MODE) * decay_rows


def spectral_tables(seq_len):
    total = 2 * seq_len
    count1 = FIRST_FACTOR
    count2 = total // count1
    half = count1 // 2
    slot = np.arange(half)
    t1 = np.arange(half)
    t2 = np.arange(count2)
    k2 = np.arange(count2)
    angle = 2 * np.pi * slot[:, None] * t1[None, :] / count1
    first = np.zeros((half, 2, half))
    first[:, 0] = np.cos(angle)
    first[:, 1] = -np.sin(angle)
    first[0, 1] = (-1.0) ** t1
    last = np.zeros((half, half, 2))
    last[:, :, 0] = np.cos(angle.T) / seq_len
    last[:, :, 1] = -np.sin(angle.T) / seq_len
    last[:, 0, 0] = 1.0 / total
    last[:, 0, 1] = (-1.0) ** t1 / total
    mid = np.zeros((half, 2, count2, 2, count2))
    back = np.zeros((half, 2, count2, 2, count2))
    for s in range(1, half):
        turn = np.exp(-2j * np.pi * t2[None, :] * (s / total + k2[:, None] / count2))
        mid[s, 0, :, 0] = turn.real
        mid[s, 0, :, 1] = -turn.imag
        mid[s, 1, :, 0] = turn.imag
        mid[s, 1, :, 1] = turn.real
        undo = np.conj(turn).T
        back[s, 0, :, 0] = undo.real
        back[s, 0, :, 1] = -undo.imag
        back[s, 1, :, 0] = undo.imag
        back[s, 1, :, 1] = undo.real
    h2 = count2 // 2
    turn = np.exp(-2j * np.pi * t2[None, :] * k2[:h2, None] / count2)
    mid[0, 0, :h2, 0] = turn.real
    mid[0, 1, :h2, 0] = turn.imag
    mid[0, 1, 0, 0] = (-1.0) ** t2
    back[0, 0, :, 0, :h2] = 2 * turn.real.T
    back[0, 0, :, 1, :h2] = 2 * turn.imag.T
    back[0, 0, :, 0, 0] = 1.0
    back[0, 0, :, 1, 0] = (-1.0) ** t2
    turn = np.exp(-2j * np.pi * t2[None, :] * (half / total + k2[:h2, None] / count2))
    mid[0, 0, h2:, 1] = turn.real
    mid[0, 1, h2:, 1] = turn.imag
    back[0, 1, :, 0, h2:] = 2 * turn.real.T
    back[0, 1, :, 1, h2:] = 2 * turn.imag.T
    unit = np.eye(CHUNK)
    tables = (
        np.kron(first.reshape(count1, half), unit),
        mid.reshape(half, 2 * count2, 2 * count2),
        back.reshape(half, 2 * count2, 2 * count2),
        np.kron(last.reshape(half, count1), unit),
    )
    return tuple(jnp.asarray(v.astype(np.float32).astype(ml_dtypes.bfloat16)) for v in tables)


def times(left, right):
    return jnp.dot(left, right, preferred_element_type=F32)


def stage_first(first_ref, x_ref, y_ref):
    count1, count2, cols = y_ref.shape
    for j in range(count2 // CHUNK):
        rows = slice(CHUNK * j, CHUNK * (j + 1))
        block = x_ref[:, rows, :].reshape(count1 // 2 * CHUNK, cols)
        y_ref[:, rows, :] = times(first_ref[...], block).reshape(count1, CHUNK, cols).astype(BF16)


def stage_last(last_ref, z_ref, out_ref):
    count1, count2, cols = z_ref.shape
    for j in range(count2 // CHUNK):
        rows = slice(CHUNK * j, CHUNK * (j + 1))
        block = z_ref[:, rows, :].reshape(count1 * CHUNK, cols)
        values = times(last_ref[...], block).reshape(count1 // 2, CHUNK, cols)
        out_ref[:, rows, :] = values.astype(out_ref.dtype)


def spectral_product(s, left_re, left_im, right_re, right_im, sign):
    both_re = left_re * right_re
    both_im = left_im * right_im
    row = lax.broadcasted_iota(jnp.int32, both_re.shape, 0)
    real_row = (row == 0) & (s == 0)
    out_re = jnp.where(real_row, both_re, both_re - sign * both_im)
    out_im = jnp.where(real_row, both_im, left_im * right_re + sign * left_re * right_im)
    return jnp.concatenate([out_re, out_im], axis=0).astype(BF16)


def conv_kernel(
    first_ref, mid_ref, back_ref, last_ref, u_ref, t_ref, out_ref, su_ref, st_ref, y_ref, z_ref
):
    count1, count2, cols = y_ref.shape
    stage_first(first_ref, u_ref, y_ref)
    stage_first(first_ref, t_ref, z_ref)

    def slot_step(s, carry):
        pair = pl.ds(2 * s, 2)
        spec_u = times(mid_ref[s], y_ref[pair].reshape(2 * count2, cols))
        spec_t = times(mid_ref[s], z_ref[pair].reshape(2 * count2, cols))
        su_ref[pair] = spec_u.astype(BF16).reshape(2, count2, cols)
        st_ref[pair] = spec_t.astype(BF16).reshape(2, count2, cols)
        product = spectral_product(
            s, spec_u[:count2], spec_u[count2:], spec_t[:count2], spec_t[count2:], 1
        )
        z_ref[pair] = times(back_ref[s], product).astype(BF16).reshape(2, count2, cols)
        return carry

    lax.fori_loop(0, count1 // 2, slot_step, 0, unroll=2)
    stage_last(last_ref, z_ref, out_ref)


def conv_back_kernel(
    first_ref, mid_ref, back_ref, last_ref, g_ref, su_ref, st_ref, du_ref, dt_ref, y_ref, z_ref
):
    count1, count2, cols = y_ref.shape
    stage_first(first_ref, g_ref, y_ref)

    def slot_step(s, carry):
        pair = pl.ds(2 * s, 2)
        spec_g = times(mid_ref[s], y_ref[pair].reshape(2 * count2, cols))
        spec_u = su_ref[pair].astype(F32)
        spec_t = st_ref[pair].astype(F32)
        product = spectral_product(s, spec_g[:count2], spec_g[count2:], spec_t[0], spec_t[1], -1)
        y_ref[pair] = times(back_ref[s], product).astype(BF16).reshape(2, count2, cols)
        product = spectral_product(s, spec_g[:count2], spec_g[count2:], spec_u[0], spec_u[1], -1)
        z_ref[pair] = times(back_ref[s], product).astype(BF16).reshape(2, count2, cols)
        return carry

    lax.fori_loop(0, count1 // 2, slot_step, 0, unroll=2)
    stage_last(last_ref, y_ref, du_ref)
    stage_last(last_ref, z_ref, dt_ref)


def long_conv(tables, signal, taps):
    seq_len, cols = signal.shape
    count1 = FIRST_FACTOR
    count2 = 2 * seq_len // count1
    timed = (count1 // 2, count2, cols)
    spectral = jax.ShapeDtypeStruct((count1, count2, cols), BF16)
    out, spec_u, spec_t = pl.pallas_call(
        conv_kernel,
        out_shape=(jax.ShapeDtypeStruct(timed, F32), spectral, spectral),
        in_specs=[VMEM_SPEC] * 6,
        out_specs=(VMEM_SPEC,) * 3,
        scratch_shapes=[pltpu.VMEM((count1, count2, cols), BF16)] * 2,
        compiler_params=pltpu.CompilerParams(vmem_limit_bytes=40 << 20),
        cost_estimate=pl.CostEstimate(
            flops=8_000_000_000, bytes_accessed=14 << 20, transcendentals=0
        ),
        name="long_conv",
    )(*tables, signal.reshape(timed), taps.reshape(timed))
    return out.reshape(seq_len, cols), spec_u, spec_t


def long_conv_back(tables, grad, spec_u, spec_t):
    seq_len, cols = grad.shape
    count1 = FIRST_FACTOR
    count2 = 2 * seq_len // count1
    timed = (count1 // 2, count2, cols)
    grad_u, grad_t = pl.pallas_call(
        conv_back_kernel,
        out_shape=(jax.ShapeDtypeStruct(timed, F32), jax.ShapeDtypeStruct(timed, F32)),
        in_specs=[VMEM_SPEC] * 7,
        out_specs=(VMEM_SPEC,) * 2,
        scratch_shapes=[pltpu.VMEM((count1, count2, cols), BF16)] * 2,
        compiler_params=pltpu.CompilerParams(vmem_limit_bytes=40 << 20),
        cost_estimate=pl.CostEstimate(
            flops=8_000_000_000, bytes_accessed=14 << 20, transcendentals=0
        ),
        name="long_conv_back",
    )(*tables, grad.reshape(timed), spec_u, spec_t)
    return grad_u.reshape(seq_len, cols), grad_t.reshape(seq_len, cols)


def shift_mp(values_in, count):
    size = lax.axis_size("mp")
    return lax.ppermute(values_in, "mp", [(i, (i + count) % size) for i in range(size)])


def swap_dp(values_in, bit):
    size = lax.axis_size("dp")
    return lax.ppermute(values_in, "dp", [(i, i ^ (1 << bit)) for i in range(size)])


def bit_orders():
    bits = lax.axis_size("dp").bit_length() - 1
    high = list(range(1, bits))
    return [0] + high, [0] + high[::-1]


def after(values_in, *others):
    return lax.optimization_barrier((values_in,) + others)[0]


def gather_blocks(block, order):
    held = {0: block}
    for bit in order[::-1]:
        for offset in list(held):
            held[offset | (1 << bit)] = swap_dp(held[offset], bit)
    return held


def by_index(stacked):
    here = lax.axis_index("dp")
    size = stacked.shape[0]
    return jnp.concatenate(
        [lax.dynamic_slice_in_dim(stacked, here ^ i, 1, 0) for i in range(size)], axis=0
    )


def gather_dp(block, order):
    held = gather_blocks(block, order)
    return by_index(jnp.stack([held[m] for m in range(len(held))]))


def place_kernel(turned, here_ref, blocks_ref, out_ref):
    count, rows, _ = blocks_ref.shape
    here = here_ref[0]
    for i in range(count):
        block = blocks_ref[here ^ i].astype(F32)
        if turned:
            out_ref[:, i * rows : (i + 1) * rows] = block.T
        else:
            out_ref[i * rows : (i + 1) * rows, :] = block


def gather_total(total, order, turned=False):
    held = gather_blocks(total.astype(BF16), order)
    stacked = jnp.stack([held[m] for m in range(len(held))])
    count, rows, cols = stacked.shape
    if rows % 128 != 0:
        full = by_index(stacked).reshape(count * rows, cols)
        return (full.T if turned else full).astype(F32)
    shape = (cols, count * rows) if turned else (count * rows, cols)
    return pl.pallas_call(
        functools.partial(place_kernel, turned),
        out_shape=jax.ShapeDtypeStruct(shape, F32),
        in_specs=[pl.BlockSpec(memory_space=pltpu.SMEM), VMEM_SPEC],
        out_specs=VMEM_SPEC,
        compiler_params=pltpu.CompilerParams(vmem_limit_bytes=24 << 20),
        cost_estimate=pl.CostEstimate(flops=0, bytes_accessed=6 << 20, transcendentals=0),
        name="place_rows",
    )(jnp.full((1,), lax.axis_index("dp"), jnp.int32), stacked)


def scatter_dp(stacked, order):
    bits = len(order)
    here = lax.axis_index("dp")
    rest = stacked.shape[1:]
    held = stacked.reshape((2,) * bits + rest)
    left = list(range(bits))[::-1]
    for bit in order:
        axis = left.index(bit)
        own = (here >> bit) & 1
        away = lax.dynamic_index_in_dim(held, 1 - own, axis, keepdims=False).astype(BF16)
        keep = lax.dynamic_index_in_dim(held, own, axis, keepdims=False)
        held = keep.astype(F32) + swap_dp(away, bit).astype(F32)
        left.remove(bit)
        if len(left) > 0:
            held = held.astype(BF16)
    return held


def sum_dp(values_in):
    for bit in range(lax.axis_size("dp").bit_length() - 1):
        values_in = values_in + swap_dp(values_in, bit)
    return values_in


def sum_mp(values_in):
    total = values_in
    for k in range(1, lax.axis_size("mp")):
        total = total + shift_mp(values_in, k)
    return total


def pack(parts):
    flat = jnp.concatenate([p.reshape(-1) for p in parts])
    fill = -flat.shape[0] % 1024
    return jnp.pad(flat, (0, fill)).reshape(-1, 128)


def unpack(packed, parts):
    flat = packed.reshape(-1)
    out, start = [], 0
    for p in parts:
        out.append(flat[start : start + p.size].reshape(p.shape))
        start += p.size
    return out


def contract_rows(left, right):
    return lax.dot_general(left, right, (((0,), (0,)), ((), ())), preferred_element_type=F32)


def contract_cols(left, right):
    return lax.dot_general(left, right, (((1,), (1,)), ((), ())), preferred_element_type=F32)


def gelu_parts(value):
    factor = math.sqrt(2.0 / math.pi)
    square = value * value
    tanh_part = jnp.tanh(factor * value * (1.0 + 0.044715 * square))
    half = 0.5 * (1.0 + tanh_part)
    slope = half + 0.5 * value * (1.0 - tanh_part * tanh_part) * (
        factor * (1.0 + 3.0 * 0.044715 * square)
    )
    return value * half, slope


JOINT = 8
ROW_STEP = 32


def middle_kernel(*refs):
    (g0, g1, g2, g3, input_ref, cot_ref, out_weight_ref, vectors_ref, bias_ref) = refs[:9]
    weights = refs[9 : 11 + 4 * JOINT]
    (
        result_ref,
        hidden_grad_ref,
        d0,
        d1,
        d2,
        d3,
        act_ref,
        pre_grad_ref,
        normed_ref,
        mix_ref,
        out_low_ref,
        bias_grad_ref,
        sums_ref,
    ) = refs[11 + 4 * JOINT : 24 + 4 * JOINT]
    weight_ref, normal_ref, scale_ref, sems = refs[24 + 4 * JOINT :]
    expand_local, reduce_local = weights[:2]
    others = weights[2:]
    rows, width = input_ref.shape
    units = weight_ref.shape[4]
    per_step = 2 * 4 * units

    for j in range(JOINT):
        for kind, local in enumerate((expand_local, reduce_local)):
            for half in range(2):
                n = (kind * 2 + half) * 2
                pltpu.make_async_copy(
                    local.at[j, half], weight_ref.at[j, kind, half, 0], sems.at[j, n]
                ).start()
                pltpu.make_async_copy(
                    others[(kind * 2 + half) * JOINT + j],
                    weight_ref.at[j, kind, half, pl.ds(1, 3)],
                    sems.at[j, n + 1],
                ).start()

    mixed = times(g0[...], out_weight_ref[0])
    for k, g in enumerate((g1, g2, g3)):
        mixed = mixed + times(g[...], out_weight_ref[k + 1])
    result_ref[...] = input_ref[...] + mixed + vectors_ref[0:1]
    sums_ref[...] = jnp.zeros_like(sums_ref)

    def norm_step(i, carry):
        part = pl.ds(i * ROW_STEP, ROW_STEP)
        values = result_ref[part, :]
        normal, scale = norm_parts(values)
        normal_ref[part, :] = normal
        scale_ref[part, :] = scale
        normed_ref[part, :] = (normal * vectors_ref[1:2] + vectors_ref[2:3]).astype(BF16)
        cot = cot_ref[part, :]
        out_low_ref[part, :] = cot.astype(BF16)
        result_ref[part, :] = values + vectors_ref[3:4]
        hidden_grad_ref[part, :] = jnp.zeros_like(cot)
        sums_ref[0:1, :] += jnp.sum(cot, axis=0, keepdims=True)
        return carry

    lax.fori_loop(0, rows // ROW_STEP, norm_step, 0)

    def hidden_step(j, carry):
        for kind in range(2):
            for half in range(2):
                n = (kind * 2 + half) * 2
                one = weight_ref.at[j, kind, half, 0]
                pltpu.make_async_copy(one, one, sems.at[j, n]).wait()
                rest = weight_ref.at[j, kind, half, pl.ds(1, 3)]
                pltpu.make_async_copy(rest, rest, sems.at[j, n + 1]).wait()
        expand = weight_ref[j, 0].reshape(per_step, width)
        reduce = weight_ref[j, 1].reshape(per_step, width)
        value, slope = gelu_parts(contract_cols(normed_ref[...], expand) + bias_ref[j])
        value = value.astype(BF16)
        columns = pl.ds(pl.multiple_of(j * per_step, per_step), per_step)
        act_ref[:, columns] = value
        result_ref[...] += times(value, reduce)
        grad = (contract_cols(out_low_ref[...], reduce) * slope).astype(BF16)
        pre_grad_ref[:, columns] = grad
        bias_grad_ref[j] = jnp.sum(grad.astype(F32), axis=0, keepdims=True)
        hidden_grad_ref[...] += times(grad, expand)
        return carry

    lax.fori_loop(0, JOINT, hidden_step, 0)

    def back_step(i, carry):
        part = pl.ds(i * ROW_STEP, ROW_STEP)
        grad = hidden_grad_ref[part, :]
        normal = normal_ref[part, :]
        res_part, gain_sum, shift_sum = norm_back(normal, scale_ref[part, :], vectors_ref[1:2], grad)
        hidden_grad = cot_ref[part, :] + res_part
        hidden_grad_ref[part, :] = hidden_grad
        mix_ref[part, :] = hidden_grad.astype(BF16)
        sums_ref[1:2, :] += gain_sum[None]
        sums_ref[2:3, :] += shift_sum[None]
        sums_ref[3:4, :] += jnp.sum(hidden_grad, axis=0, keepdims=True)
        return carry

    lax.fori_loop(0, rows // ROW_STEP, back_step, 0)
    for k, d in enumerate((d0, d1, d2, d3)):
        d[...] = contract_cols(mix_ref[...], out_weight_ref[k]).astype(BF16)


def middle(gated, block_input, cotangent, out_weight, vectors, bias, local, others):
    rows, width = block_input.shape
    groups, channels, _ = out_weight.shape
    units = others[0].shape[1]
    hidden = JOINT * 2 * groups * units
    sh = jax.ShapeDtypeStruct
    any_spec = pl.BlockSpec(memory_space=pl.ANY)
    return pl.pallas_call(
        middle_kernel,
        out_shape=(
            sh((rows, width), F32),
            sh((rows, width), F32),
            *[sh((rows, channels), BF16)] * 4,
            sh((rows, hidden), BF16),
            sh((rows, hidden), BF16),
            sh((rows, width), BF16),
            sh((rows, width), BF16),
            sh((rows, width), BF16),
            sh((JOINT, 1, hidden // JOINT), F32),
            sh((8, width), F32),
        ),
        in_specs=[VMEM_SPEC] * 9 + [any_spec] * (2 + 4 * JOINT),
        out_specs=(VMEM_SPEC,) * 13,
        scratch_shapes=[
            pltpu.VMEM((JOINT, 2, 2, groups, units, width), BF16),
            pltpu.VMEM((rows, width), F32),
            pltpu.VMEM((rows, 1), F32),
            pltpu.SemaphoreType.DMA((JOINT, 8)),
        ],
        compiler_params=pltpu.CompilerParams(vmem_limit_bytes=58 << 20),
        cost_estimate=pl.CostEstimate(
            flops=20_000_000_000, bytes_accessed=45 << 20, transcendentals=rows * hidden
        ),
        name="middle",
    )(*gated, block_input, cotangent, out_weight, vectors, bias, *local, *others)


def per_device(
    block_input,
    lengths,
    mixer_gain,
    mixer_shift,
    input_weight,
    input_bias,
    conv_weight,
    conv_bias,
    enter_weight,
    enter_bias,
    middle_weight,
    middle_bias,
    inner_weight,
    inner_bias,
    frequency,
    filter_weight,
    skip_scale,
    output_weight,
    output_bias,
    feed_gain,
    feed_shift,
    expand_weight,
    expand_bias,
    reduce_weight,
    reduce_bias,
    cotangent,
):
    own_rows, width = block_input.shape
    channels = input_weight.shape[2]
    hidden = expand_weight.shape[1]
    mp_size = lax.axis_size("mp")
    dp_size = lax.axis_size("dp")
    mp_here = lax.axis_index("mp")
    dp_here = lax.axis_index("dp")
    seq_len = own_rows * mp_size
    order_a, order_b = bit_orders()
    bits = len(order_a)

    mixer_normal, mixer_scale = norm_parts(block_input)
    mixer_normed = (mixer_normal * mixer_gain + mixer_shift).astype(BF16)
    mixer_rows = lax.all_gather(mixer_normed, "mp", axis=0, tiled=True)

    share = hidden // dp_size
    units = share // 2
    inner = dp_size // JOINT
    out_share = channels // dp_size

    def offset_of(joint, inside):
        return (joint >> 2) | ((joint & 1) << 1) | ((joint & 2) << 1) | (inside << 3)

    offsets = [offset_of(j, i) for j in range(JOINT) for i in range(inner)]
    expand_turned = expand_weight.T
    local = []
    for weight in (expand_turned, reduce_weight):
        blocks = weight.reshape(dp_size, share, width)
        blocks = jnp.concatenate(
            [lax.dynamic_slice_in_dim(blocks, dp_here ^ m, 1, 0) for m in offsets], axis=0
        )
        blocks = blocks.reshape(JOINT, inner, 2, units, width).transpose(0, 2, 1, 3, 4)
        local.append(blocks.reshape(JOINT, 2, inner * units, width))
    expand_part = lax.dynamic_slice_in_dim(expand_turned, dp_here * share, share, 0)
    reduce_part = lax.dynamic_slice_in_dim(reduce_weight, dp_here * share, share, 0)
    output_part = lax.dynamic_slice_in_dim(output_weight, dp_here * out_share, out_share, 0)

    output_part = after(output_part, mixer_rows)
    output_pieces = jnp.stack([shift_mp(output_part, k) for k in range(1, mp_size)])
    output_other = gather_dp(output_pieces, order_a)
    others = []
    for part in (expand_part, reduce_part):
        part = after(part, mixer_rows)
        pieces = jnp.stack([shift_mp(part, k) for k in range(1, mp_size)])
        for half, order in enumerate((order_a, order_b)):
            held = gather_blocks(pieces[:, half * units : (half + 1) * units], order)
            for j in range(JOINT):
                block = jnp.stack([held[offset_of(j, i)] for i in range(inner)], axis=1)
                others.append(block.reshape(mp_size - 1, inner * units, width))
    all_bias = jnp.stack([expand_bias] + [shift_mp(expand_bias, k) for k in range(1, mp_size)])
    all_bias = by_index(all_bias.reshape(mp_size, dp_size, 2, units).transpose(1, 0, 2, 3))
    all_bias = jnp.stack([all_bias[m] for m in offsets])
    all_bias = all_bias.reshape(JOINT, inner, mp_size, 2, units).transpose(0, 3, 2, 1, 4)
    all_bias = all_bias.reshape(JOINT, 1, 2 * mp_size * inner * units)

    enter_flat = input_weight.reshape(width, 3 * channels)
    projected = times(mixer_rows, enter_flat) + input_bias.reshape(3 * channels)
    taps3 = conv_weight.reshape(3, 3 * channels)
    mixed_in = (
        taps3[0] * projected
        + taps3[1] * delayed(projected, 1)
        + taps3[2] * delayed(projected, 2)
        + conv_bias.reshape(3 * channels)
    )
    value_path = mixed_in[:, :channels]
    first_gate = mixed_in[:, channels : 2 * channels]
    second_gate = mixed_in[:, 2 * channels :]
    conv_input = (first_gate * value_path).astype(BF16)

    features, time_grid = position_features(seq_len, enter_weight.shape[0])
    channel_ids = mp_here * channels + jnp.arange(channels, dtype=jnp.int32)
    decay_rows = decay_table(time_grid, channel_ids, width)
    filter_weights = (
        enter_weight,
        enter_bias,
        middle_weight,
        middle_bias,
        inner_weight,
        inner_bias,
        frequency,
        filter_weight,
    )

    def local_bank(weight_set):
        return filter_bank(weight_set, features, decay_rows)

    filter_taps, bank_back = jax.vjp(local_bank, filter_weights)
    tables = spectral_tables(seq_len)
    long_out, spec_u, spec_t = long_conv(tables, conv_input, filter_taps.astype(BF16))
    conv_out = long_out + skip_scale * conv_input.astype(F32)
    positions = jnp.arange(seq_len, dtype=jnp.int32)
    row_mask = (positions < lengths[0]).astype(F32)[:, None]
    gated = (row_mask * second_gate * conv_out).astype(BF16)

    def to_rows(values_in):
        blocks = values_in.reshape(mp_size, own_rows, channels)
        pieces = []
        for k in range(mp_size):
            piece = lax.dynamic_index_in_dim(blocks, (mp_here + k) % mp_size, 0, keepdims=False)
            pieces.append(shift_mp(piece, k) if k > 0 else piece)
        return pieces

    def to_channels(pieces):
        arrived = jnp.stack([shift_mp(pieces[k], -k) if k > 0 else pieces[k] for k in range(mp_size)])
        blocks = [
            lax.dynamic_slice_in_dim(arrived, (z - mp_here) % mp_size, 1, 0) for z in range(mp_size)
        ]
        return jnp.concatenate(blocks, axis=0).reshape(seq_len, channels)

    gated_rows = to_rows(gated)
    out_weight = output_other.transpose(1, 0, 2, 3).reshape(mp_size - 1, channels, width)
    out_weight = jnp.concatenate([output_weight[None], out_weight])
    vectors = jnp.stack([output_bias, feed_gain, feed_shift, reduce_bias] + [reduce_bias] * 4)
    (
        result,
        hidden_grad,
        *gated_grads,
        activated,
        pre_grad,
        feed_normed,
        mix_low,
        out_low,
        bias_grad,
        sums,
    ) = middle(gated_rows, block_input, cotangent, out_weight, vectors, all_bias, local, others)
    gated_grad = to_channels(gated_grads)

    def reduce_groups(left, right, turned):
        halved = 2 * mp_size * inner * units * JOINT // 2
        shape = (2, 2, 2, mp_size) + (2,) * (bits - 3) + (units, width)
        keep = contract_rows(left[:, :halved], right).astype(BF16).reshape(shape)
        away = contract_rows(left[:, halved:], right).astype(BF16).reshape(shape)
        keep = (keep.astype(F32) + swap_dp(away, 0).astype(F32)).astype(BF16)
        pieces = []
        for half, order in enumerate((order_a, order_b)):
            held = keep[:, :, half]
            names = [2, 1, "group"] + list(range(3, bits))[::-1]
            for bit in order[1:]:
                axis = names.index(bit)
                away = lax.index_in_dim(held, 1, axis, keepdims=False)
                held = lax.index_in_dim(held, 0, axis, keepdims=False)
                held = (held.astype(F32) + swap_dp(away, bit).astype(F32)).astype(BF16)
                names.remove(bit)
            pieces.append(held)
        mine = jnp.concatenate(pieces, axis=1)
        total = mine[0].astype(F32)
        for k in range(1, mp_size):
            total = total + shift_mp(mine[k], -k).astype(F32)
        return gather_total(total, order_b if turned else order_a, turned)

    reduce_weight_grad = reduce_groups(activated, out_low, False)
    expand_weight_grad = reduce_groups(pre_grad, feed_normed, True)
    output_grads = jnp.stack([contract_rows(g, mix_low).astype(BF16) for g in gated_rows], axis=0)
    output_grads = output_grads.reshape(mp_size, dp_size, out_share, width).transpose(1, 0, 2, 3)
    mine = scatter_dp(output_grads, order_a)
    total = mine[0]
    for k in range(1, mp_size):
        total = total + shift_mp(mine[k].astype(BF16), -k).astype(F32)
    output_weight_grad = gather_dp(total.astype(BF16), order_a).astype(F32).reshape(channels, width)

    masked_grad = gated_grad.astype(F32) * row_mask
    second_grad = masked_grad * conv_out
    conv_grad_low = (masked_grad * second_gate).astype(BF16)
    conv_grad = conv_grad_low.astype(F32)
    skip_scale_grad = jnp.sum(conv_grad * conv_input.astype(F32), axis=0)
    conv_input_grad, taps_grad = long_conv_back(tables, conv_grad_low, spec_u, spec_t)
    conv_input_grad = conv_input_grad + skip_scale * conv_grad
    mixed_grad = jnp.concatenate(
        [conv_input_grad * first_gate, conv_input_grad * value_path, second_grad], axis=1
    )
    conv_weight_grad = jnp.stack(
        [jnp.sum(mixed_grad * delayed(projected, k), axis=0) for k in range(3)]
    )
    conv_bias_grad = jnp.sum(mixed_grad, axis=0)
    projected_low = (
        taps3[0] * mixed_grad
        + taps3[1] * advanced(mixed_grad, 1)
        + taps3[2] * advanced(mixed_grad, 2)
    ).astype(BF16)
    mixer_normed_grad = lax.psum_scatter(
        contract_cols(projected_low, enter_flat).astype(BF16),
        "mp",
        scatter_dimension=0,
        tiled=True,
    ).astype(F32)
    input_weight_grad = contract_rows(mixer_rows, projected_low)
    input_bias_grad = jnp.sum(projected_low.astype(F32), axis=0)
    input_weight_grad = scatter_dp(input_weight_grad.reshape(dp_size, -1, 3 * channels), order_a)
    input_weight_grad = gather_total(input_weight_grad, order_a).reshape(width, 3, channels)
    bank_grads = bank_back(taps_grad)[0]
    input_part, mixer_gain_grad, mixer_shift_grad = norm_back(
        mixer_normal, mixer_scale, mixer_gain, mixer_normed_grad
    )
    input_grad = hidden_grad + input_part

    bias_grad = bias_grad.reshape(JOINT, 2, mp_size, inner, units).transpose(0, 3, 2, 1, 4)
    bias_grad = bias_grad.reshape(dp_size, mp_size, share)
    bias_grad = by_index(jnp.stack([bias_grad[offsets.index(m)] for m in range(dp_size)]))
    bias_grad = bias_grad.transpose(1, 0, 2).reshape(mp_size, hidden)
    bias_grad = jnp.concatenate(
        [lax.dynamic_slice_in_dim(bias_grad, (mp_here - z) % mp_size, 1, 0) for z in range(mp_size)]
    )

    everywhere = [sums[3], sums[1], sums[2], sums[0], *bank_grads[:7], bias_grad]
    along_dp = [input_bias_grad, conv_weight_grad, conv_bias_grad, bank_grads[7], skip_scale_grad]
    packed_all = pack(everywhere)
    summed = sum_dp(jnp.concatenate([packed_all, pack(along_dp)]))
    along_dp = unpack(summed[packed_all.shape[0] :], along_dp)
    everywhere = unpack(sum_mp(summed[: packed_all.shape[0]]), everywhere)
    norm_sums = [mixer_gain_grad, mixer_shift_grad]
    norm_sums = unpack(sum_mp(sum_dp(pack(norm_sums))), norm_sums)
    expand_bias_grad = lax.dynamic_index_in_dim(everywhere[11], mp_here, 0, keepdims=False)
    return (
        result,
        input_grad,
        norm_sums[0],
        norm_sums[1],
        input_weight_grad,
        along_dp[0].reshape(3, channels),
        along_dp[1].reshape(3, 3, channels),
        along_dp[2].reshape(3, channels),
        *everywhere[4:11],
        along_dp[3],
        along_dp[4],
        output_weight_grad,
        everywhere[0],
        everywhere[1],
        everywhere[2],
        expand_weight_grad,
        expand_bias_grad,
        reduce_weight_grad,
        everywhere[3],
    )


ROWS = P(("dp", "mp"), None)
FIRST = P("mp", None)
SECOND = P(None, "mp")
THIRD = P(None, None, "mp")


def solution(mesh):
    return jax.shard_map(
        per_device,
        mesh=mesh,
        in_specs=(
            ROWS, P("dp"), P(), P(), THIRD, SECOND, THIRD, SECOND,
            P(), P(), P(), P(), P(), P(), P(), SECOND,
            P("mp"), FIRST, P(), P(), P(), SECOND, P("mp"), FIRST, P(), ROWS,
        ),
        out_specs=(
            ROWS, ROWS, P(), P(), THIRD, SECOND, THIRD, SECOND,
            P(), P(), P(), P(), P(), P(), P(), SECOND,
            P("mp"), FIRST, P(), P(), P(), SECOND, P("mp"), FIRST, P(),
        ),
        check_vma=False,
    )
```

```python
import functools
import math

import jax
import jax.numpy as jnp
import ml_dtypes
import numpy as np
from jax import lax
from jax.experimental import pallas as pl
from jax.experimental.pallas import tpu as pltpu
from jax.sharding import PartitionSpec as P

HIGHEST_MODE = lax.Precision.HIGHEST
EPSILON = 1e-05
FIRST_FACTOR = 64
CHUNK = 16
F32 = jnp.float32
BF16 = jnp.bfloat16
VMEM_SPEC = pl.BlockSpec(memory_space=pltpu.VMEM)
SMEM_SPEC = pl.BlockSpec(memory_space=pltpu.SMEM)
ANY_SPEC = pl.BlockSpec(memory_space=pl.ANY)


def norm_parts(values_in):
    centred = values_in - jnp.mean(values_in, axis=-1, keepdims=True)
    variance = jnp.mean(centred * centred, axis=-1, keepdims=True)
    scale = lax.rsqrt(variance + EPSILON)
    return centred * scale, scale


def norm_back(normal, scale, gain, grad):
    inner = grad * gain
    part = scale * (
        inner
        - jnp.mean(inner, axis=-1, keepdims=True)
        - normal * jnp.mean(inner * normal, axis=-1, keepdims=True)
    )
    return part, jnp.sum(grad * normal, axis=0), jnp.sum(grad, axis=0)


FEATURE_ROWS = 40
TAP_STEP = 256


def position_features(total, emb_count):
    place = np.arange(total, dtype=np.float64)
    bands = (emb_count - 1) // 2
    freq_grid = 1e-4 + np.arange(bands) * ((bands - 1 - 1e-4) / (bands - 1))
    angles = 2.0 * math.pi / total * freq_grid[:, None] * place[None, :]
    rows = np.concatenate([place[None] / (total - 1), np.cos(angles), -np.sin(angles)])
    rows = np.pad(rows, ((0, FEATURE_ROWS - emb_count), (0, 0)))
    return jnp.asarray(rows.astype(np.float32))


def exact(left, right, left_dim, right_dim):
    dims = (((left_dim,), (right_dim,)), ((), ()))
    return lax.dot_general(
        left, right, dims, precision=HIGHEST_MODE, preferred_element_type=F32
    )


def decay_block(first_row, rows, channels, seq_len, channel_total, group):
    slowest = math.log(0.01) / 1.5
    fastest = math.log(0.01) / 0.3
    row = lax.broadcasted_iota(jnp.int32, (rows, channels), 0) + first_row
    channel = lax.broadcasted_iota(jnp.int32, (rows, channels), 1) + group * channels
    rates = jnp.abs(slowest + (fastest - slowest) * channel.astype(F32) / (channel_total - 1))
    return jnp.exp(-(row.astype(F32) / (seq_len - 1)) * rates)


def filter_kernel(
    channel_total, here_ref, features_ref, enter_ref, middle_ref, inner_ref, columns_ref, filter_ref, *outs
):
    taps_ref, value_ref, sine_ref, cosine_ref = outs
    seq_len, channels = taps_ref.shape
    frequency = columns_ref[:, 3:4]
    hidden = features_ref[...]
    for n, weight_ref in enumerate((enter_ref, middle_ref, inner_ref)):
        value = exact(weight_ref[...], hidden, 0, 0) + columns_ref[:, n : n + 1]
        value_ref[n] = value
        hidden = jnp.sin(frequency * value)
        sine_ref[n] = hidden
        cosine_ref[n] = jnp.cos(frequency * value)
    for start in range(0, seq_len, TAP_STEP):
        rows = slice(start, start + TAP_STEP)
        decay = decay_block(start, TAP_STEP, channels, seq_len, channel_total, here_ref[1])
        taps = exact(sine_ref[2, :, rows], filter_ref[...], 0, 0)
        taps_ref[rows, :] = (taps * decay).astype(BF16)


def filter_back_kernel(
    channel_total,
    here_ref,
    features_ref,
    middle_ref,
    inner_ref,
    columns_ref,
    filter_ref,
    value_ref,
    sine_ref,
    cosine_ref,
    grad_ref,
    packed_ref,
    filter_grad_ref,
    hidden_ref,
):
    seq_len, channels = grad_ref.shape
    units = filter_ref.shape[0]
    frequency = columns_ref[:, 3:4]
    filter_grad_ref[...] = jnp.zeros_like(filter_grad_ref)
    for start in range(0, seq_len, TAP_STEP):
        rows = slice(start, start + TAP_STEP)
        decay = decay_block(start, TAP_STEP, channels, seq_len, channel_total, here_ref[1])
        grad = grad_ref[rows, :] * decay
        filter_grad_ref[...] += exact(sine_ref[2, :, rows], grad, 1, 0)
        hidden_ref[:, rows] = exact(filter_ref[...], grad, 1, 1)
    packed_ref[...] = jnp.zeros_like(packed_ref)
    grad = hidden_ref[...]
    frequency_grad = jnp.zeros((units, 1), F32)
    for n in (2, 1, 0):
        inside = grad * cosine_ref[n]
        frequency_grad += jnp.sum(inside * value_ref[n], axis=1, keepdims=True)
        inside = inside * frequency
        packed_ref[:, 3 * units + n : 3 * units + n + 1] = jnp.sum(inside, axis=1, keepdims=True)
        below = features_ref[...] if n == 0 else sine_ref[n - 1]
        packed_ref[: below.shape[0], n * units : (n + 1) * units] = exact(below, inside, 1, 1)
        if n > 0:
            grad = exact((middle_ref, inner_ref)[n - 1][...], inside, 1, 0)
    packed_ref[:, 3 * units + 3 : 3 * units + 4] = frequency_grad


def spectral_tables(seq_len):
    total = 2 * seq_len
    count1 = FIRST_FACTOR
    count2 = total // count1
    half = count1 // 2
    slot = np.arange(half)
    t1 = np.arange(half)
    t2 = np.arange(count2)
    k2 = np.arange(count2)
    angle = 2 * np.pi * slot[:, None] * t1[None, :] / count1
    first = np.zeros((half, 2, half))
    first[:, 0] = np.cos(angle)
    first[:, 1] = -np.sin(angle)
    first[0, 1] = (-1.0) ** t1
    last = np.zeros((half, half, 2))
    last[:, :, 0] = np.cos(angle.T) / seq_len
    last[:, :, 1] = -np.sin(angle.T) / seq_len
    last[:, 0, 0] = 1.0 / total
    last[:, 0, 1] = (-1.0) ** t1 / total
    mid = np.zeros((half, 2, count2, 2, count2))
    back = np.zeros((half, 2, count2, 2, count2))
    for s in range(1, half):
        turn = np.exp(-2j * np.pi * t2[None, :] * (s / total + k2[:, None] / count2))
        mid[s, 0, :, 0] = turn.real
        mid[s, 0, :, 1] = -turn.imag
        mid[s, 1, :, 0] = turn.imag
        mid[s, 1, :, 1] = turn.real
        undo = np.conj(turn).T
        back[s, 0, :, 0] = undo.real
        back[s, 0, :, 1] = -undo.imag
        back[s, 1, :, 0] = undo.imag
        back[s, 1, :, 1] = undo.real
    h2 = count2 // 2
    turn = np.exp(-2j * np.pi * t2[None, :] * k2[:h2, None] / count2)
    mid[0, 0, :h2, 0] = turn.real
    mid[0, 1, :h2, 0] = turn.imag
    mid[0, 1, 0, 0] = (-1.0) ** t2
    back[0, 0, :, 0, :h2] = 2 * turn.real.T
    back[0, 0, :, 1, :h2] = 2 * turn.imag.T
    back[0, 0, :, 0, 0] = 1.0
    back[0, 0, :, 1, 0] = (-1.0) ** t2
    turn = np.exp(-2j * np.pi * t2[None, :] * (half / total + k2[:h2, None] / count2))
    mid[0, 0, h2:, 1] = turn.real
    mid[0, 1, h2:, 1] = turn.imag
    back[0, 1, :, 0, h2:] = 2 * turn.real.T
    back[0, 1, :, 1, h2:] = 2 * turn.imag.T
    unit = np.eye(CHUNK)
    tables = (
        np.kron(first.reshape(count1, half), unit),
        mid.reshape(half, 2 * count2, 2 * count2),
        back.reshape(half, 2 * count2, 2 * count2),
        np.kron(last.reshape(half, count1), unit),
    )
    return tuple(jnp.asarray(v.astype(np.float32).astype(ml_dtypes.bfloat16)) for v in tables)


def times(left, right):
    return jnp.dot(left, right, preferred_element_type=F32)


def stage_first(first_ref, x_ref, y_ref):
    count1, count2, cols = y_ref.shape
    for j in range(count2 // CHUNK):
        rows = slice(CHUNK * j, CHUNK * (j + 1))
        block = x_ref[:, rows, :].reshape(count1 // 2 * CHUNK, cols)
        y_ref[:, rows, :] = times(first_ref[...], block).reshape(count1, CHUNK, cols).astype(BF16)


def stage_last(last_ref, z_ref, out_ref):
    count1, count2, cols = z_ref.shape
    for j in range(count2 // CHUNK):
        rows = slice(CHUNK * j, CHUNK * (j + 1))
        block = z_ref[:, rows, :].reshape(count1 * CHUNK, cols)
        values = times(last_ref[...], block).reshape(count1 // 2, CHUNK, cols)
        out_ref[:, rows, :] = values.astype(out_ref.dtype)


def spectral_product(s, left_re, left_im, right_re, right_im, sign):
    both_re = left_re * right_re
    both_im = left_im * right_im
    row = lax.broadcasted_iota(jnp.int32, both_re.shape, 0)
    real_row = (row == 0) & (s == 0)
    out_re = jnp.where(real_row, both_re, both_re - sign * both_im)
    out_im = jnp.where(real_row, both_im, left_im * right_re + sign * left_re * right_im)
    return jnp.concatenate([out_re, out_im], axis=0).astype(BF16)


def conv_kernel(
    first_ref, mid_ref, back_ref, last_ref, u_ref, t_ref, out_ref, su_ref, st_ref, y_ref, z_ref
):
    count1, count2, cols = y_ref.shape
    stage_first(first_ref, u_ref, y_ref)
    stage_first(first_ref, t_ref, z_ref)

    def slot_step(s, carry):
        pair = pl.ds(2 * s, 2)
        spec_u = times(mid_ref[s], y_ref[pair].reshape(2 * count2, cols))
        spec_t = times(mid_ref[s], z_ref[pair].reshape(2 * count2, cols))
        su_ref[pair] = spec_u.astype(BF16).reshape(2, count2, cols)
        st_ref[pair] = spec_t.astype(BF16).reshape(2, count2, cols)
        product = spectral_product(
            s, spec_u[:count2], spec_u[count2:], spec_t[:count2], spec_t[count2:], 1
        )
        z_ref[pair] = times(back_ref[s], product).astype(BF16).reshape(2, count2, cols)
        return carry

    lax.fori_loop(0, count1 // 2, slot_step, 0, unroll=2)
    stage_last(last_ref, z_ref, out_ref)


def conv_back_kernel(
    first_ref, mid_ref, back_ref, last_ref, g_ref, su_ref, st_ref, *refs
):
    du_ref, dt_ref, y_ref, z_ref, x_ref = refs
    count1, count2, cols = y_ref.shape
    stage_first(first_ref, g_ref, y_ref)

    def slot_step(s, carry):
        pair = pl.ds(2 * s, 2)
        spec_g = times(mid_ref[s], y_ref[pair].reshape(2 * count2, cols))
        spec_u = su_ref[pair].astype(F32)
        spec_t = st_ref[pair].astype(F32)
        product = spectral_product(s, spec_g[:count2], spec_g[count2:], spec_t[0], spec_t[1], -1)
        y_ref[pair] = times(back_ref[s], product).astype(BF16).reshape(2, count2, cols)
        product = spectral_product(s, spec_g[:count2], spec_g[count2:], spec_u[0], spec_u[1], -1)
        z_ref[pair] = times(back_ref[s], product).astype(BF16).reshape(2, count2, cols)
        return carry

    lax.fori_loop(0, count1 // 2, slot_step, 0, unroll=2)
    stage_last(last_ref, y_ref, x_ref)
    stage_last(last_ref, z_ref, dt_ref)
    groups, rows, _ = du_ref.shape
    rows -= CHUNK
    step = count1 // 2 // groups
    for place in range(groups):
        block = x_ref[place * step : (place + 1) * step]
        du_ref[place, :rows, :] = block.reshape(rows, cols)
        du_ref[place, rows:, :] = x_ref[(place + 1) % groups * step, :CHUNK, :]


def kernel_call(kernel, name, outs, in_specs, scratch, flops, size, limit, args):
    return pl.pallas_call(
        kernel,
        out_shape=tuple(jax.ShapeDtypeStruct(shape, dtype) for shape, dtype in outs),
        in_specs=in_specs,
        out_specs=(VMEM_SPEC,) * len(outs),
        scratch_shapes=scratch,
        compiler_params=pltpu.CompilerParams(vmem_limit_bytes=limit << 20),
        cost_estimate=pl.CostEstimate(flops=flops, bytes_accessed=size << 20, transcendentals=0),
        name=name,
    )(*args)


def long_conv(tables, signal, taps):
    seq_len, cols = taps.shape
    count1 = FIRST_FACTOR
    count2 = 2 * seq_len // count1
    timed = (count1 // 2, count2, cols)
    spectral = (count1, count2, cols)
    out, spec_u, spec_t = kernel_call(
        conv_kernel,
        "long_conv",
        [(timed, BF16), (spectral, BF16), (spectral, BF16)],
        [VMEM_SPEC] * 6,
        [pltpu.VMEM(spectral, BF16)] * 2,
        9_000_000_000,
        14,
        40,
        (*tables, signal.reshape(timed), taps.reshape(timed)),
    )
    return out.reshape(signal.shape), spec_u, spec_t


def long_conv_back(tables, grad, spec_u, spec_t):
    groups, rows, cols = grad.shape
    count1 = FIRST_FACTOR
    count2 = 2 * groups * rows // count1
    timed = (count1 // 2, count2, cols)
    spectral = (count1, count2, cols)
    grad_u, grad_t = kernel_call(
        conv_back_kernel,
        "long_conv_back",
        [((groups, rows + CHUNK, cols), BF16), (timed, F32)],
        [VMEM_SPEC] * 7,
        [pltpu.VMEM(spectral, BF16)] * 2 + [pltpu.VMEM(timed, BF16)],
        9_000_000_000,
        14,
        40,
        (*tables, grad.reshape(timed), spec_u, spec_t),
    )
    return grad_u, grad_t.reshape(groups * rows, cols)


def shift_mp(values_in, count):
    size = lax.axis_size("mp")
    return lax.ppermute(values_in, "mp", [(i, (i + count) % size) for i in range(size)])


def swap_dp(values_in, bit):
    size = lax.axis_size("dp")
    return lax.ppermute(values_in, "dp", [(i, i ^ (1 << bit)) for i in range(size)])


def bit_orders():
    bits = lax.axis_size("dp").bit_length() - 1
    high = list(range(1, bits))
    return [0] + high, [0] + high[::-1]


def after(values_in, *others):
    return lax.optimization_barrier((values_in,) + others)[0]


def gather_offsets(half):
    first, second = ((4, 2), (2, 4))[half]
    return [(0, first), (second, first | second), (1, first | 1), (second | 1, first | second | 1)]


def gather_start(block, half, *beside):
    bit = bit_orders()[half][2]
    return jnp.stack([after(block, *beside) if beside else block, swap_dp(block, bit)])


def gather_rest(pair, half, *beside):
    others = swap_dp(pair, bit_orders()[half][1])
    if beside:
        others = after(others, *beside)
    return [pair, others, swap_dp(pair, 0), swap_dp(others, 0)]


def split_blocks(pieces, axis, rows, *beside):
    out = []
    for half in range(2):
        part = lax.slice_in_dim(pieces, half * rows, (half + 1) * rows, axis=axis)
        out.extend(gather_rest(gather_start(part, half), half, *beside))
    return out


def add_across(part, bit, *beside):
    keep = after(part[0], *beside) if beside else part[0]
    return (keep.astype(F32) + swap_dp(part[1], bit).astype(F32)).astype(BF16)


def sum_groups(mine):
    total = mine[0].astype(F32)
    for k in range(1, lax.axis_size("mp")):
        total = total + shift_mp(mine[k], -k).astype(F32)
    return total


def own_group(grads):
    return lax.psum(sum_groups(grads), "dp")


def each_block(here, blocks):
    for half in range(2):
        for n, offsets in enumerate(gather_offsets(half)):
            for i, offset in enumerate(offsets):
                yield blocks[4 * half + n].at[i], half, here ^ offset


def place_feed_kernel(here_ref, *refs):
    *blocks, expand_ref, reduce_ref = refs
    share = blocks[0].shape[1]
    for block, half, index in each_block(here_ref[0], blocks):
        place = pl.ds(pl.multiple_of(index * share, share), share)
        if half == 0:
            expand_ref[:, place] = block[...].astype(F32).T
        else:
            reduce_ref[place, :] = block[...].astype(F32)


def place_input_kernel(here_ref, *refs):
    *blocks, input_ref, output_ref, full_ref = refs
    rows = blocks[0].shape[2]
    parts = full_ref.shape[0]
    for block, half, index in each_block(here_ref[0], blocks):
        place = pl.ds(pl.multiple_of((index * 2 + half) * rows, rows), rows)
        full_ref[:, place, :] = block[:parts].astype(F32)
        output_ref[place, :] = block[parts].astype(F32)
    for p in range(parts):
        input_ref[p] = full_ref[p].T


def sum_dp(values_in):
    for bit in range(lax.axis_size("dp").bit_length() - 1):
        values_in = values_in + swap_dp(values_in, bit)
    return values_in


def contract_rows(left, right):
    return lax.dot_general(left, right, (((0,), (0,)), ((), ())), preferred_element_type=F32)


def contract_cols(left, right):
    return lax.dot_general(left, right, (((1,), (1,)), ((), ())), preferred_element_type=F32)


def gelu_parts(value):
    factor = math.sqrt(2.0 / math.pi)
    square = value * value
    tanh_part = jnp.tanh(factor * value * (1.0 + 0.044715 * square))
    half = 0.5 * (1.0 + tanh_part)
    slope = half + 0.5 * value * (1.0 - tanh_part * tanh_part) * (
        factor * (1.0 + 3.0 * 0.044715 * square)
    )
    return value * half, slope


ROW_STEP = 32
SMALL_ROWS = 32


def fold_rows(wide_ref, narrow_ref):
    channels = narrow_ref.shape[1]
    for i in range(wide_ref.shape[1] // channels):
        narrow_ref[8 * i : 8 * i + 8, :] = wide_ref[:, i * channels : (i + 1) * channels]


def unfold_rows(narrow):
    rows, channels = narrow.shape
    return narrow.reshape(rows // 8, 8, channels).transpose(1, 0, 2).reshape(8, -1)


def store_grad(refs, k, part, here, values):
    rows = values.shape[0] // 8
    for i in range(4):
        bit1, bit2 = (i & 1) ^ (here >> 1 & 1), (i >> 1) ^ (here >> 2)
        first, second = (bit2, bit1) if k < 2 else (bit1, bit2)
        pair = [values[(2 * i + n) * rows : (2 * i + n + 1) * rows].astype(BF16) for n in range(2)]
        even = here & 1 == 0
        refs[0][k // 2, first, second, part] = jnp.where(even, pair[0], pair[1])
        refs[1][k // 2, first, second, part] = jnp.where(even, pair[1], pair[0])


def start_input_weights(here_ref, local, blocks, weight_ref, sem):
    others = pl.ds(1, weight_ref.shape[0] - 1)
    pltpu.make_async_copy(local, weight_ref.at[0], sem).start()
    if len(blocks) == 1:
        pltpu.make_async_copy(blocks[0], weight_ref.at[others], sem).start()
        return
    rows = blocks[0].shape[3]
    for block, half, index in each_block(here_ref[0], blocks):
        start = pl.multiple_of((index * 2 + half) * rows, rows)
        pltpu.make_async_copy(block, weight_ref.at[others, :, pl.ds(start, rows)], sem).start()


def group_at(here_ref, k, groups):
    return lax.rem(here_ref[1] + (groups - k), groups)


def wait_whole(ref, sem):
    pltpu.make_async_copy(ref, ref, sem).wait()


def enter_kernel(count, here_ref, input_ref, halo_ref, vectors_ref, small_ref, local_ref, *refs):
    blocks = refs[:count]
    conv_input_ref, second_ref, gates_ref, projected_ref, normed_ref = refs[count : count + 5]
    weight_ref, rows_ref, sem = refs[count + 5 :]
    rows = input_ref.shape[0]
    groups, _, channels = conv_input_ref.shape
    start_input_weights(here_ref, local_ref, blocks, weight_ref, sem)

    def normed(values):
        return (norm_parts(values)[0] * vectors_ref[0:1] + vectors_ref[1:2]).astype(BF16)

    rows_ref[:CHUNK, :] = normed(halo_ref[...])

    def norm_step(i, carry):
        start = pl.multiple_of(i * ROW_STEP, ROW_STEP)
        values = normed(input_ref[pl.ds(start, ROW_STEP), :])
        normed_ref[pl.ds(start, ROW_STEP), :] = values
        rows_ref[pl.ds(start + CHUNK, ROW_STEP), :] = values
        return carry

    lax.fori_loop(0, rows // ROW_STEP, norm_step, 0)
    wait_whole(weight_ref, sem)
    row = lax.broadcasted_iota(jnp.int32, (rows + CHUNK, channels), 0)
    begins = (row < CHUNK) & (here_ref[1] == 0)
    for k in range(groups):
        mixed = []
        for p in range(3):
            small = small_ref[k, 8 * p : 8 * p + 8, :]
            values = contract_cols(rows_ref[...], weight_ref[k, p]) + small[0:1]
            values = jnp.where(begins, 0.0, values)
            projected_ref[k, p] = values.astype(BF16)
            mixed.append(
                small[1:2] * values[CHUNK:]
                + small[2:3] * values[CHUNK - 1 : -1]
                + small[3:4] * values[CHUNK - 2 : -2]
                + small[4:5]
            )
        conv_input_ref[group_at(here_ref, k, groups)] = (mixed[1] * mixed[0]).astype(BF16)
        gates_ref[k, 0] = mixed[0].astype(BF16)
        gates_ref[k, 1] = mixed[1].astype(BF16)
        second_ref[k] = mixed[2].astype(BF16)


def enter(here, block_input, halo, vectors, small, local, blocks):
    rows, width = block_input.shape
    parts, channels, _ = local.shape
    groups = small.shape[0]
    outs = [
        ((groups, rows, channels), BF16),
        ((groups, rows, channels), BF16),
        ((groups, 2, rows, channels), BF16),
        ((groups, parts, rows + CHUNK, channels), BF16),
        ((rows, width), BF16),
    ]
    return kernel_call(
        functools.partial(enter_kernel, len(blocks)),
        "enter",
        outs,
        [SMEM_SPEC] + [VMEM_SPEC] * 4 + [ANY_SPEC] * (1 + len(blocks)),
        [
            pltpu.VMEM((groups, parts, channels, width), BF16),
            pltpu.VMEM((rows + CHUNK, width), BF16),
            pltpu.SemaphoreType.DMA,
        ],
        2 * rows * width * parts * groups * channels,
        16,
        40,
        (here, block_input, halo, vectors, small, local, *blocks),
    )


def middle_kernel(count, sorted_units, here_ref, *refs):
    long_ref, conv_ref, second_ref, input_ref, cot_ref, vectors_ref, small_ref, bias_ref = refs[:8]
    expand_local, reduce_local, output_local = refs[8:11]
    blocks = refs[11 : 11 + count]
    (
        result_ref,
        hidden_grad_ref,
        conv_grad_ref,
        second_grad_ref,
        gated_ref,
        act_ref,
        pre_grad_ref,
        normed_ref,
        mix_ref,
        out_low_ref,
        bias_grad_ref,
        all_sums_ref,
        skip_grad_ref,
    ) = refs[11 + count : 24 + count]
    expand_ref, reduce_ref, output_ref, normal_ref, scale_ref, sums_ref, sems = refs[24 + count :]
    rows, width = input_ref.shape
    groups, hidden, _ = expand_ref.shape
    channels = output_ref.shape[1]
    others = pl.ds(1, groups - 1)
    here = here_ref[0]

    pltpu.make_async_copy(output_local, output_ref.at[0], sems.at[0]).start()
    pltpu.make_async_copy(expand_local, expand_ref.at[0], sems.at[1]).start()
    pltpu.make_async_copy(reduce_local, reduce_ref.at[0], sems.at[2]).start()
    if sorted_units:
        share = hidden // 8
        half_share = channels // 16
        for block, half, index in each_block(here, blocks):
            ref = (expand_ref, reduce_ref)[half]
            start = pl.multiple_of((index * 2 + half) * half_share, half_share)
            pltpu.make_async_copy(
                block.at[:, pl.ds(share, half_share)],
                output_ref.at[others, pl.ds(start, half_share)],
                sems.at[0],
            ).start()
            start = pl.multiple_of(index * share, share)
            pltpu.make_async_copy(
                block.at[:, pl.ds(0, share)],
                ref.at[others, pl.ds(start, share)],
                sems.at[1 + half],
            ).start()
    else:
        for n, (block, ref) in enumerate(zip(blocks, (output_ref, expand_ref, reduce_ref))):
            pltpu.make_async_copy(block, ref.at[others], sems.at[n]).start()

    position = here_ref[1] * rows + lax.broadcasted_iota(jnp.int32, (rows, channels), 0)
    mask = jnp.where(position < here_ref[2], 1.0, 0.0)

    def conv_out(k):
        skip = small_ref[k, 24:25, :]
        group = group_at(here_ref, k, groups)
        return long_ref[group].astype(F32) + skip * conv_ref[group].astype(F32)

    for k in range(groups):
        gated = mask * second_ref[k].astype(F32) * conv_out(k)
        gated_ref[:, k * channels : (k + 1) * channels] = gated.astype(BF16)
    wait_whole(output_ref, sems.at[0])
    mixed = times(gated_ref[...], output_ref[...].reshape(groups * channels, width))
    result_ref[...] = input_ref[...] + mixed + vectors_ref[0:1]
    sums_ref[...] = jnp.zeros_like(sums_ref)

    def norm_step(i, carry):
        part = pl.ds(pl.multiple_of(i * ROW_STEP, ROW_STEP), ROW_STEP)
        values = result_ref[part, :]
        normal, scale = norm_parts(values)
        normal_ref[part, :] = normal
        scale_ref[part, :] = scale
        normed_ref[part, :] = (normal * vectors_ref[1:2] + vectors_ref[2:3]).astype(BF16)
        cot = cot_ref[part, :]
        out_low_ref[part, :] = cot.astype(BF16)
        result_ref[part, :] = values + vectors_ref[3:4]
        hidden_grad_ref[part, :] = jnp.zeros_like(cot)
        sums_ref[0:1, :] += jnp.sum(cot, axis=0, keepdims=True)
        return carry

    lax.fori_loop(0, rows // ROW_STEP, norm_step, 0)
    wait_whole(expand_ref, sems.at[1])
    wait_whole(reduce_ref, sems.at[2])
    per_step = hidden // 2

    def store_units(ref, k, half, values):
        if not sorted_units:
            start = pl.multiple_of((lax.rem(k, 2) * 2 + half) * per_step, per_step)
            ref[k // 2, :, pl.ds(start, per_step)] = values
            return
        share = hidden // 8
        for i in range(4):
            bit0 = (here & 1) ^ (i & 1)
            bit1 = ((here >> 1) & 1) ^ (i >> 1)
            bit2 = ((here >> 2) & 1) ^ half
            outer = jnp.where(k < 2, bit2 * 2 + bit1, bit1 * 2 + bit2)
            start = ((k // 2 * 4 + outer) * 2 + lax.rem(k, 2)) * share
            columns = pl.ds(pl.multiple_of(start, share), share)
            ref[bit0, :, columns] = values[:, i * share : (i + 1) * share]

    def hidden_step(j, carry):
        k, half = j // 2, lax.rem(j, 2)
        units = pl.ds(pl.multiple_of(half * per_step, per_step), per_step)
        expand = expand_ref[k, units, :]
        reduce = reduce_ref[k, units, :]
        value, slope = gelu_parts(contract_cols(normed_ref[...], expand) + bias_ref[j])
        value = value.astype(BF16)
        store_units(act_ref, k, half, value)
        result_ref[...] += times(value, reduce)
        grad = (contract_cols(out_low_ref[...], reduce) * slope).astype(BF16)
        store_units(pre_grad_ref, k, half, grad)
        bias_grad_ref[j] = jnp.sum(grad.astype(F32), axis=0, keepdims=True)
        hidden_grad_ref[...] += times(grad, expand)
        return carry

    lax.fori_loop(0, 2 * groups, hidden_step, 0)

    def back_step(i, carry):
        part = pl.ds(pl.multiple_of(i * ROW_STEP, ROW_STEP), ROW_STEP)
        res_part, gain_sum, shift_sum = norm_back(
            normal_ref[part, :], scale_ref[part, :], vectors_ref[1:2], hidden_grad_ref[part, :]
        )
        hidden_grad = cot_ref[part, :] + res_part
        hidden_grad_ref[part, :] = hidden_grad
        mix_ref[part, :] = hidden_grad.astype(BF16)
        sums_ref[1:2, :] += gain_sum[None]
        sums_ref[2:3, :] += shift_sum[None]
        sums_ref[3:4, :] += jnp.sum(hidden_grad, axis=0, keepdims=True)
        return carry

    lax.fori_loop(0, rows // ROW_STEP, back_step, 0)
    fold_rows(sums_ref, all_sums_ref)
    for k in range(groups):
        group = group_at(here_ref, k, groups)
        masked_grad = contract_cols(mix_ref[...], output_ref[k]) * mask
        second_grad_ref[k] = (masked_grad * conv_out(k)).astype(BF16)
        conv_grad = (masked_grad * second_ref[k].astype(F32)).astype(BF16)
        conv_grad_ref[group] = conv_grad
        products = conv_grad.astype(F32) * conv_ref[group].astype(F32)
        skip_grad_ref[k] = jnp.sum(products, axis=0, keepdims=True)


def grad_shapes(groups, channels, width, split, parts):
    if split:
        return [((2, 2, 2, groups // 2 * parts, channels // 8, width), BF16)] * 2
    return [((groups * parts, channels, width), BF16), ((8, 128), BF16)]


def middle(
    here, long_out, conv_input, second, block_input, cotangent, vectors, small, bias, local, blocks
):
    rows, width = block_input.shape
    groups, _, channels = small.shape
    hidden = local[0].shape[0]
    grouped = ((groups, rows, channels), BF16)
    square = ((rows, width), BF16)
    wide = ((2, rows, groups * hidden // 2), BF16)
    outs = (
        [((rows, width), F32)] * 2
        + [grouped, grouped, square, wide, wide, square, square, square]
        + [((2 * groups, 1, hidden // 2), F32)]
        + [((8 * width // channels, channels), F32), ((groups, 1, channels), F32)]
    )
    return kernel_call(
        functools.partial(middle_kernel, len(blocks), len(blocks) == 8),
        "middle",
        outs,
        [SMEM_SPEC] + [VMEM_SPEC] * 8 + [ANY_SPEC] * (3 + len(blocks)),
        [
            pltpu.VMEM((groups, hidden, width), BF16),
            pltpu.VMEM((groups, hidden, width), BF16),
            pltpu.VMEM((groups, channels, width), BF16),
            pltpu.VMEM((rows, width), F32),
            pltpu.VMEM((rows, 1), F32),
            pltpu.VMEM((8, width), F32),
            pltpu.SemaphoreType.DMA((3,)),
        ],
        20_000_000_000,
        48,
        62,
        (
            here,
            long_out,
            conv_input,
            second,
            block_input,
            cotangent,
            vectors,
            small,
            bias,
            *local,
            *blocks,
        ),
    )


def leave_kernel(count, here_ref, *refs):
    (
        du_ref,
        conv_grad_ref,
        halo_gates_ref,
        halo_grads_ref,
        small_ref,
        vectors_ref,
        normed_ref,
        gated_ref,
        mix_ref,
        skip_grad_ref,
        bias_grad_ref,
        second_grad_any,
        gates_any,
        projected_any,
        input_any,
        hidden_grad_any,
        local_ref,
    ) = refs[:17]
    blocks = refs[17 : 17 + count]
    input_grad_ref, small_grad_ref, all_sums_ref, *weight_outs = refs[17 + count : 22 + count]
    low_ref, weight_ref, sums_ref, sem, *rest = refs[22 + count :]
    second_grad_ref, gates_ref, projected_ref, input_ref, hidden_grad_ref = rest[:5]
    sems, out_sems = rest[5:7]
    weight_grads = rest[7:]
    rows, width = input_ref.shape
    groups = small_ref.shape[0]
    channels = small_ref.shape[2]
    loads = [
        [
            pltpu.make_async_copy(source.at[k], target.at[k], sems.at[n, k])
            for n, (source, target) in enumerate(
                (
                    (second_grad_any, second_grad_ref),
                    (gates_any, gates_ref),
                    (projected_any, projected_ref),
                )
            )
        ]
        for k in range(groups)
    ]
    late_loads = [
        pltpu.make_async_copy(input_any, input_ref, sems.at[3, 0]),
        pltpu.make_async_copy(hidden_grad_any, hidden_grad_ref, sems.at[3, 1]),
    ]
    for copy in loads[0] + loads[1]:
        copy.start()
    start_input_weights(here_ref, local_ref, blocks, weight_ref, sem)
    for copy in loads[2] + loads[3] + late_loads:
        copy.start()
    row = lax.broadcasted_iota(jnp.int32, (rows + CHUNK, channels), 0)
    ends = (row >= rows) & (here_ref[1] == groups - 1)
    small_grad_ref[...] = jnp.zeros_like(small_grad_ref)

    def keep_grad(k, p, weight_grad):
        if count > 1:
            store_grad(weight_grads, k, k % 2 * 4 + p, here_ref[0], weight_grad)
        else:
            weight_grads[0][4 * k + p] = weight_grad.astype(BF16)

    for k in range(groups):
        nk = (k + 1) % groups
        for copy in loads[k]:
            copy.wait()

        def extended(values, halo):
            return jnp.concatenate([values, halo], axis=0).astype(F32)

        group = group_at(here_ref, k, groups)
        conv_grad = extended(conv_grad_ref[group], halo_grads_ref[0, group])
        skip = small_ref[k, 24:25, :]
        input_side = du_ref[group].astype(F32) + skip * conv_grad
        grads = (
            input_side * extended(gates_ref[k, 1], halo_gates_ref[nk, 1]),
            input_side * extended(gates_ref[k, 0], halo_gates_ref[nk, 0]),
            extended(second_grad_ref[k], halo_grads_ref[1, nk]),
        )
        for p, grad in enumerate(grads):
            grad = jnp.where(ends, 0.0, grad)
            small = small_ref[k, 8 * p : 8 * p + 8, :]
            low = (
                small[1:2] * grad[:rows]
                + small[2:3] * grad[1 : rows + 1]
                + small[3:4] * grad[2 : rows + 2]
            ).astype(BF16)
            low_ref[:, (3 * k + p) * channels : (3 * k + p + 1) * channels] = low
            keep_grad(k, p, contract_rows(low, normed_ref[...]))
            projected = projected_ref[k, p].astype(F32)
            own = grad[:rows]
            small_grad_ref[k, 8 * p : 8 * p + 1, :] = jnp.sum(
                low.astype(F32), axis=0, keepdims=True
            )
            for tap in range(3):
                delayed = projected[CHUNK - tap : rows + CHUNK - tap]
                small_grad_ref[k, 8 * p + 1 + tap : 8 * p + 2 + tap, :] = jnp.sum(
                    own * delayed, axis=0, keepdims=True
                )
            small_grad_ref[k, 8 * p + 4 : 8 * p + 5, :] = jnp.sum(own, axis=0, keepdims=True)
        gated = gated_ref[:, k * channels : (k + 1) * channels]
        keep_grad(k, 3, contract_rows(gated, mix_ref[...]))
        small_grad_ref[k, 24:25, :] = skip_grad_ref[k]
        per_half = bias_grad_ref.shape[2] // channels
        for n in range(2 * per_half):
            bias_row = bias_grad_ref[2 * k + n // per_half]
            first = n % per_half * channels
            small_grad_ref[k, 25 + n : 26 + n, :] = bias_row[:, first : first + channels]
        if count > 1 and k % 2 == 1:
            for n in range(2):
                pltpu.make_async_copy(
                    weight_grads[n].at[k // 2], weight_outs[n].at[k // 2], out_sems.at[n, k // 2]
                ).start()
    if count == 1:
        for n in range(2):
            pltpu.make_async_copy(weight_grads[n], weight_outs[n], out_sems.at[n, 0]).start()
    wait_whole(weight_ref, sem)
    input_grad_ref[...] = times(
        low_ref[...], weight_ref[...].reshape(groups * 3 * channels, width)
    )
    sums_ref[...] = jnp.zeros_like(sums_ref)
    for copy in late_loads:
        copy.wait()

    def back_step(i, carry):
        part = pl.ds(pl.multiple_of(i * ROW_STEP, ROW_STEP), ROW_STEP)
        normal, scale = norm_parts(input_ref[part, :])
        input_part, gain_sum, shift_sum = norm_back(
            normal, scale, vectors_ref[0:1], input_grad_ref[part, :]
        )
        input_grad_ref[part, :] = hidden_grad_ref[part, :] + input_part
        sums_ref[0:1, :] += gain_sum[None]
        sums_ref[1:2, :] += shift_sum[None]
        return carry

    lax.fori_loop(0, rows // ROW_STEP, back_step, 0)
    fold_rows(sums_ref, all_sums_ref)
    for n in range(2):
        if count > 1:
            for half in range(2):
                pltpu.make_async_copy(
                    weight_grads[n].at[half], weight_outs[n].at[half], out_sems.at[n, half]
                ).wait()
        else:
            pltpu.make_async_copy(weight_grads[n], weight_outs[n], out_sems.at[n, 0]).wait()


def leave(
    here,
    conv_input_grad,
    conv_grad,
    second_grad,
    gates,
    projected,
    halo_gates,
    halo_grads,
    small,
    block_input,
    hidden_grad,
    vectors,
    normed,
    gated,
    mix_low,
    skip_grad,
    bias_grad,
    local,
    blocks,
):
    rows, width = block_input.shape
    groups, _, channels = small.shape
    grads = grad_shapes(groups, channels, width, len(blocks) > 1, 4)
    outs = [
        ((rows, width), F32),
        ((groups, SMALL_ROWS, channels), F32),
        ((8 * width // channels, channels), F32),
        *grads,
    ]
    return pl.pallas_call(
        functools.partial(leave_kernel, len(blocks)),
        out_shape=tuple(jax.ShapeDtypeStruct(shape, dtype) for shape, dtype in outs),
        in_specs=[SMEM_SPEC] + [VMEM_SPEC] * 11 + [ANY_SPEC] * (6 + len(blocks)),
        out_specs=(VMEM_SPEC,) * 3 + (ANY_SPEC,) * 2,
        scratch_shapes=[
            pltpu.VMEM((rows, 3 * groups * channels), BF16),
            pltpu.VMEM((groups, 3, channels, width), BF16),
            pltpu.VMEM((8, width), F32),
            pltpu.SemaphoreType.DMA,
            *[
                pltpu.VMEM(a.shape, a.dtype)
                for a in (second_grad, gates, projected, block_input, hidden_grad)
            ],
            pltpu.SemaphoreType.DMA((4, groups)),
            pltpu.SemaphoreType.DMA((2, 2)),
            *[pltpu.VMEM(shape, dtype) for shape, dtype in grads],
        ],
        compiler_params=pltpu.CompilerParams(vmem_limit_bytes=60 << 20),
        cost_estimate=pl.CostEstimate(
            flops=16_000_000_000, bytes_accessed=34 << 20, transcendentals=0
        ),
        name="leave",
    )(
        here,
        conv_input_grad,
        conv_grad,
        halo_gates,
        halo_grads,
        small,
        vectors,
        normed,
        gated,
        mix_low,
        skip_grad,
        bias_grad,
        second_grad,
        gates,
        projected,
        block_input,
        hidden_grad,
        local,
        *blocks,
    )


def per_device(
    block_input,
    lengths,
    mixer_gain,
    mixer_shift,
    input_weight,
    input_bias,
    conv_weight,
    conv_bias,
    enter_weight,
    enter_bias,
    middle_weight,
    middle_bias,
    inner_weight,
    inner_bias,
    frequency,
    filter_weight,
    skip_scale,
    output_weight,
    output_bias,
    feed_gain,
    feed_shift,
    expand_weight,
    expand_bias,
    reduce_weight,
    reduce_bias,
    cotangent,
):
    own_rows, width = block_input.shape
    channels = input_weight.shape[2]
    hidden = expand_weight.shape[1]
    mp_size = lax.axis_size("mp")
    dp_size = lax.axis_size("dp")
    mp_here = lax.axis_index("mp")
    dp_here = lax.axis_index("dp")
    seq_len = own_rows * mp_size
    split = dp_size == 8
    share = hidden // dp_size
    out_share = channels // dp_size
    here = jnp.stack([dp_here, mp_here, lengths[0]]).astype(jnp.int32)

    small_own = jnp.concatenate(
        [
            jnp.concatenate(
                [input_bias[:, None], conv_weight.transpose(1, 0, 2), conv_bias[:, None]]
                + [jnp.zeros((3, 3, channels), F32)],
                axis=1,
            ).reshape(24, channels),
            skip_scale[None],
            expand_bias.reshape(-1, channels),
        ]
    )
    small_own = jnp.pad(small_own, ((0, SMALL_ROWS - small_own.shape[0]), (0, 0)))

    def other_groups(values):
        return jnp.stack([shift_mp(values, k) for k in range(1, mp_size)])

    def turned_groups(stacked, start, sign):
        return jnp.concatenate(
            [
                lax.dynamic_slice_in_dim(stacked, (mp_here + sign * k) % mp_size, 1, 0)
                for k in range(start, mp_size)
            ]
        )

    features = position_features(seq_len, enter_weight.shape[0])
    columns = jnp.stack([enter_bias, middle_bias, inner_bias, frequency], axis=1)
    net_units = frequency.shape[0]
    net_shape = ((3, net_units, seq_len), F32)
    taps_low, *net_values = kernel_call(
        functools.partial(filter_kernel, width),
        "filter_taps",
        [((seq_len, channels), BF16)] + [net_shape] * 3,
        [SMEM_SPEC] + [VMEM_SPEC] * 6,
        [],
        4_000_000_000,
        6,
        32,
        (
            here,
            features,
            jnp.pad(enter_weight, ((0, FEATURE_ROWS - enter_weight.shape[0]), (0, 0))),
            middle_weight,
            inner_weight,
            columns,
            filter_weight,
        ),
    )
    small = jnp.stack([small_own] + [shift_mp(small_own, k) for k in range(1, mp_size)])
    halo = shift_mp(block_input[-CHUNK:], 1)

    input_turned = input_weight.transpose(1, 2, 0)
    expand_turned = expand_weight.T
    if split:
        input_part = lax.dynamic_slice_in_dim(input_turned, dp_here * out_share, out_share, 1)
        input_pieces = after(other_groups(input_part), taps_low, small, halo)
        input_blocks = split_blocks(input_pieces, 2, out_share // 2)
    else:
        input_blocks = [other_groups(input_turned)]
    tables = spectral_tables(seq_len)

    if split:
        expand_part = lax.dynamic_slice_in_dim(expand_turned, dp_here * share, share, 0)
        reduce_part = lax.dynamic_slice_in_dim(reduce_weight, dp_here * share, share, 0)
        output_part = lax.dynamic_slice_in_dim(output_weight, dp_here * out_share, out_share, 0)
        half = out_share // 2
        feed_part = jnp.concatenate(
            [expand_part, output_part[:half], reduce_part, output_part[half:]]
        )
        feed_groups = lax.all_gather(feed_part, "mp")
    else:
        feed_blocks = [other_groups(w) for w in (output_weight, expand_turned, reduce_weight)]

    mixer_vectors = jnp.stack([mixer_gain, mixer_shift])
    conv_input, second_gate, gates, projected, mixer_normed = enter(
        here,
        block_input,
        halo,
        mixer_vectors,
        small,
        input_turned,
        input_blocks,
    )
    halo_gates = shift_mp(gates[:, :, :CHUNK], -1)

    def exchange(values):
        return lax.all_to_all(values, "mp", 0, 0)

    arrived_input = exchange(conv_input)
    if split:
        feed_pieces = turned_groups(after(feed_groups, conv_input), 1, -1)
        halves = (feed_pieces[:, : share + half], feed_pieces[:, share + half :])
        pairs = [gather_start(part, n, arrived_input) for n, part in enumerate(halves)]
        arrived_input = after(arrived_input, *pairs)
    long_out, spec_u, spec_t = long_conv(tables, arrived_input, taps_low)
    long_out = exchange(long_out)
    if split:
        feed_blocks = [
            block for n, pair in enumerate(pairs) for block in gather_rest(pair, n, long_out)
        ]
    vectors = jnp.stack([output_bias, feed_gain, feed_shift, reduce_bias])
    bias = small[:, 25 : 25 + hidden // channels].reshape(2 * mp_size, 1, hidden // 2)
    (
        result,
        hidden_grad,
        conv_grad,
        second_grad,
        gated,
        activated,
        pre_grad,
        feed_normed,
        mix_low,
        out_low,
        bias_grad,
        feed_sums,
        skip_grad,
    ) = middle(
        here,
        long_out,
        conv_input,
        second_gate,
        block_input,
        cotangent,
        vectors,
        small,
        bias,
        (expand_turned, reduce_weight, output_weight),
        feed_blocks,
    )
    halo_grads = shift_mp(jnp.stack([conv_grad[:, :CHUNK], second_grad[:, :CHUNK]]), -1)
    arrived_grad = exchange(conv_grad)

    if split:
        pairs = ((activated, out_low), (pre_grad, feed_normed))
        arrived = [
            swap_dp(contract_rows(u[1], right).astype(BF16), 0) for u, right in pairs
        ]
    else:
        def feed_grads(left, right):
            grads = [contract_rows(part, right).astype(BF16) for part in left]
            return own_group(jnp.concatenate(grads).reshape(mp_size, hidden, width))

        reduce_weight_grad = feed_grads(activated, out_low)
        expand_weight_grad = feed_grads(pre_grad, feed_normed).T

    arrived_grad = after(arrived_grad, halo_gates, halo_grads)
    conv_input_grad, taps_grad = long_conv_back(tables, arrived_grad, spec_u, spec_t)
    if split:
        pairs = [(after(u, taps_grad), right) for u, right in pairs]
        kept = [
            (contract_rows(u[0], right) + other.astype(F32)).astype(BF16)
            for (u, right), other in zip(pairs, arrived)
        ]
        held = [k.reshape(2, 2, 2, mp_size // 2, share, width) for k in kept]
        first_stages = [
            [jnp.stack([h[n, i] for h in held], axis=1) for i in range(2)] for n in range(2)
        ]
    conv_input_grad = exchange(conv_input_grad)
    if split:
        conv_input_grad = after(conv_input_grad, first_stages[0][1], first_stages[1][1])
    input_grad, small_grad, mixer_sums, grads_kept, grads_away = leave(
        here,
        conv_input_grad,
        conv_grad,
        second_grad,
        gates,
        projected,
        halo_gates,
        halo_grads,
        small,
        block_input,
        hidden_grad,
        mixer_vectors,
        mixer_normed,
        gated,
        mix_low,
        skip_grad,
        bias_grad,
        input_turned,
        input_blocks,
    )
    if split:
        stages = [add_across(part, bit, small_grad) for part, bit in zip(first_stages, (2, 1))]
        held = (grads_kept.astype(F32) + swap_dp(grads_away, 0).astype(F32)).astype(BF16)
        stages = [add_across(part, bit) for part, bit in zip(stages, (1, 2))]
        feed_grads = jnp.concatenate(stages, axis=1).transpose(1, 0, 2, 3)
        feed_grads = turned_groups(feed_grads, 0, -1).reshape(-1, width)
        feed_total = lax.psum_scatter(feed_grads, "mp", scatter_dimension=0, tiled=True)
        taps_grad = after(taps_grad, held)
    else:
        taps_grad = after(taps_grad, grads_kept)
    net_grads, filter_weight_grad = kernel_call(
        functools.partial(filter_back_kernel, width),
        "filter_back",
        [((net_units, 4 * net_units), F32), ((net_units, channels), F32)],
        [SMEM_SPEC] + [VMEM_SPEC] * 9,
        [pltpu.VMEM((net_units, seq_len), F32)],
        8_000_000_000,
        6,
        32,
        (
            here,
            features,
            middle_weight,
            inner_weight,
            columns,
            filter_weight,
            *net_values,
            taps_grad,
        ),
    )
    packed = [net_grads, feed_sums, mixer_sums, filter_weight_grad]
    packed.append(small_grad.reshape(-1, channels))
    ends = [sum(p.shape[0] for p in packed[:n]) for n in range(len(packed) + 1)]
    packed = jnp.concatenate(packed)
    def small_sums(packed):
        summed = sum_dp(packed)
        by_group = summed[ends[4] :].reshape(mp_size, SMALL_ROWS, channels)
        along_mp = [jnp.concatenate([summed[: ends[3]], by_group[k]]) for k in range(mp_size)]
        along_mp = sum_groups(along_mp)
        return summed, along_mp

    if split:
        held = [add_across(held[0], 2, net_grads), add_across(held[1], 1, net_grads)]
        packed = after(packed, *held)
        held = [add_across(held[0], 1), add_across(held[1], 2)]
        feed_total = after(feed_total, *held)
        mine = jnp.concatenate(held).reshape(mp_size, 4, out_share, width)
        input_total = sum_groups(mine)
        reduce_total, expand_total = feed_total[:share], feed_total[share:]
        summed, along_mp = small_sums(packed)
        input_total = after(input_total, summed)
        blocks = []
        for n, total in enumerate((expand_total, reduce_total)):
            blocks.extend(gather_rest(gather_start(total.astype(BF16), n), n))
        expand_weight_grad, reduce_weight_grad = kernel_call(
            place_feed_kernel,
            "place_feed",
            [((width, hidden), F32), ((hidden, width), F32)],
            [SMEM_SPEC] + [VMEM_SPEC] * len(blocks),
            [],
            0,
            14,
            32,
            (here, *blocks),
        )
        blocks = split_blocks(input_total.astype(BF16), 1, out_share // 2, expand_weight_grad, along_mp)
        input_weight_grad, output_weight_grad = kernel_call(
            place_input_kernel,
            "place_input",
            [((3, width, channels), F32), ((channels, width), F32)],
            [SMEM_SPEC] + [VMEM_SPEC] * len(blocks),
            [pltpu.VMEM((3, channels, width), F32)],
            0,
            8,
            24,
            (here, *blocks),
        )
        input_weight_grad = input_weight_grad.transpose(1, 0, 2)
    else:
        input_total = own_group(grads_kept.reshape(mp_size, 4, channels, width))
        input_weight_grad = input_total[:3].transpose(2, 0, 1)
        output_weight_grad = input_total[3]
        summed, along_mp = small_sums(packed)

    everywhere, groups_sum = along_mp[: ends[3]], along_mp[ends[3] :]
    net = everywhere[: ends[1]]
    net_bias = net[:, 3 * net_units :].T
    feed_sums = unfold_rows(everywhere[ends[1] : ends[2]])
    mixer_sums = unfold_rows(everywhere[ends[2] : ends[3]])
    parts = groups_sum[:24].reshape(3, 8, channels)
    return (
        result,
        input_grad,
        mixer_sums[0],
        mixer_sums[1],
        input_weight_grad,
        parts[:, 0],
        parts[:, 1:4].transpose(1, 0, 2),
        parts[:, 4],
        net[: enter_weight.shape[0], :net_units],
        net_bias[0],
        net[:, net_units : 2 * net_units],
        net_bias[1],
        net[:, 2 * net_units : 3 * net_units],
        net_bias[2],
        net_bias[3],
        summed[ends[3] : ends[4]],
        groups_sum[24],
        output_weight_grad,
        feed_sums[3],
        feed_sums[1],
        feed_sums[2],
        expand_weight_grad,
        groups_sum[25 : 25 + hidden // channels].reshape(hidden),
        reduce_weight_grad,
        feed_sums[0],
    )


ROWS = P(("dp", "mp"), None)
FIRST = P("mp", None)
SECOND = P(None, "mp")
THIRD = P(None, None, "mp")


def solution(mesh):
    return jax.shard_map(
        per_device,
        mesh=mesh,
        in_specs=(
            ROWS, P("dp"), P(), P(), THIRD, SECOND, THIRD, SECOND,
            P(), P(), P(), P(), P(), P(), P(), SECOND,
            P("mp"), FIRST, P(), P(), P(), SECOND, P("mp"), FIRST, P(), ROWS,
        ),
        out_specs=(
            ROWS, ROWS, P(), P(), THIRD, SECOND, THIRD, SECOND,
            P(), P(), P(), P(), P(), P(), P(), SECOND,
            P("mp"), FIRST, P(), P(), P(), SECOND, P("mp"), FIRST, P(),
        ),
        check_vma=False,
    )
```

```python
import functools
import math

import jax
import jax.numpy as jnp
import ml_dtypes
import numpy as np
from jax import lax
from jax.experimental import pallas as pl
from jax.experimental.pallas import tpu as pltpu
from jax.sharding import PartitionSpec as P

HIGHEST_MODE = lax.Precision.HIGHEST
EPSILON = 1e-05
FIRST_FACTOR = 64
CHUNK = 16
F32 = jnp.float32
BF16 = jnp.bfloat16
VMEM_SPEC = pl.BlockSpec(memory_space=pltpu.VMEM)
SMEM_SPEC = pl.BlockSpec(memory_space=pltpu.SMEM)
ANY_SPEC = pl.BlockSpec(memory_space=pl.ANY)
HBM_SPEC = pl.BlockSpec(memory_space=pltpu.HBM)


def norm_parts(values_in):
    centred = values_in - jnp.mean(values_in, axis=-1, keepdims=True)
    variance = jnp.mean(centred * centred, axis=-1, keepdims=True)
    scale = lax.rsqrt(variance + EPSILON)
    return centred * scale, scale


def norm_back(normal, scale, gain, grad):
    inner = grad * gain
    part = scale * (
        inner
        - jnp.mean(inner, axis=-1, keepdims=True)
        - normal * jnp.mean(inner * normal, axis=-1, keepdims=True)
    )
    return part, jnp.sum(grad * normal, axis=0), jnp.sum(grad, axis=0)


FEATURE_ROWS = 40
TAP_STEP = 256


def position_features(total, emb_count):
    place = np.arange(total, dtype=np.float64)
    bands = (emb_count - 1) // 2
    freq_grid = 1e-4 + np.arange(bands) * ((bands - 1 - 1e-4) / (bands - 1))
    angles = 2.0 * math.pi / total * freq_grid[:, None] * place[None, :]
    rows = np.concatenate([place[None] / (total - 1), np.cos(angles), -np.sin(angles)])
    rows = np.pad(rows, ((0, FEATURE_ROWS - emb_count), (0, 0)))
    return jnp.asarray(rows.astype(np.float32))


def exact(left, right, left_dim, right_dim):
    dims = (((left_dim,), (right_dim,)), ((), ()))
    return lax.dot_general(
        left, right, dims, precision=HIGHEST_MODE, preferred_element_type=F32
    )


def decay_block(first_row, rows, channels, seq_len, channel_total, group):
    slowest = math.log(0.01) / 1.5
    fastest = math.log(0.01) / 0.3
    row = lax.broadcasted_iota(jnp.int32, (rows, channels), 0) + first_row
    channel = lax.broadcasted_iota(jnp.int32, (rows, channels), 1) + group * channels
    rates = jnp.abs(slowest + (fastest - slowest) * channel.astype(F32) / (channel_total - 1))
    return jnp.exp(-(row.astype(F32) / (seq_len - 1)) * rates)


def filter_kernel(
    channel_total, here_ref, features_ref, enter_ref, middle_ref, inner_ref, columns_ref, filter_ref, *outs
):
    taps_ref, value_ref, sine_ref, cosine_ref = outs
    seq_len, channels = taps_ref.shape
    frequency = columns_ref[:, 3:4]
    hidden = features_ref[...]
    for n, weight_ref in enumerate((enter_ref, middle_ref, inner_ref)):
        value = exact(weight_ref[...], hidden, 0, 0) + columns_ref[:, n : n + 1]
        value_ref[n] = value
        hidden = jnp.sin(frequency * value)
        sine_ref[n] = hidden
        cosine_ref[n] = jnp.cos(frequency * value)
    for start in range(0, seq_len, TAP_STEP):
        rows = slice(start, start + TAP_STEP)
        decay = decay_block(start, TAP_STEP, channels, seq_len, channel_total, here_ref[1])
        taps = exact(sine_ref[2, :, rows], filter_ref[...], 0, 0)
        taps_ref[rows, :] = (taps * decay).astype(BF16)


def filter_back_kernel(
    channel_total,
    here_ref,
    features_ref,
    middle_ref,
    inner_ref,
    columns_ref,
    filter_ref,
    value_ref,
    sine_ref,
    cosine_ref,
    grad_ref,
    packed_ref,
    filter_grad_ref,
    hidden_ref,
):
    seq_len, channels = grad_ref.shape
    units = filter_ref.shape[0]
    frequency = columns_ref[:, 3:4]
    filter_grad_ref[...] = jnp.zeros_like(filter_grad_ref)
    for start in range(0, seq_len, TAP_STEP):
        rows = slice(start, start + TAP_STEP)
        decay = decay_block(start, TAP_STEP, channels, seq_len, channel_total, here_ref[1])
        grad = grad_ref[rows, :] * decay
        filter_grad_ref[...] += exact(sine_ref[2, :, rows], grad, 1, 0)
        hidden_ref[:, rows] = exact(filter_ref[...], grad, 1, 1)
    packed_ref[...] = jnp.zeros_like(packed_ref)
    grad = hidden_ref[...]
    frequency_grad = jnp.zeros((units, 1), F32)
    for n in (2, 1, 0):
        inside = grad * cosine_ref[n]
        frequency_grad += jnp.sum(inside * value_ref[n], axis=1, keepdims=True)
        inside = inside * frequency
        packed_ref[:, 3 * units + n : 3 * units + n + 1] = jnp.sum(inside, axis=1, keepdims=True)
        below = features_ref[...] if n == 0 else sine_ref[n - 1]
        packed_ref[: below.shape[0], n * units : (n + 1) * units] = exact(below, inside, 1, 1)
        if n > 0:
            grad = exact((middle_ref, inner_ref)[n - 1][...], inside, 1, 0)
    packed_ref[:, 3 * units + 3 : 3 * units + 4] = frequency_grad


def spectral_tables(seq_len):
    total = 2 * seq_len
    count1 = FIRST_FACTOR
    count2 = total // count1
    half = count1 // 2
    slot = np.arange(half)
    t1 = np.arange(half)
    t2 = np.arange(count2)
    k2 = np.arange(count2)
    angle = 2 * np.pi * slot[:, None] * t1[None, :] / count1
    first = np.zeros((half, 2, half))
    first[:, 0] = np.cos(angle)
    first[:, 1] = -np.sin(angle)
    first[0, 1] = (-1.0) ** t1
    last = np.zeros((half, half, 2))
    last[:, :, 0] = np.cos(angle.T) / seq_len
    last[:, :, 1] = -np.sin(angle.T) / seq_len
    last[:, 0, 0] = 1.0 / total
    last[:, 0, 1] = (-1.0) ** t1 / total
    mid = np.zeros((half, 2, count2, 2, count2))
    back = np.zeros((half, 2, count2, 2, count2))
    for s in range(1, half):
        turn = np.exp(-2j * np.pi * t2[None, :] * (s / total + k2[:, None] / count2))
        mid[s, 0, :, 0] = turn.real
        mid[s, 0, :, 1] = -turn.imag
        mid[s, 1, :, 0] = turn.imag
        mid[s, 1, :, 1] = turn.real
        undo = np.conj(turn).T
        back[s, 0, :, 0] = undo.real
        back[s, 0, :, 1] = -undo.imag
        back[s, 1, :, 0] = undo.imag
        back[s, 1, :, 1] = undo.real
    h2 = count2 // 2
    turn = np.exp(-2j * np.pi * t2[None, :] * k2[:h2, None] / count2)
    mid[0, 0, :h2, 0] = turn.real
    mid[0, 1, :h2, 0] = turn.imag
    mid[0, 1, 0, 0] = (-1.0) ** t2
    back[0, 0, :, 0, :h2] = 2 * turn.real.T
    back[0, 0, :, 1, :h2] = 2 * turn.imag.T
    back[0, 0, :, 0, 0] = 1.0
    back[0, 0, :, 1, 0] = (-1.0) ** t2
    turn = np.exp(-2j * np.pi * t2[None, :] * (half / total + k2[:h2, None] / count2))
    mid[0, 0, h2:, 1] = turn.real
    mid[0, 1, h2:, 1] = turn.imag
    back[0, 1, :, 0, h2:] = 2 * turn.real.T
    back[0, 1, :, 1, h2:] = 2 * turn.imag.T
    unit = np.eye(CHUNK)
    tables = (
        np.kron(first.reshape(count1, half), unit),
        mid.reshape(half, 2 * count2, 2 * count2),
        back.reshape(half, 2 * count2, 2 * count2),
        np.kron(last.reshape(half, count1), unit),
    )
    return tuple(jnp.asarray(v.astype(np.float32).astype(ml_dtypes.bfloat16)) for v in tables)


def times(left, right):
    return jnp.dot(left, right, preferred_element_type=F32)


def stage_first(first_ref, x_ref, y_ref):
    count1, count2, cols = y_ref.shape
    for j in range(count2 // CHUNK):
        rows = slice(CHUNK * j, CHUNK * (j + 1))
        block = x_ref[:, rows, :].reshape(count1 // 2 * CHUNK, cols)
        y_ref[:, rows, :] = times(first_ref[...], block).reshape(count1, CHUNK, cols).astype(BF16)


def stage_last(last_ref, z_ref, out_ref):
    count1, count2, cols = z_ref.shape
    for j in range(count2 // CHUNK):
        rows = slice(CHUNK * j, CHUNK * (j + 1))
        block = z_ref[:, rows, :].reshape(count1 * CHUNK, cols)
        values = times(last_ref[...], block).reshape(count1 // 2, CHUNK, cols)
        out_ref[:, rows, :] = values.astype(out_ref.dtype)


def spectral_product(s, left_re, left_im, right_re, right_im, sign):
    both_re = left_re * right_re
    both_im = left_im * right_im
    row = lax.broadcasted_iota(jnp.int32, both_re.shape, 0)
    real_row = (row == 0) & (s == 0)
    out_re = jnp.where(real_row, both_re, both_re - sign * both_im)
    out_im = jnp.where(real_row, both_im, left_im * right_re + sign * left_re * right_im)
    return jnp.concatenate([out_re, out_im], axis=0).astype(BF16)


def conv_kernel(
    first_ref, mid_ref, back_ref, last_ref, u_ref, t_ref, out_ref, su_out, st_out, *refs
):
    y_ref, z_ref, su_ref, st_ref, sems = refs
    count1, count2, cols = y_ref.shape
    stage_first(first_ref, u_ref, y_ref)
    stage_first(first_ref, t_ref, z_ref)

    def slot_step(s, carry):
        pair = pl.ds(2 * s, 2)
        spec_u = times(mid_ref[s], y_ref[pair].reshape(2 * count2, cols))
        spec_t = times(mid_ref[s], z_ref[pair].reshape(2 * count2, cols))
        su_ref[pair] = spec_u.astype(BF16).reshape(2, count2, cols)
        st_ref[pair] = spec_t.astype(BF16).reshape(2, count2, cols)
        product = spectral_product(
            s, spec_u[:count2], spec_u[count2:], spec_t[:count2], spec_t[count2:], 1
        )
        z_ref[pair] = times(back_ref[s], product).astype(BF16).reshape(2, count2, cols)
        return carry

    lax.fori_loop(0, count1 // 2, slot_step, 0, unroll=2)
    stores = [
        pltpu.make_async_copy(su_ref, su_out, sems.at[0]),
        pltpu.make_async_copy(st_ref, st_out, sems.at[1]),
    ]
    for copy in stores:
        copy.start()
    stage_last(last_ref, z_ref, out_ref)
    for copy in stores:
        copy.wait()


def conv_back_kernel(
    first_ref, mid_ref, back_ref, last_ref, g_ref, su_any, st_any, *refs
):
    du_ref, dt_ref, y_ref, z_ref, x_ref, su_ref, st_ref, sems = refs
    count1, count2, cols = y_ref.shape
    loads = [
        pltpu.make_async_copy(su_any, su_ref, sems.at[0]),
        pltpu.make_async_copy(st_any, st_ref, sems.at[1]),
    ]
    for copy in loads:
        copy.start()
    stage_first(first_ref, g_ref, y_ref)

    for copy in loads:
        copy.wait()

    def slot_step(s, carry):
        pair = pl.ds(2 * s, 2)
        spec_g = times(mid_ref[s], y_ref[pair].reshape(2 * count2, cols))
        spec_u = su_ref[pair].astype(F32)
        spec_t = st_ref[pair].astype(F32)
        product = spectral_product(s, spec_g[:count2], spec_g[count2:], spec_t[0], spec_t[1], -1)
        y_ref[pair] = times(back_ref[s], product).astype(BF16).reshape(2, count2, cols)
        product = spectral_product(s, spec_g[:count2], spec_g[count2:], spec_u[0], spec_u[1], -1)
        z_ref[pair] = times(back_ref[s], product).astype(BF16).reshape(2, count2, cols)
        return carry

    lax.fori_loop(0, count1 // 2, slot_step, 0, unroll=2)
    stage_last(last_ref, y_ref, x_ref)
    stage_last(last_ref, z_ref, dt_ref)
    groups, rows, _ = du_ref.shape
    rows -= CHUNK
    step = count1 // 2 // groups
    for place in range(groups):
        block = x_ref[place * step : (place + 1) * step]
        du_ref[place, :rows, :] = block.reshape(rows, cols)
        du_ref[place, rows:, :] = x_ref[(place + 1) % groups * step, :CHUNK, :]


def kernel_call(kernel, name, outs, in_specs, scratch, flops, size, limit, args, copied=()):
    return pl.pallas_call(
        kernel,
        out_shape=tuple(jax.ShapeDtypeStruct(shape, dtype) for shape, dtype in outs),
        in_specs=in_specs,
        out_specs=tuple(HBM_SPEC if n in copied else VMEM_SPEC for n in range(len(outs))),
        scratch_shapes=scratch,
        compiler_params=pltpu.CompilerParams(vmem_limit_bytes=limit << 20),
        cost_estimate=pl.CostEstimate(flops=flops, bytes_accessed=size << 20, transcendentals=0),
        name=name,
    )(*args)


def long_conv(tables, signal, taps):
    seq_len, cols = taps.shape
    count1 = FIRST_FACTOR
    count2 = 2 * seq_len // count1
    timed = (count1 // 2, count2, cols)
    spectral = (count1, count2, cols)
    out, spec_u, spec_t = kernel_call(
        conv_kernel,
        "long_conv",
        [(timed, BF16), (spectral, BF16), (spectral, BF16)],
        [VMEM_SPEC] * 6,
        [pltpu.VMEM(spectral, BF16)] * 4 + [pltpu.SemaphoreType.DMA((2,))],
        9_000_000_000,
        14,
        40,
        (*tables, signal.reshape(timed), taps.reshape(timed)),
        copied=(1, 2),
    )
    return out.reshape(signal.shape), spec_u, spec_t


def long_conv_back(tables, grad, spec_u, spec_t):
    groups, rows, cols = grad.shape
    count1 = FIRST_FACTOR
    count2 = 2 * groups * rows // count1
    timed = (count1 // 2, count2, cols)
    spectral = (count1, count2, cols)
    grad_u, grad_t = kernel_call(
        conv_back_kernel,
        "long_conv_back",
        [((groups, rows + CHUNK, cols), BF16), (timed, F32)],
        [VMEM_SPEC] * 5 + [HBM_SPEC] * 2,
        [pltpu.VMEM(spectral, BF16)] * 2
        + [pltpu.VMEM(timed, BF16)]
        + [pltpu.VMEM(spectral, BF16)] * 2
        + [pltpu.SemaphoreType.DMA((2,))],
        9_000_000_000,
        14,
        40,
        (*tables, grad.reshape(timed), spec_u, spec_t),
    )
    return grad_u, grad_t.reshape(groups * rows, cols)


def shift_mp(values_in, count):
    size = lax.axis_size("mp")
    return lax.ppermute(values_in, "mp", [(i, (i + count) % size) for i in range(size)])


def swap_dp(values_in, bit):
    size = lax.axis_size("dp")
    return lax.ppermute(values_in, "dp", [(i, i ^ (1 << bit)) for i in range(size)])


def bit_orders():
    bits = lax.axis_size("dp").bit_length() - 1
    high = list(range(1, bits))
    return [0] + high, [0] + high[::-1]


def after(values_in, *others):
    return lax.optimization_barrier((values_in,) + others)[0]


def gather_offsets(half):
    first, second = ((4, 2), (2, 4))[half]
    return [(0, first), (second, first | second), (1, first | 1), (second | 1, first | second | 1)]


def gather_start(block, half, *beside):
    bit = bit_orders()[half][2]
    return jnp.stack([after(block, *beside) if beside else block, swap_dp(block, bit)])


def gather_rest(pair, half, *beside):
    others = swap_dp(pair, bit_orders()[half][1])
    if beside:
        others = after(others, *beside)
    return [pair, others, swap_dp(pair, 0), swap_dp(others, 0)]


def split_blocks(pieces, axis, rows, *beside):
    out = []
    for half in range(2):
        part = lax.slice_in_dim(pieces, half * rows, (half + 1) * rows, axis=axis)
        out.extend(gather_rest(gather_start(part, half), half, *beside))
    return out


def add_across(part, bit, *beside):
    keep = after(part[0], *beside) if beside else part[0]
    return (keep.astype(F32) + swap_dp(part[1], bit).astype(F32)).astype(BF16)


def sum_groups(mine):
    total = mine[0].astype(F32)
    for k in range(1, lax.axis_size("mp")):
        total = total + shift_mp(mine[k], -k).astype(F32)
    return total


def own_group(grads):
    return lax.psum(sum_groups(grads), "dp")


def each_block(here, blocks):
    for half in range(2):
        for n, offsets in enumerate(gather_offsets(half)):
            for i, offset in enumerate(offsets):
                yield blocks[4 * half + n].at[i], half, here ^ offset


def place_feed_kernel(here_ref, *refs):
    *blocks, expand_ref, reduce_ref = refs
    share = blocks[0].shape[1]
    for block, half, index in each_block(here_ref[0], blocks):
        place = pl.ds(pl.multiple_of(index * share, share), share)
        if half == 0:
            expand_ref[:, place] = block[...].astype(F32).T
        else:
            reduce_ref[place, :] = block[...].astype(F32)


def place_input_kernel(here_ref, *refs):
    *blocks, input_ref, output_ref, full_ref = refs
    rows = blocks[0].shape[2]
    parts = full_ref.shape[0]
    for block, half, index in each_block(here_ref[0], blocks):
        place = pl.ds(pl.multiple_of((index * 2 + half) * rows, rows), rows)
        full_ref[:, place, :] = block[:parts].astype(F32)
        output_ref[place, :] = block[parts].astype(F32)
    for p in range(parts):
        input_ref[p] = full_ref[p].T


def sum_dp(values_in):
    for bit in range(lax.axis_size("dp").bit_length() - 1):
        values_in = values_in + swap_dp(values_in, bit)
    return values_in


def contract_rows(left, right):
    return lax.dot_general(left, right, (((0,), (0,)), ((), ())), preferred_element_type=F32)


def contract_cols(left, right):
    return lax.dot_general(left, right, (((1,), (1,)), ((), ())), preferred_element_type=F32)


def gelu_parts(value):
    factor = math.sqrt(2.0 / math.pi)
    square = value * value
    tanh_part = jnp.tanh(factor * value * (1.0 + 0.044715 * square))
    half = 0.5 * (1.0 + tanh_part)
    slope = half + 0.5 * value * (1.0 - tanh_part * tanh_part) * (
        factor * (1.0 + 3.0 * 0.044715 * square)
    )
    return value * half, slope


ROW_STEP = 32
SMALL_ROWS = 32


def fold_rows(wide_ref, narrow_ref):
    channels = narrow_ref.shape[1]
    for i in range(wide_ref.shape[1] // channels):
        narrow_ref[8 * i : 8 * i + 8, :] = wide_ref[:, i * channels : (i + 1) * channels]


def unfold_rows(narrow):
    rows, channels = narrow.shape
    return narrow.reshape(rows // 8, 8, channels).transpose(1, 0, 2).reshape(8, -1)


def store_grad(refs, k, part, here, values):
    rows = values.shape[0] // 8
    for i in range(4):
        bit1, bit2 = (i & 1) ^ (here >> 1 & 1), (i >> 1) ^ (here >> 2)
        first, second = (bit2, bit1) if k < 2 else (bit1, bit2)
        pair = [values[(2 * i + n) * rows : (2 * i + n + 1) * rows].astype(BF16) for n in range(2)]
        even = here & 1 == 0
        refs[0][k // 2, first, second, part] = jnp.where(even, pair[0], pair[1])
        refs[1][k // 2, first, second, part] = jnp.where(even, pair[1], pair[0])


def start_input_weights(here_ref, local, blocks, weight_ref, sem):
    others = pl.ds(1, weight_ref.shape[0] - 1)
    pltpu.make_async_copy(local, weight_ref.at[0], sem).start()
    if len(blocks) == 1:
        pltpu.make_async_copy(blocks[0], weight_ref.at[others], sem).start()
        return
    rows = blocks[0].shape[3]
    for block, half, index in each_block(here_ref[0], blocks):
        start = pl.multiple_of((index * 2 + half) * rows, rows)
        pltpu.make_async_copy(block, weight_ref.at[others, :, pl.ds(start, rows)], sem).start()


def group_at(here_ref, k, groups):
    return lax.rem(here_ref[1] + (groups - k), groups)


def wait_whole(ref, sem):
    pltpu.make_async_copy(ref, ref, sem).wait()


def enter_kernel(count, here_ref, input_ref, halo_ref, vectors_ref, small_ref, local_ref, *refs):
    blocks = refs[:count]
    outs = refs[count : count + 5]
    weight_ref, rows_ref, sem, *results, out_sems = refs[count + 5 :]
    conv_input_ref, second_ref, gates_ref, projected_ref, normed_ref = results

    def store(n, k):
        return pltpu.make_async_copy(results[n].at[k], outs[n].at[k], out_sems.at[n, k])

    store_normed = pltpu.make_async_copy(normed_ref, outs[4], out_sems.at[4, 0])
    rows = input_ref.shape[0]
    groups, _, channels = conv_input_ref.shape
    start_input_weights(here_ref, local_ref, blocks, weight_ref, sem)

    def normed(values):
        return (norm_parts(values)[0] * vectors_ref[0:1] + vectors_ref[1:2]).astype(BF16)

    rows_ref[:CHUNK, :] = normed(halo_ref[...])

    def norm_step(i, carry):
        start = pl.multiple_of(i * ROW_STEP, ROW_STEP)
        values = normed(input_ref[pl.ds(start, ROW_STEP), :])
        normed_ref[pl.ds(start, ROW_STEP), :] = values
        rows_ref[pl.ds(start + CHUNK, ROW_STEP), :] = values
        return carry

    lax.fori_loop(0, rows // ROW_STEP, norm_step, 0)
    store_normed.start()
    wait_whole(weight_ref, sem)
    row = lax.broadcasted_iota(jnp.int32, (rows + CHUNK, channels), 0)
    begins = (row < CHUNK) & (here_ref[1] == 0)
    for k in range(groups):
        mixed = []
        for p in range(3):
            small = small_ref[k, 8 * p : 8 * p + 8, :]
            values = contract_cols(rows_ref[...], weight_ref[k, p]) + small[0:1]
            values = jnp.where(begins, 0.0, values)
            projected_ref[k, p] = values.astype(BF16)
            mixed.append(
                small[1:2] * values[CHUNK:]
                + small[2:3] * values[CHUNK - 1 : -1]
                + small[3:4] * values[CHUNK - 2 : -2]
                + small[4:5]
            )
        group = group_at(here_ref, k, groups)
        conv_input_ref[group] = (mixed[1] * mixed[0]).astype(BF16)
        gates_ref[k, 0] = mixed[0].astype(BF16)
        gates_ref[k, 1] = mixed[1].astype(BF16)
        second_ref[k] = mixed[2].astype(BF16)
        for n in range(4):
            store(n, group if n == 0 else k).start()
    store_normed.wait()
    for k in range(groups):
        for n in range(4):
            store(n, k).wait()


def enter(here, block_input, halo, vectors, small, local, blocks):
    rows, width = block_input.shape
    parts, channels, _ = local.shape
    groups = small.shape[0]
    outs = [
        ((groups, rows, channels), BF16),
        ((groups, rows, channels), BF16),
        ((groups, 2, rows, channels), BF16),
        ((groups, parts, rows + CHUNK, channels), BF16),
        ((rows, width), BF16),
    ]
    return kernel_call(
        functools.partial(enter_kernel, len(blocks)),
        "enter",
        outs,
        [SMEM_SPEC] + [VMEM_SPEC] * 4 + [ANY_SPEC] * (1 + len(blocks)),
        [
            pltpu.VMEM((groups, parts, channels, width), BF16),
            pltpu.VMEM((rows + CHUNK, width), BF16),
            pltpu.SemaphoreType.DMA,
            *[pltpu.VMEM(shape, dtype) for shape, dtype in outs],
            pltpu.SemaphoreType.DMA((5, groups)),
        ],
        2 * rows * width * parts * groups * channels,
        16,
        40,
        (here, block_input, halo, vectors, small, local, *blocks),
        copied=(0, 1, 2, 3, 4),
    )


def middle_kernel(count, sorted_units, here_ref, *refs):
    long_ref, conv_ref, second_ref, input_ref, cot_ref, vectors_ref, small_ref, bias_ref = refs[:8]
    expand_local, reduce_local, output_local = refs[8:11]
    blocks = refs[11 : 11 + count]
    (
        result_ref,
        hidden_grad_ref,
        conv_grad_ref,
        second_grad_ref,
        gated_ref,
        act_ref,
        pre_grad_ref,
        normed_ref,
        mix_ref,
        out_low_ref,
        bias_grad_ref,
        all_sums_ref,
        skip_grad_ref,
    ) = refs[11 + count : 24 + count]
    expand_ref, reduce_ref, output_ref, normal_ref, scale_ref, sums_ref, sems = refs[
        24 + count : 31 + count
    ]
    early_outs = (act_ref, pre_grad_ref, normed_ref, out_low_ref)
    act_ref, pre_grad_ref, normed_ref, out_low_ref, out_sems = refs[31 + count :]
    stores = [
        pltpu.make_async_copy(source, target, out_sems.at[n])
        for n, (source, target) in enumerate(
            zip((act_ref, pre_grad_ref, normed_ref, out_low_ref), early_outs)
        )
    ]
    rows, width = input_ref.shape
    groups, hidden, _ = expand_ref.shape
    channels = output_ref.shape[1]
    others = pl.ds(1, groups - 1)
    here = here_ref[0]

    pltpu.make_async_copy(output_local, output_ref.at[0], sems.at[0]).start()
    pltpu.make_async_copy(expand_local, expand_ref.at[0], sems.at[1]).start()
    pltpu.make_async_copy(reduce_local, reduce_ref.at[0], sems.at[2]).start()
    if sorted_units:
        share = hidden // 8
        half_share = channels // 16
        for block, half, index in each_block(here, blocks):
            ref = (expand_ref, reduce_ref)[half]
            start = pl.multiple_of((index * 2 + half) * half_share, half_share)
            pltpu.make_async_copy(
                block.at[:, pl.ds(share, half_share)],
                output_ref.at[others, pl.ds(start, half_share)],
                sems.at[0],
            ).start()
            start = pl.multiple_of(index * share, share)
            pltpu.make_async_copy(
                block.at[:, pl.ds(0, share)],
                ref.at[others, pl.ds(start, share)],
                sems.at[1 + half],
            ).start()
    else:
        for n, (block, ref) in enumerate(zip(blocks, (output_ref, expand_ref, reduce_ref))):
            pltpu.make_async_copy(block, ref.at[others], sems.at[n]).start()

    position = here_ref[1] * rows + lax.broadcasted_iota(jnp.int32, (rows, channels), 0)
    mask = jnp.where(position < here_ref[2], 1.0, 0.0)

    def conv_out(k):
        skip = small_ref[k, 24:25, :]
        group = group_at(here_ref, k, groups)
        return long_ref[group].astype(F32) + skip * conv_ref[group].astype(F32)

    for k in range(groups):
        gated = mask * second_ref[k].astype(F32) * conv_out(k)
        gated_ref[:, k * channels : (k + 1) * channels] = gated.astype(BF16)
    wait_whole(output_ref, sems.at[0])
    mixed = times(gated_ref[...], output_ref[...].reshape(groups * channels, width))
    result_ref[...] = input_ref[...] + mixed + vectors_ref[0:1]
    sums_ref[...] = jnp.zeros_like(sums_ref)

    def norm_step(i, carry):
        part = pl.ds(pl.multiple_of(i * ROW_STEP, ROW_STEP), ROW_STEP)
        values = result_ref[part, :]
        normal, scale = norm_parts(values)
        normal_ref[part, :] = normal
        scale_ref[part, :] = scale
        normed_ref[part, :] = (normal * vectors_ref[1:2] + vectors_ref[2:3]).astype(BF16)
        cot = cot_ref[part, :]
        out_low_ref[part, :] = cot.astype(BF16)
        result_ref[part, :] = values + vectors_ref[3:4]
        hidden_grad_ref[part, :] = jnp.zeros_like(cot)
        sums_ref[0:1, :] += jnp.sum(cot, axis=0, keepdims=True)
        return carry

    lax.fori_loop(0, rows // ROW_STEP, norm_step, 0)
    wait_whole(expand_ref, sems.at[1])
    wait_whole(reduce_ref, sems.at[2])
    per_step = hidden // 2

    def store_units(ref, k, half, values):
        if not sorted_units:
            start = pl.multiple_of((lax.rem(k, 2) * 2 + half) * per_step, per_step)
            ref[k // 2, :, pl.ds(start, per_step)] = values
            return
        share = hidden // 8
        for i in range(4):
            bit0 = (here & 1) ^ (i & 1)
            bit1 = ((here >> 1) & 1) ^ (i >> 1)
            bit2 = ((here >> 2) & 1) ^ half
            outer = jnp.where(k < 2, bit2 * 2 + bit1, bit1 * 2 + bit2)
            start = ((k // 2 * 4 + outer) * 2 + lax.rem(k, 2)) * share
            columns = pl.ds(pl.multiple_of(start, share), share)
            ref[bit0, :, columns] = values[:, i * share : (i + 1) * share]

    def hidden_step(j, carry):
        k, half = j // 2, lax.rem(j, 2)
        units = pl.ds(pl.multiple_of(half * per_step, per_step), per_step)
        expand = expand_ref[k, units, :]
        reduce = reduce_ref[k, units, :]
        value, slope = gelu_parts(contract_cols(normed_ref[...], expand) + bias_ref[j])
        value = value.astype(BF16)
        store_units(act_ref, k, half, value)
        result_ref[...] += times(value, reduce)
        grad = (contract_cols(out_low_ref[...], reduce) * slope).astype(BF16)
        store_units(pre_grad_ref, k, half, grad)
        bias_grad_ref[j] = jnp.sum(grad.astype(F32), axis=0, keepdims=True)
        hidden_grad_ref[...] += times(grad, expand)
        return carry

    lax.fori_loop(0, 2 * groups, hidden_step, 0)
    for copy in stores:
        copy.start()

    def back_step(i, carry):
        part = pl.ds(pl.multiple_of(i * ROW_STEP, ROW_STEP), ROW_STEP)
        res_part, gain_sum, shift_sum = norm_back(
            normal_ref[part, :], scale_ref[part, :], vectors_ref[1:2], hidden_grad_ref[part, :]
        )
        hidden_grad = cot_ref[part, :] + res_part
        hidden_grad_ref[part, :] = hidden_grad
        mix_ref[part, :] = hidden_grad.astype(BF16)
        sums_ref[1:2, :] += gain_sum[None]
        sums_ref[2:3, :] += shift_sum[None]
        sums_ref[3:4, :] += jnp.sum(hidden_grad, axis=0, keepdims=True)
        return carry

    lax.fori_loop(0, rows // ROW_STEP, back_step, 0)
    fold_rows(sums_ref, all_sums_ref)
    for k in range(groups):
        group = group_at(here_ref, k, groups)
        masked_grad = contract_cols(mix_ref[...], output_ref[k]) * mask
        second_grad_ref[k] = (masked_grad * conv_out(k)).astype(BF16)
        conv_grad = (masked_grad * second_ref[k].astype(F32)).astype(BF16)
        conv_grad_ref[group] = conv_grad
        products = conv_grad.astype(F32) * conv_ref[group].astype(F32)
        skip_grad_ref[k] = jnp.sum(products, axis=0, keepdims=True)
    for copy in stores:
        copy.wait()


def grad_shapes(groups, channels, width, split, parts):
    if split:
        return [((2, 2, 2, groups // 2 * parts, channels // 8, width), BF16)] * 2
    return [((groups * parts, channels, width), BF16), ((8, 128), BF16)]


def middle(
    here, long_out, conv_input, second, block_input, cotangent, vectors, small, bias, local, blocks
):
    rows, width = block_input.shape
    groups, _, channels = small.shape
    hidden = local[0].shape[0]
    grouped = ((groups, rows, channels), BF16)
    square = ((rows, width), BF16)
    wide = ((2, rows, groups * hidden // 2), BF16)
    outs = (
        [((rows, width), F32)] * 2
        + [grouped, grouped, square, wide, wide, square, square, square]
        + [((2 * groups, 1, hidden // 2), F32)]
        + [((8 * width // channels, channels), F32), ((groups, 1, channels), F32)]
    )
    return kernel_call(
        functools.partial(middle_kernel, len(blocks), len(blocks) == 8),
        "middle",
        outs,
        [SMEM_SPEC] + [VMEM_SPEC] * 8 + [ANY_SPEC] * (3 + len(blocks)),
        [
            pltpu.VMEM((groups, hidden, width), BF16),
            pltpu.VMEM((groups, hidden, width), BF16),
            pltpu.VMEM((groups, channels, width), BF16),
            pltpu.VMEM((rows, width), F32),
            pltpu.VMEM((rows, 1), F32),
            pltpu.VMEM((8, width), F32),
            pltpu.SemaphoreType.DMA((3,)),
            pltpu.VMEM(wide[0], BF16),
            pltpu.VMEM(wide[0], BF16),
            pltpu.VMEM((rows, width), BF16),
            pltpu.VMEM((rows, width), BF16),
            pltpu.SemaphoreType.DMA((4,)),
        ],
        20_000_000_000,
        48,
        62,
        (
            here,
            long_out,
            conv_input,
            second,
            block_input,
            cotangent,
            vectors,
            small,
            bias,
            *local,
            *blocks,
        ),
        copied=(5, 6, 7, 9),
    )


def leave_kernel(count, here_ref, *refs):
    (
        du_ref,
        conv_grad_ref,
        halo_gates_ref,
        halo_grads_ref,
        small_ref,
        vectors_ref,
        normed_ref,
        gated_ref,
        mix_ref,
        skip_grad_ref,
        bias_grad_ref,
        second_grad_any,
        gates_any,
        projected_any,
        input_any,
        hidden_grad_any,
        local_ref,
    ) = refs[:17]
    blocks = refs[17 : 17 + count]
    input_grad_ref, small_grad_ref, all_sums_ref, *weight_outs = refs[17 + count : 22 + count]
    low_ref, weight_ref, sums_ref, sem, *rest = refs[22 + count :]
    second_grad_ref, gates_ref, projected_ref, input_ref, hidden_grad_ref = rest[:5]
    sems, out_sems = rest[5:7]
    weight_grads = rest[7:]
    rows, width = input_ref.shape
    groups = small_ref.shape[0]
    channels = small_ref.shape[2]
    loads = [
        [
            pltpu.make_async_copy(source.at[k], target.at[k], sems.at[n, k])
            for n, (source, target) in enumerate(
                (
                    (second_grad_any, second_grad_ref),
                    (gates_any, gates_ref),
                    (projected_any, projected_ref),
                )
            )
        ]
        for k in range(groups)
    ]
    late_loads = [
        pltpu.make_async_copy(input_any, input_ref, sems.at[3, 0]),
        pltpu.make_async_copy(hidden_grad_any, hidden_grad_ref, sems.at[3, 1]),
    ]
    for copy in loads[0] + loads[1]:
        copy.start()
    start_input_weights(here_ref, local_ref, blocks, weight_ref, sem)
    for copy in loads[2] + loads[3] + late_loads:
        copy.start()
    row = lax.broadcasted_iota(jnp.int32, (rows + CHUNK, channels), 0)
    ends = (row >= rows) & (here_ref[1] == groups - 1)
    small_grad_ref[...] = jnp.zeros_like(small_grad_ref)

    def keep_grad(k, p, weight_grad):
        if count > 1:
            store_grad(weight_grads, k, k % 2 * 4 + p, here_ref[0], weight_grad)
        else:
            weight_grads[0][4 * k + p] = weight_grad.astype(BF16)

    for k in range(groups):
        nk = (k + 1) % groups
        for copy in loads[k]:
            copy.wait()

        def extended(values, halo):
            return jnp.concatenate([values, halo], axis=0).astype(F32)

        group = group_at(here_ref, k, groups)
        conv_grad = extended(conv_grad_ref[group], halo_grads_ref[0, group])
        skip = small_ref[k, 24:25, :]
        input_side = du_ref[group].astype(F32) + skip * conv_grad
        grads = (
            input_side * extended(gates_ref[k, 1], halo_gates_ref[nk, 1]),
            input_side * extended(gates_ref[k, 0], halo_gates_ref[nk, 0]),
            extended(second_grad_ref[k], halo_grads_ref[1, nk]),
        )
        for p, grad in enumerate(grads):
            grad = jnp.where(ends, 0.0, grad)
            small = small_ref[k, 8 * p : 8 * p + 8, :]
            low = (
                small[1:2] * grad[:rows]
                + small[2:3] * grad[1 : rows + 1]
                + small[3:4] * grad[2 : rows + 2]
            ).astype(BF16)
            low_ref[:, (3 * k + p) * channels : (3 * k + p + 1) * channels] = low
            keep_grad(k, p, contract_rows(low, normed_ref[...]))
            projected = projected_ref[k, p].astype(F32)
            own = grad[:rows]
            small_grad_ref[k, 8 * p : 8 * p + 1, :] = jnp.sum(
                low.astype(F32), axis=0, keepdims=True
            )
            for tap in range(3):
                delayed = projected[CHUNK - tap : rows + CHUNK - tap]
                small_grad_ref[k, 8 * p + 1 + tap : 8 * p + 2 + tap, :] = jnp.sum(
                    own * delayed, axis=0, keepdims=True
                )
            small_grad_ref[k, 8 * p + 4 : 8 * p + 5, :] = jnp.sum(own, axis=0, keepdims=True)
        gated = gated_ref[:, k * channels : (k + 1) * channels]
        keep_grad(k, 3, contract_rows(gated, mix_ref[...]))
        small_grad_ref[k, 24:25, :] = skip_grad_ref[k]
        per_half = bias_grad_ref.shape[2] // channels
        for n in range(2 * per_half):
            bias_row = bias_grad_ref[2 * k + n // per_half]
            first = n % per_half * channels
            small_grad_ref[k, 25 + n : 26 + n, :] = bias_row[:, first : first + channels]
        if count > 1 and k % 2 == 1:
            for n in range(2):
                pltpu.make_async_copy(
                    weight_grads[n].at[k // 2], weight_outs[n].at[k // 2], out_sems.at[n, k // 2]
                ).start()
    if count == 1:
        for n in range(2):
            pltpu.make_async_copy(weight_grads[n], weight_outs[n], out_sems.at[n, 0]).start()
    wait_whole(weight_ref, sem)
    input_grad_ref[...] = times(
        low_ref[...], weight_ref[...].reshape(groups * 3 * channels, width)
    )
    sums_ref[...] = jnp.zeros_like(sums_ref)
    for copy in late_loads:
        copy.wait()

    def back_step(i, carry):
        part = pl.ds(pl.multiple_of(i * ROW_STEP, ROW_STEP), ROW_STEP)
        normal, scale = norm_parts(input_ref[part, :])
        input_part, gain_sum, shift_sum = norm_back(
            normal, scale, vectors_ref[0:1], input_grad_ref[part, :]
        )
        input_grad_ref[part, :] = hidden_grad_ref[part, :] + input_part
        sums_ref[0:1, :] += gain_sum[None]
        sums_ref[1:2, :] += shift_sum[None]
        return carry

    lax.fori_loop(0, rows // ROW_STEP, back_step, 0)
    fold_rows(sums_ref, all_sums_ref)
    for n in range(2):
        if count > 1:
            for half in range(2):
                pltpu.make_async_copy(
                    weight_grads[n].at[half], weight_outs[n].at[half], out_sems.at[n, half]
                ).wait()
        else:
            pltpu.make_async_copy(weight_grads[n], weight_outs[n], out_sems.at[n, 0]).wait()


def leave(
    here,
    conv_input_grad,
    conv_grad,
    second_grad,
    gates,
    projected,
    halo_gates,
    halo_grads,
    small,
    block_input,
    hidden_grad,
    vectors,
    normed,
    gated,
    mix_low,
    skip_grad,
    bias_grad,
    local,
    blocks,
):
    rows, width = block_input.shape
    groups, _, channels = small.shape
    grads = grad_shapes(groups, channels, width, len(blocks) > 1, 4)
    outs = [
        ((rows, width), F32),
        ((groups, SMALL_ROWS, channels), F32),
        ((8 * width // channels, channels), F32),
        *grads,
    ]
    return pl.pallas_call(
        functools.partial(leave_kernel, len(blocks)),
        out_shape=tuple(jax.ShapeDtypeStruct(shape, dtype) for shape, dtype in outs),
        in_specs=[SMEM_SPEC] + [VMEM_SPEC] * 11 + [HBM_SPEC] * 5 + [ANY_SPEC] * (1 + len(blocks)),
        out_specs=(VMEM_SPEC,) * 3 + (HBM_SPEC,) * 2,
        scratch_shapes=[
            pltpu.VMEM((rows, 3 * groups * channels), BF16),
            pltpu.VMEM((groups, 3, channels, width), BF16),
            pltpu.VMEM((8, width), F32),
            pltpu.SemaphoreType.DMA,
            *[
                pltpu.VMEM(a.shape, a.dtype)
                for a in (second_grad, gates, projected, block_input, hidden_grad)
            ],
            pltpu.SemaphoreType.DMA((4, groups)),
            pltpu.SemaphoreType.DMA((2, 2)),
            *[pltpu.VMEM(shape, dtype) for shape, dtype in grads],
        ],
        compiler_params=pltpu.CompilerParams(vmem_limit_bytes=60 << 20),
        cost_estimate=pl.CostEstimate(
            flops=16_000_000_000, bytes_accessed=34 << 20, transcendentals=0
        ),
        name="leave",
    )(
        here,
        conv_input_grad,
        conv_grad,
        halo_gates,
        halo_grads,
        small,
        vectors,
        normed,
        gated,
        mix_low,
        skip_grad,
        bias_grad,
        second_grad,
        gates,
        projected,
        block_input,
        hidden_grad,
        local,
        *blocks,
    )


def per_device(
    block_input,
    lengths,
    mixer_gain,
    mixer_shift,
    input_weight,
    input_bias,
    conv_weight,
    conv_bias,
    enter_weight,
    enter_bias,
    middle_weight,
    middle_bias,
    inner_weight,
    inner_bias,
    frequency,
    filter_weight,
    skip_scale,
    output_weight,
    output_bias,
    feed_gain,
    feed_shift,
    expand_weight,
    expand_bias,
    reduce_weight,
    reduce_bias,
    cotangent,
):
    own_rows, width = block_input.shape
    channels = input_weight.shape[2]
    hidden = expand_weight.shape[1]
    mp_size = lax.axis_size("mp")
    dp_size = lax.axis_size("dp")
    mp_here = lax.axis_index("mp")
    dp_here = lax.axis_index("dp")
    seq_len = own_rows * mp_size
    split = dp_size == 8
    share = hidden // dp_size
    out_share = channels // dp_size
    here = jnp.stack([dp_here, mp_here, lengths[0]]).astype(jnp.int32)

    small_own = jnp.concatenate(
        [
            jnp.concatenate(
                [input_bias[:, None], conv_weight.transpose(1, 0, 2), conv_bias[:, None]]
                + [jnp.zeros((3, 3, channels), F32)],
                axis=1,
            ).reshape(24, channels),
            skip_scale[None],
            expand_bias.reshape(-1, channels),
        ]
    )
    small_own = jnp.pad(small_own, ((0, SMALL_ROWS - small_own.shape[0]), (0, 0)))

    def other_groups(values):
        return jnp.stack([shift_mp(values, k) for k in range(1, mp_size)])

    def turned_groups(stacked, start, sign):
        return jnp.concatenate(
            [
                lax.dynamic_slice_in_dim(stacked, (mp_here + sign * k) % mp_size, 1, 0)
                for k in range(start, mp_size)
            ]
        )

    features = position_features(seq_len, enter_weight.shape[0])
    columns = jnp.stack([enter_bias, middle_bias, inner_bias, frequency], axis=1)
    net_units = frequency.shape[0]
    net_shape = ((3, net_units, seq_len), F32)
    taps_low, *net_values = kernel_call(
        functools.partial(filter_kernel, width),
        "filter_taps",
        [((seq_len, channels), BF16)] + [net_shape] * 3,
        [SMEM_SPEC] + [VMEM_SPEC] * 6,
        [],
        4_000_000_000,
        6,
        32,
        (
            here,
            features,
            jnp.pad(enter_weight, ((0, FEATURE_ROWS - enter_weight.shape[0]), (0, 0))),
            middle_weight,
            inner_weight,
            columns,
            filter_weight,
        ),
    )
    small_rows = jnp.concatenate([small_own, block_input[-CHUNK:].reshape(-1, channels)])
    small_rows = jnp.stack([small_rows] + [shift_mp(small_rows, k) for k in range(1, mp_size)])
    small = small_rows[:, :SMALL_ROWS]
    halo = small_rows[1, SMALL_ROWS:].reshape(CHUNK, width)

    input_turned = input_weight.transpose(1, 2, 0)
    expand_turned = expand_weight.T
    if split:
        input_part = lax.dynamic_slice_in_dim(input_turned, dp_here * out_share, out_share, 1)
        input_pieces = after(other_groups(input_part), small_rows)
        input_blocks = split_blocks(input_pieces, 2, out_share // 2)
    else:
        input_blocks = [other_groups(input_turned)]
    tables = spectral_tables(seq_len)

    if split:
        expand_part = lax.dynamic_slice_in_dim(expand_turned, dp_here * share, share, 0)
        reduce_part = lax.dynamic_slice_in_dim(reduce_weight, dp_here * share, share, 0)
        output_part = lax.dynamic_slice_in_dim(output_weight, dp_here * out_share, out_share, 0)
        half = out_share // 2
        feed_part = jnp.concatenate(
            [expand_part, output_part[:half], reduce_part, output_part[half:]]
        )
        feed_groups = lax.all_gather(after(feed_part, input_pieces), "mp")
    else:
        feed_blocks = [other_groups(w) for w in (output_weight, expand_turned, reduce_weight)]

    mixer_vectors = jnp.stack([mixer_gain, mixer_shift])
    conv_input, second_gate, gates, projected, mixer_normed = enter(
        here,
        block_input,
        halo,
        mixer_vectors,
        small,
        input_turned,
        input_blocks,
    )
    halo_gates = shift_mp(gates[:, :, :CHUNK], -1)

    def exchange(values):
        return lax.all_to_all(values, "mp", 0, 0)

    arrived_input = exchange(conv_input)
    if split:
        feed_pieces = turned_groups(after(feed_groups, conv_input), 1, -1)
        halves = (feed_pieces[:, : share + half], feed_pieces[:, share + half :])
        pairs = [gather_start(part, n, arrived_input) for n, part in enumerate(halves)]
        arrived_input = after(arrived_input, *pairs)
    long_out, spec_u, spec_t = long_conv(tables, arrived_input, taps_low)
    long_out = after(exchange(long_out), halo_gates)
    if split:
        feed_blocks = [
            block for n, pair in enumerate(pairs) for block in gather_rest(pair, n, long_out)
        ]
    vectors = jnp.stack([output_bias, feed_gain, feed_shift, reduce_bias])
    bias = small[:, 25 : 25 + hidden // channels].reshape(2 * mp_size, 1, hidden // 2)
    (
        result,
        hidden_grad,
        conv_grad,
        second_grad,
        gated,
        activated,
        pre_grad,
        feed_normed,
        mix_low,
        out_low,
        bias_grad,
        feed_sums,
        skip_grad,
    ) = middle(
        here,
        long_out,
        conv_input,
        second_gate,
        block_input,
        cotangent,
        vectors,
        small,
        bias,
        (expand_turned, reduce_weight, output_weight),
        feed_blocks,
    )
    halo_grads = shift_mp(jnp.stack([conv_grad[:, :CHUNK], second_grad[:, :CHUNK]]), -1)
    arrived_grad = exchange(conv_grad)

    if split:
        pairs = ((activated, out_low), (pre_grad, feed_normed))
    else:
        def feed_grads(left, right):
            grads = [contract_rows(part, right).astype(BF16) for part in left]
            return own_group(jnp.concatenate(grads).reshape(mp_size, hidden, width))

        reduce_weight_grad = feed_grads(activated, out_low)
        expand_weight_grad = feed_grads(pre_grad, feed_normed).T

    arrived_grad = after(arrived_grad, halo_grads)
    conv_input_grad, taps_grad = long_conv_back(tables, arrived_grad, spec_u, spec_t)
    if split:
        late = [(after(u, taps_grad), right) for u, right in pairs]
        arrived = [
            swap_dp(contract_rows(u[1], right).astype(BF16), 0) for u, right in (pairs[0], late[1])
        ]
        pairs = late
        kept = [
            (contract_rows(u[0], right) + other.astype(F32)).astype(BF16)
            for (u, right), other in zip(pairs, arrived)
        ]
        held = [k.reshape(2, 2, 2, mp_size // 2, share, width) for k in kept]
        first_stages = [
            [jnp.stack([h[n, i] for h in held], axis=1) for i in range(2)] for n in range(2)
        ]
    conv_input_grad = exchange(conv_input_grad)
    if split:
        conv_input_grad = after(
            conv_input_grad, halo_grads, first_stages[0][1], first_stages[1][1]
        )
    input_grad, small_grad, mixer_sums, grads_kept, grads_away = leave(
        here,
        conv_input_grad,
        conv_grad,
        second_grad,
        gates,
        projected,
        halo_gates,
        halo_grads,
        small,
        block_input,
        hidden_grad,
        mixer_vectors,
        mixer_normed,
        gated,
        mix_low,
        skip_grad,
        bias_grad,
        input_turned,
        input_blocks,
    )
    if split:
        held = (grads_kept.astype(F32) + swap_dp(grads_away, 0).astype(F32)).astype(BF16)
        taps_grad = after(taps_grad, held)
    else:
        taps_grad = after(taps_grad, grads_kept)
    net_grads, filter_weight_grad = kernel_call(
        functools.partial(filter_back_kernel, width),
        "filter_back",
        [((net_units, 4 * net_units), F32), ((net_units, channels), F32)],
        [SMEM_SPEC] + [VMEM_SPEC] * 9,
        [pltpu.VMEM((net_units, seq_len), F32)],
        8_000_000_000,
        6,
        32,
        (
            here,
            features,
            middle_weight,
            inner_weight,
            columns,
            filter_weight,
            *net_values,
            taps_grad,
        ),
    )
    packed = [net_grads, feed_sums, mixer_sums, filter_weight_grad]
    packed.append(small_grad.reshape(-1, channels))
    ends = [sum(p.shape[0] for p in packed[:n]) for n in range(len(packed) + 1)]
    packed = jnp.concatenate(packed)
    def small_sums(summed):
        by_group = summed[ends[4] :].reshape(mp_size, SMALL_ROWS, channels)
        return sum_groups(
            [jnp.concatenate([summed[: ends[3]], by_group[k]]) for k in range(mp_size)]
        )

    if split:
        stages = [
            add_across(part, bit, small_grad) for part, bit in zip(first_stages, (2, 1))
        ]
        stages = [add_across(part, bit) for part, bit in zip(stages, (1, 2))]
        feed_grads = jnp.concatenate(stages, axis=1).transpose(1, 0, 2, 3)
        feed_grads = turned_groups(feed_grads, 0, -1).reshape(-1, width)
        feed_total = lax.psum_scatter(feed_grads, "mp", scatter_dimension=0, tiled=True)
        held = [add_across(held[0], 2, net_grads), add_across(held[1], 1, net_grads)]
        packed = after(packed, *held)
        held = [add_across(held[0], 1), add_across(held[1], 2)]
        feed_total = after(feed_total, *held)
        mine = jnp.concatenate(held).reshape(mp_size, 4, out_share, width)
        mine = turned_groups(mine, 0, -1).reshape(-1, width)
        input_total = lax.psum_scatter(mine, "mp", scatter_dimension=0, tiled=True)
        input_total = input_total.reshape(4, out_share, width)
        reduce_total, expand_total = feed_total[:share], feed_total[share:]
        summed = sum_dp(packed)
        blocks = []
        for n, total in enumerate((expand_total, reduce_total)):
            blocks.extend(gather_rest(gather_start(total, n), n))
        input_total = after(input_total, summed, blocks[1], blocks[5])
        expand_weight_grad, reduce_weight_grad = kernel_call(
            place_feed_kernel,
            "place_feed",
            [((width, hidden), F32), ((hidden, width), F32)],
            [SMEM_SPEC] + [VMEM_SPEC] * len(blocks),
            [],
            0,
            14,
            32,
            (here, *blocks),
        )
        along_mp = small_sums(after(summed, input_total))
        blocks = split_blocks(input_total, 1, out_share // 2, expand_weight_grad)
        input_weight_grad, output_weight_grad = kernel_call(
            place_input_kernel,
            "place_input",
            [((3, width, channels), F32), ((channels, width), F32)],
            [SMEM_SPEC] + [VMEM_SPEC] * len(blocks),
            [pltpu.VMEM((3, channels, width), F32)],
            0,
            8,
            24,
            (here, *blocks),
        )
        input_weight_grad = input_weight_grad.transpose(1, 0, 2)
    else:
        input_total = own_group(grads_kept.reshape(mp_size, 4, channels, width))
        input_weight_grad = input_total[:3].transpose(2, 0, 1)
        output_weight_grad = input_total[3]
        summed = sum_dp(packed)
        along_mp = small_sums(summed)

    everywhere, groups_sum = along_mp[: ends[3]], along_mp[ends[3] :]
    net = everywhere[: ends[1]]
    net_bias = net[:, 3 * net_units :].T
    feed_sums = unfold_rows(everywhere[ends[1] : ends[2]])
    mixer_sums = unfold_rows(everywhere[ends[2] : ends[3]])
    parts = groups_sum[:24].reshape(3, 8, channels)
    return (
        result,
        input_grad,
        mixer_sums[0],
        mixer_sums[1],
        input_weight_grad,
        parts[:, 0],
        parts[:, 1:4].transpose(1, 0, 2),
        parts[:, 4],
        net[: enter_weight.shape[0], :net_units],
        net_bias[0],
        net[:, net_units : 2 * net_units],
        net_bias[1],
        net[:, 2 * net_units : 3 * net_units],
        net_bias[2],
        net_bias[3],
        summed[ends[3] : ends[4]],
        groups_sum[24],
        output_weight_grad,
        feed_sums[3],
        feed_sums[1],
        feed_sums[2],
        expand_weight_grad,
        groups_sum[25 : 25 + hidden // channels].reshape(hidden),
        reduce_weight_grad,
        feed_sums[0],
    )


ROWS = P(("dp", "mp"), None)
FIRST = P("mp", None)
SECOND = P(None, "mp")
THIRD = P(None, None, "mp")


def solution(mesh):
    return jax.shard_map(
        per_device,
        mesh=mesh,
        in_specs=(
            ROWS, P("dp"), P(), P(), THIRD, SECOND, THIRD, SECOND,
            P(), P(), P(), P(), P(), P(), P(), SECOND,
            P("mp"), FIRST, P(), P(), P(), SECOND, P("mp"), FIRST, P(), ROWS,
        ),
        out_specs=(
            ROWS, ROWS, P(), P(), THIRD, SECOND, THIRD, SECOND,
            P(), P(), P(), P(), P(), P(), P(), SECOND,
            P("mp"), FIRST, P(), P(), P(), SECOND, P("mp"), FIRST, P(),
        ),
        check_vma=False,
    )
```

```python
import functools
import math

import jax
import jax.numpy as jnp
import ml_dtypes
import numpy as np
from jax import lax
from jax.experimental import pallas as pl
from jax.experimental.pallas import tpu as pltpu
from jax.sharding import PartitionSpec as P

HIGHEST_MODE = lax.Precision.HIGHEST
EPSILON = 1e-05
FIRST_FACTOR = 64
CHUNK = 16
F32 = jnp.float32
BF16 = jnp.bfloat16
VMEM_SPEC = pl.BlockSpec(memory_space=pltpu.VMEM)
SMEM_SPEC = pl.BlockSpec(memory_space=pltpu.SMEM)
ANY_SPEC = pl.BlockSpec(memory_space=pl.ANY)
HBM_SPEC = pl.BlockSpec(memory_space=pltpu.HBM)


def norm_parts(values_in):
    centred = values_in - jnp.mean(values_in, axis=-1, keepdims=True)
    variance = jnp.mean(centred * centred, axis=-1, keepdims=True)
    scale = lax.rsqrt(variance + EPSILON)
    return centred * scale, scale


def norm_back(normal, scale, gain, grad):
    inner = grad * gain
    part = scale * (
        inner
        - jnp.mean(inner, axis=-1, keepdims=True)
        - normal * jnp.mean(inner * normal, axis=-1, keepdims=True)
    )
    return part, jnp.sum(grad * normal, axis=0), jnp.sum(grad, axis=0)


FEATURE_ROWS = 40
TAP_STEP = 256


def position_features(total, emb_count):
    place = np.arange(total, dtype=np.float64)
    bands = (emb_count - 1) // 2
    freq_grid = 1e-4 + np.arange(bands) * ((bands - 1 - 1e-4) / (bands - 1))
    angles = 2.0 * math.pi / total * freq_grid[:, None] * place[None, :]
    rows = np.concatenate([place[None] / (total - 1), np.cos(angles), -np.sin(angles)])
    rows = np.pad(rows, ((0, FEATURE_ROWS - emb_count), (0, 0)))
    return jnp.asarray(rows.astype(np.float32))


def exact(left, right, left_dim, right_dim):
    dims = (((left_dim,), (right_dim,)), ((), ()))
    return lax.dot_general(
        left, right, dims, precision=HIGHEST_MODE, preferred_element_type=F32
    )


def decay_block(first_row, rows, channels, seq_len, channel_total, group):
    slowest = math.log(0.01) / 1.5
    fastest = math.log(0.01) / 0.3
    row = lax.broadcasted_iota(jnp.int32, (rows, channels), 0) + first_row
    channel = lax.broadcasted_iota(jnp.int32, (rows, channels), 1) + group * channels
    rates = jnp.abs(slowest + (fastest - slowest) * channel.astype(F32) / (channel_total - 1))
    return jnp.exp(-(row.astype(F32) / (seq_len - 1)) * rates)


def filter_kernel(
    channel_total, here_ref, features_ref, enter_ref, middle_ref, inner_ref, columns_ref, filter_ref, *outs
):
    taps_ref, value_ref, sine_ref, cosine_ref = outs
    seq_len, channels = taps_ref.shape
    frequency = columns_ref[:, 3:4]
    hidden = features_ref[...]
    for n, weight_ref in enumerate((enter_ref, middle_ref, inner_ref)):
        value = exact(weight_ref[...], hidden, 0, 0) + columns_ref[:, n : n + 1]
        value_ref[n] = value
        hidden = jnp.sin(frequency * value)
        sine_ref[n] = hidden
        cosine_ref[n] = jnp.cos(frequency * value)
    for start in range(0, seq_len, TAP_STEP):
        rows = slice(start, start + TAP_STEP)
        decay = decay_block(start, TAP_STEP, channels, seq_len, channel_total, here_ref[1])
        taps = exact(sine_ref[2, :, rows], filter_ref[...], 0, 0)
        taps_ref[rows, :] = (taps * decay).astype(BF16)


def filter_back_kernel(
    channel_total,
    here_ref,
    features_ref,
    middle_ref,
    inner_ref,
    columns_ref,
    filter_ref,
    value_ref,
    sine_ref,
    cosine_ref,
    grad_ref,
    packed_ref,
    filter_grad_ref,
    hidden_ref,
):
    seq_len, channels = grad_ref.shape
    units = filter_ref.shape[0]
    frequency = columns_ref[:, 3:4]
    filter_grad_ref[...] = jnp.zeros_like(filter_grad_ref)
    for start in range(0, seq_len, TAP_STEP):
        rows = slice(start, start + TAP_STEP)
        decay = decay_block(start, TAP_STEP, channels, seq_len, channel_total, here_ref[1])
        grad = grad_ref[rows, :] * decay
        filter_grad_ref[...] += exact(sine_ref[2, :, rows], grad, 1, 0)
        hidden_ref[:, rows] = exact(filter_ref[...], grad, 1, 1)
    packed_ref[...] = jnp.zeros_like(packed_ref)
    grad = hidden_ref[...]
    frequency_grad = jnp.zeros((units, 1), F32)
    for n in (2, 1, 0):
        inside = grad * cosine_ref[n]
        frequency_grad += jnp.sum(inside * value_ref[n], axis=1, keepdims=True)
        inside = inside * frequency
        packed_ref[:, 3 * units + n : 3 * units + n + 1] = jnp.sum(inside, axis=1, keepdims=True)
        below = features_ref[...] if n == 0 else sine_ref[n - 1]
        packed_ref[: below.shape[0], n * units : (n + 1) * units] = exact(below, inside, 1, 1)
        if n > 0:
            grad = exact((middle_ref, inner_ref)[n - 1][...], inside, 1, 0)
    packed_ref[:, 3 * units + 3 : 3 * units + 4] = frequency_grad


def spectral_tables(seq_len):
    total = 2 * seq_len
    count1 = FIRST_FACTOR
    count2 = total // count1
    half = count1 // 2
    slot = np.arange(half)
    t1 = np.arange(half)
    t2 = np.arange(count2)
    k2 = np.arange(count2)
    angle = 2 * np.pi * slot[:, None] * t1[None, :] / count1
    first = np.zeros((half, 2, half))
    first[:, 0] = np.cos(angle)
    first[:, 1] = -np.sin(angle)
    first[0, 1] = (-1.0) ** t1
    last = np.zeros((half, half, 2))
    last[:, :, 0] = np.cos(angle.T) / seq_len
    last[:, :, 1] = -np.sin(angle.T) / seq_len
    last[:, 0, 0] = 1.0 / total
    last[:, 0, 1] = (-1.0) ** t1 / total
    mid = np.zeros((half, 2, count2, 2, count2))
    back = np.zeros((half, 2, count2, 2, count2))
    for s in range(1, half):
        turn = np.exp(-2j * np.pi * t2[None, :] * (s / total + k2[:, None] / count2))
        mid[s, 0, :, 0] = turn.real
        mid[s, 0, :, 1] = -turn.imag
        mid[s, 1, :, 0] = turn.imag
        mid[s, 1, :, 1] = turn.real
        undo = np.conj(turn).T
        back[s, 0, :, 0] = undo.real
        back[s, 0, :, 1] = -undo.imag
        back[s, 1, :, 0] = undo.imag
        back[s, 1, :, 1] = undo.real
    h2 = count2 // 2
    turn = np.exp(-2j * np.pi * t2[None, :] * k2[:h2, None] / count2)
    mid[0, 0, :h2, 0] = turn.real
    mid[0, 1, :h2, 0] = turn.imag
    mid[0, 1, 0, 0] = (-1.0) ** t2
    back[0, 0, :, 0, :h2] = 2 * turn.real.T
    back[0, 0, :, 1, :h2] = 2 * turn.imag.T
    back[0, 0, :, 0, 0] = 1.0
    back[0, 0, :, 1, 0] = (-1.0) ** t2
    turn = np.exp(-2j * np.pi * t2[None, :] * (half / total + k2[:h2, None] / count2))
    mid[0, 0, h2:, 1] = turn.real
    mid[0, 1, h2:, 1] = turn.imag
    back[0, 1, :, 0, h2:] = 2 * turn.real.T
    back[0, 1, :, 1, h2:] = 2 * turn.imag.T
    unit = np.eye(CHUNK)
    tables = (
        np.kron(first.reshape(count1, half), unit),
        mid.reshape(half, 2 * count2, 2 * count2),
        back.reshape(half, 2 * count2, 2 * count2),
        np.kron(last.reshape(half, count1), unit),
    )
    return tuple(jnp.asarray(v.astype(np.float32).astype(ml_dtypes.bfloat16)) for v in tables)


def times(left, right):
    return jnp.dot(left, right, preferred_element_type=F32)


def stage_first(first_ref, x_ref, y_ref):
    count1, count2, cols = y_ref.shape
    for j in range(count2 // CHUNK):
        rows = slice(CHUNK * j, CHUNK * (j + 1))
        block = x_ref[:, rows, :].reshape(count1 // 2 * CHUNK, cols)
        y_ref[:, rows, :] = times(first_ref[...], block).reshape(count1, CHUNK, cols).astype(BF16)


def stage_last(last_ref, z_ref, out_ref):
    count1, count2, cols = z_ref.shape
    for j in range(count2 // CHUNK):
        rows = slice(CHUNK * j, CHUNK * (j + 1))
        block = z_ref[:, rows, :].reshape(count1 * CHUNK, cols)
        values = times(last_ref[...], block).reshape(count1 // 2, CHUNK, cols)
        out_ref[:, rows, :] = values.astype(out_ref.dtype)


def spectral_product(s, left_re, left_im, right_re, right_im, sign):
    both_re = left_re * right_re
    both_im = left_im * right_im
    row = lax.broadcasted_iota(jnp.int32, both_re.shape, 0)
    real_row = (row == 0) & (s == 0)
    out_re = jnp.where(real_row, both_re, both_re - sign * both_im)
    out_im = jnp.where(real_row, both_im, left_im * right_re + sign * left_re * right_im)
    return jnp.concatenate([out_re, out_im], axis=0).astype(BF16)


def conv_kernel(
    first_ref, mid_ref, back_ref, last_ref, u_ref, t_ref, out_ref, su_out, st_out, *refs
):
    y_ref, z_ref, su_ref, st_ref, sems = refs
    count1, count2, cols = y_ref.shape
    stage_first(first_ref, u_ref, y_ref)
    stage_first(first_ref, t_ref, z_ref)

    def slot_step(s, carry):
        pair = pl.ds(2 * s, 2)
        spec_u = times(mid_ref[s], y_ref[pair].reshape(2 * count2, cols))
        spec_t = times(mid_ref[s], z_ref[pair].reshape(2 * count2, cols))
        su_ref[pair] = spec_u.astype(BF16).reshape(2, count2, cols)
        st_ref[pair] = spec_t.astype(BF16).reshape(2, count2, cols)
        product = spectral_product(
            s, spec_u[:count2], spec_u[count2:], spec_t[:count2], spec_t[count2:], 1
        )
        z_ref[pair] = times(back_ref[s], product).astype(BF16).reshape(2, count2, cols)
        return carry

    lax.fori_loop(0, count1 // 2, slot_step, 0, unroll=2)
    stores = [
        pltpu.make_async_copy(su_ref, su_out, sems.at[0]),
        pltpu.make_async_copy(st_ref, st_out, sems.at[1]),
    ]
    for copy in stores:
        copy.start()
    stage_last(last_ref, z_ref, out_ref)
    for copy in stores:
        copy.wait()


def conv_back_kernel(
    first_ref, mid_ref, back_ref, last_ref, g_ref, su_any, st_any, *refs
):
    du_ref, dt_ref, y_ref, z_ref, x_ref, su_ref, st_ref, sems = refs
    count1, count2, cols = y_ref.shape
    loads = [
        pltpu.make_async_copy(su_any, su_ref, sems.at[0]),
        pltpu.make_async_copy(st_any, st_ref, sems.at[1]),
    ]
    for copy in loads:
        copy.start()
    stage_first(first_ref, g_ref, y_ref)

    for copy in loads:
        copy.wait()

    def slot_step(s, carry):
        pair = pl.ds(2 * s, 2)
        spec_g = times(mid_ref[s], y_ref[pair].reshape(2 * count2, cols))
        spec_u = su_ref[pair].astype(F32)
        spec_t = st_ref[pair].astype(F32)
        product = spectral_product(s, spec_g[:count2], spec_g[count2:], spec_t[0], spec_t[1], -1)
        y_ref[pair] = times(back_ref[s], product).astype(BF16).reshape(2, count2, cols)
        product = spectral_product(s, spec_g[:count2], spec_g[count2:], spec_u[0], spec_u[1], -1)
        z_ref[pair] = times(back_ref[s], product).astype(BF16).reshape(2, count2, cols)
        return carry

    lax.fori_loop(0, count1 // 2, slot_step, 0, unroll=2)
    stage_last(last_ref, y_ref, x_ref)
    stage_last(last_ref, z_ref, dt_ref)
    groups, rows, _ = du_ref.shape
    rows -= CHUNK
    step = count1 // 2 // groups
    for place in range(groups):
        block = x_ref[place * step : (place + 1) * step]
        du_ref[place, :rows, :] = block.reshape(rows, cols)
        du_ref[place, rows:, :] = x_ref[(place + 1) % groups * step, :CHUNK, :]


def kernel_call(kernel, name, outs, in_specs, scratch, flops, size, limit, args, copied=()):
    return pl.pallas_call(
        kernel,
        out_shape=tuple(jax.ShapeDtypeStruct(shape, dtype) for shape, dtype in outs),
        in_specs=in_specs,
        out_specs=tuple(HBM_SPEC if n in copied else VMEM_SPEC for n in range(len(outs))),
        scratch_shapes=scratch,
        compiler_params=pltpu.CompilerParams(vmem_limit_bytes=limit << 20),
        cost_estimate=pl.CostEstimate(flops=flops, bytes_accessed=size << 20, transcendentals=0),
        name=name,
    )(*args)


def long_conv(tables, signal, taps):
    seq_len, cols = taps.shape
    count1 = FIRST_FACTOR
    count2 = 2 * seq_len // count1
    timed = (count1 // 2, count2, cols)
    spectral = (count1, count2, cols)
    out, spec_u, spec_t = kernel_call(
        conv_kernel,
        "long_conv",
        [(timed, BF16), (spectral, BF16), (spectral, BF16)],
        [VMEM_SPEC] * 6,
        [pltpu.VMEM(spectral, BF16)] * 4 + [pltpu.SemaphoreType.DMA((2,))],
        9_000_000_000,
        14,
        40,
        (*tables, signal.reshape(timed), taps.reshape(timed)),
        copied=(1, 2),
    )
    return out.reshape(signal.shape), spec_u, spec_t


def long_conv_back(tables, grad, spec_u, spec_t):
    groups, rows, cols = grad.shape
    count1 = FIRST_FACTOR
    count2 = 2 * groups * rows // count1
    timed = (count1 // 2, count2, cols)
    spectral = (count1, count2, cols)
    grad_u, grad_t = kernel_call(
        conv_back_kernel,
        "long_conv_back",
        [((groups, rows + CHUNK, cols), BF16), (timed, F32)],
        [VMEM_SPEC] * 5 + [HBM_SPEC] * 2,
        [pltpu.VMEM(spectral, BF16)] * 2
        + [pltpu.VMEM(timed, BF16)]
        + [pltpu.VMEM(spectral, BF16)] * 2
        + [pltpu.SemaphoreType.DMA((2,))],
        9_000_000_000,
        14,
        40,
        (*tables, grad.reshape(timed), spec_u, spec_t),
    )
    return grad_u, grad_t.reshape(groups * rows, cols)


def shift_mp(values_in, count):
    size = lax.axis_size("mp")
    return lax.ppermute(values_in, "mp", [(i, (i + count) % size) for i in range(size)])


def swap_dp(values_in, bit):
    size = lax.axis_size("dp")
    return lax.ppermute(values_in, "dp", [(i, i ^ (1 << bit)) for i in range(size)])


def bit_orders():
    bits = lax.axis_size("dp").bit_length() - 1
    high = list(range(1, bits))
    return [0] + high, [0] + high[::-1]


def after(values_in, *others):
    return lax.optimization_barrier((values_in,) + others)[0]


def gather_offsets(half):
    first, second = ((4, 2), (2, 4))[half]
    return [(0, first), (second, first | second), (1, first | 1), (second | 1, first | second | 1)]


def gather_start(block, half, *beside):
    bit = bit_orders()[half][2]
    return jnp.stack([after(block, *beside) if beside else block, swap_dp(block, bit)])


def gather_rest(pair, half, *beside):
    others = swap_dp(pair, bit_orders()[half][1])
    if beside:
        others = after(others, *beside)
    return [pair, others, swap_dp(pair, 0), swap_dp(others, 0)]


def split_blocks(pieces, axis, rows, *beside):
    out = []
    for half in range(2):
        part = lax.slice_in_dim(pieces, half * rows, (half + 1) * rows, axis=axis)
        out.extend(gather_rest(gather_start(part, half), half, *beside))
    return out


def add_across(part, bit, *beside):
    keep = after(part[0], *beside) if beside else part[0]
    return (keep.astype(F32) + swap_dp(part[1], bit).astype(F32)).astype(BF16)


def sum_groups(mine):
    total = mine[0].astype(F32)
    for k in range(1, lax.axis_size("mp")):
        total = total + shift_mp(mine[k], -k).astype(F32)
    return total


def own_group(grads):
    return lax.psum(sum_groups(grads), "dp")


def each_block(here, blocks):
    for half in range(2):
        for n, offsets in enumerate(gather_offsets(half)):
            for i, offset in enumerate(offsets):
                yield blocks[4 * half + n].at[i], half, here ^ offset


def place_feed_kernel(here_ref, *refs):
    *blocks, expand_ref, reduce_ref = refs
    share = blocks[0].shape[1]
    for block, half, index in each_block(here_ref[0], blocks):
        place = pl.ds(pl.multiple_of(index * share, share), share)
        if half == 0:
            expand_ref[:, place] = block[...].astype(F32).T
        else:
            reduce_ref[place, :] = block[...].astype(F32)


def place_input_kernel(here_ref, *refs):
    *blocks, input_ref, output_ref, full_ref = refs
    rows = blocks[0].shape[2]
    parts = full_ref.shape[0]
    for block, half, index in each_block(here_ref[0], blocks):
        place = pl.ds(pl.multiple_of((index * 2 + half) * rows, rows), rows)
        full_ref[:, place, :] = block[:parts].astype(F32)
        output_ref[place, :] = block[parts].astype(F32)
    for p in range(parts):
        input_ref[p] = full_ref[p].T


def sum_dp(values_in):
    for bit in range(lax.axis_size("dp").bit_length() - 1):
        values_in = values_in + swap_dp(values_in, bit)
    return values_in


def contract_rows(left, right):
    return lax.dot_general(left, right, (((0,), (0,)), ((), ())), preferred_element_type=F32)


def contract_cols(left, right):
    return lax.dot_general(left, right, (((1,), (1,)), ((), ())), preferred_element_type=F32)


def gelu_parts(value):
    factor = math.sqrt(2.0 / math.pi)
    square = value * value
    tanh_part = jnp.tanh(factor * value * (1.0 + 0.044715 * square))
    half = 0.5 * (1.0 + tanh_part)
    slope = half + 0.5 * value * (1.0 - tanh_part * tanh_part) * (
        factor * (1.0 + 3.0 * 0.044715 * square)
    )
    return value * half, slope


ROW_STEP = 32
SMALL_ROWS = 32


def fold_rows(wide_ref, narrow_ref):
    channels = narrow_ref.shape[1]
    for i in range(wide_ref.shape[1] // channels):
        narrow_ref[8 * i : 8 * i + 8, :] = wide_ref[:, i * channels : (i + 1) * channels]


def unfold_rows(narrow):
    rows, channels = narrow.shape
    return narrow.reshape(rows // 8, 8, channels).transpose(1, 0, 2).reshape(8, -1)


def store_grad(refs, k, part, here, values):
    rows = values.shape[0] // 8
    for i in range(4):
        bit1, bit2 = (i & 1) ^ (here >> 1 & 1), (i >> 1) ^ (here >> 2)
        first, second = (bit2, bit1) if k < 2 else (bit1, bit2)
        pair = [values[(2 * i + n) * rows : (2 * i + n + 1) * rows].astype(BF16) for n in range(2)]
        even = here & 1 == 0
        refs[0][k // 2, first, second, part] = jnp.where(even, pair[0], pair[1])
        refs[1][k // 2, first, second, part] = jnp.where(even, pair[1], pair[0])


def start_input_weights(here_ref, local, blocks, weight_ref, sem):
    others = pl.ds(1, weight_ref.shape[0] - 1)
    pltpu.make_async_copy(local, weight_ref.at[0], sem).start()
    if len(blocks) == 1:
        pltpu.make_async_copy(blocks[0], weight_ref.at[others], sem).start()
        return
    rows = blocks[0].shape[3]
    for block, half, index in each_block(here_ref[0], blocks):
        start = pl.multiple_of((index * 2 + half) * rows, rows)
        pltpu.make_async_copy(block, weight_ref.at[others, :, pl.ds(start, rows)], sem).start()


def group_at(here_ref, k, groups):
    return lax.rem(here_ref[1] + (groups - k), groups)


def wait_whole(ref, sem):
    pltpu.make_async_copy(ref, ref, sem).wait()


def enter_kernel(count, here_ref, input_ref, halo_ref, vectors_ref, small_ref, local_ref, *refs):
    blocks = refs[:count]
    outs = refs[count : count + 5]
    weight_ref, rows_ref, sem, *results, out_sems = refs[count + 5 :]
    conv_input_ref, second_ref, gates_ref, projected_ref, normed_ref = results

    def store(n, k):
        return pltpu.make_async_copy(results[n].at[k], outs[n].at[k], out_sems.at[n, k])

    store_normed = pltpu.make_async_copy(normed_ref, outs[4], out_sems.at[4, 0])
    rows = input_ref.shape[0]
    groups, _, channels = conv_input_ref.shape
    start_input_weights(here_ref, local_ref, blocks, weight_ref, sem)

    def normed(values):
        return (norm_parts(values)[0] * vectors_ref[0:1] + vectors_ref[1:2]).astype(BF16)

    rows_ref[:CHUNK, :] = normed(halo_ref[...])

    def norm_step(i, carry):
        start = pl.multiple_of(i * ROW_STEP, ROW_STEP)
        values = normed(input_ref[pl.ds(start, ROW_STEP), :])
        normed_ref[pl.ds(start, ROW_STEP), :] = values
        rows_ref[pl.ds(start + CHUNK, ROW_STEP), :] = values
        return carry

    lax.fori_loop(0, rows // ROW_STEP, norm_step, 0)
    store_normed.start()
    wait_whole(weight_ref, sem)
    row = lax.broadcasted_iota(jnp.int32, (rows + CHUNK, channels), 0)
    begins = (row < CHUNK) & (here_ref[1] == 0)
    for k in range(groups):
        mixed = []
        for p in range(3):
            small = small_ref[k, 8 * p : 8 * p + 8, :]
            values = contract_cols(rows_ref[...], weight_ref[k, p]) + small[0:1]
            values = jnp.where(begins, 0.0, values)
            projected_ref[k, p] = values.astype(BF16)
            mixed.append(
                small[1:2] * values[CHUNK:]
                + small[2:3] * values[CHUNK - 1 : -1]
                + small[3:4] * values[CHUNK - 2 : -2]
                + small[4:5]
            )
        group = group_at(here_ref, k, groups)
        conv_input_ref[group] = (mixed[1] * mixed[0]).astype(BF16)
        gates_ref[k, 0] = mixed[0].astype(BF16)
        gates_ref[k, 1] = mixed[1].astype(BF16)
        second_ref[k] = mixed[2].astype(BF16)
        for n in range(4):
            store(n, group if n == 0 else k).start()
    store_normed.wait()
    for k in range(groups):
        for n in range(4):
            store(n, k).wait()


def enter(here, block_input, halo, vectors, small, local, blocks):
    rows, width = block_input.shape
    parts, channels, _ = local.shape
    groups = small.shape[0]
    outs = [
        ((groups, rows, channels), BF16),
        ((groups, rows, channels), BF16),
        ((groups, 2, rows, channels), BF16),
        ((groups, parts, rows + CHUNK, channels), BF16),
        ((rows, width), BF16),
    ]
    return kernel_call(
        functools.partial(enter_kernel, len(blocks)),
        "enter",
        outs,
        [SMEM_SPEC] + [VMEM_SPEC] * 4 + [ANY_SPEC] * (1 + len(blocks)),
        [
            pltpu.VMEM((groups, parts, channels, width), BF16),
            pltpu.VMEM((rows + CHUNK, width), BF16),
            pltpu.SemaphoreType.DMA,
            *[pltpu.VMEM(shape, dtype) for shape, dtype in outs],
            pltpu.SemaphoreType.DMA((5, groups)),
        ],
        2 * rows * width * parts * groups * channels,
        16,
        40,
        (here, block_input, halo, vectors, small, local, *blocks),
        copied=(0, 1, 2, 3, 4),
    )


def middle_kernel(count, sorted_units, here_ref, *refs):
    long_ref, conv_ref, second_ref, input_ref, cot_ref, vectors_ref, small_ref, bias_ref = refs[:8]
    expand_local, reduce_local, output_local = refs[8:11]
    blocks = refs[11 : 11 + count]
    (
        result_ref,
        hidden_grad_ref,
        conv_grad_ref,
        second_grad_ref,
        gated_ref,
        act_ref,
        pre_grad_ref,
        normed_ref,
        mix_ref,
        out_low_ref,
        bias_grad_ref,
        all_sums_ref,
        skip_grad_ref,
    ) = refs[11 + count : 24 + count]
    expand_ref, reduce_ref, output_ref, normal_ref, scale_ref, sums_ref, sems = refs[
        24 + count : 31 + count
    ]
    early_outs = (act_ref, pre_grad_ref, normed_ref, out_low_ref)
    act_ref, pre_grad_ref, normed_ref, out_low_ref, out_sems = refs[31 + count :]
    stores = [
        pltpu.make_async_copy(source, target, out_sems.at[n])
        for n, (source, target) in enumerate(
            zip((act_ref, pre_grad_ref, normed_ref, out_low_ref), early_outs)
        )
    ]
    rows, width = input_ref.shape
    groups, hidden, _ = expand_ref.shape
    channels = output_ref.shape[1]
    others = pl.ds(1, groups - 1)
    here = here_ref[0]

    pltpu.make_async_copy(output_local, output_ref.at[0], sems.at[0]).start()
    pltpu.make_async_copy(expand_local, expand_ref.at[0], sems.at[1]).start()
    pltpu.make_async_copy(reduce_local, reduce_ref.at[0], sems.at[2]).start()
    if sorted_units:
        share = hidden // 8
        half_share = channels // 16
        for block, half, index in each_block(here, blocks):
            ref = (expand_ref, reduce_ref)[half]
            start = pl.multiple_of((index * 2 + half) * half_share, half_share)
            pltpu.make_async_copy(
                block.at[:, pl.ds(share, half_share)],
                output_ref.at[others, pl.ds(start, half_share)],
                sems.at[0],
            ).start()
            start = pl.multiple_of(index * share, share)
            pltpu.make_async_copy(
                block.at[:, pl.ds(0, share)],
                ref.at[others, pl.ds(start, share)],
                sems.at[1 + half],
            ).start()
    else:
        for n, (block, ref) in enumerate(zip(blocks, (output_ref, expand_ref, reduce_ref))):
            pltpu.make_async_copy(block, ref.at[others], sems.at[n]).start()

    position = here_ref[1] * rows + lax.broadcasted_iota(jnp.int32, (rows, channels), 0)
    mask = jnp.where(position < here_ref[2], 1.0, 0.0)

    def conv_out(k):
        skip = small_ref[k, 24:25, :]
        group = group_at(here_ref, k, groups)
        return long_ref[group].astype(F32) + skip * conv_ref[group].astype(F32)

    for k in range(groups):
        gated = mask * second_ref[k].astype(F32) * conv_out(k)
        gated_ref[:, k * channels : (k + 1) * channels] = gated.astype(BF16)
    wait_whole(output_ref, sems.at[0])
    mixed = times(gated_ref[...], output_ref[...].reshape(groups * channels, width))
    result_ref[...] = input_ref[...] + mixed + vectors_ref[0:1]
    sums_ref[...] = jnp.zeros_like(sums_ref)

    def norm_step(i, carry):
        part = pl.ds(pl.multiple_of(i * ROW_STEP, ROW_STEP), ROW_STEP)
        values = result_ref[part, :]
        normal, scale = norm_parts(values)
        normal_ref[part, :] = normal
        scale_ref[part, :] = scale
        normed_ref[part, :] = (normal * vectors_ref[1:2] + vectors_ref[2:3]).astype(BF16)
        cot = cot_ref[part, :]
        out_low_ref[part, :] = cot.astype(BF16)
        result_ref[part, :] = values + vectors_ref[3:4]
        hidden_grad_ref[part, :] = jnp.zeros_like(cot)
        sums_ref[0:1, :] += jnp.sum(cot, axis=0, keepdims=True)
        return carry

    lax.fori_loop(0, rows // ROW_STEP, norm_step, 0)
    wait_whole(expand_ref, sems.at[1])
    wait_whole(reduce_ref, sems.at[2])
    per_step = hidden // 2

    def store_units(ref, k, half, values):
        if not sorted_units:
            start = pl.multiple_of((lax.rem(k, 2) * 2 + half) * per_step, per_step)
            ref[k // 2, :, pl.ds(start, per_step)] = values
            return
        share = hidden // 8
        for i in range(4):
            bit0 = (here & 1) ^ (i & 1)
            bit1 = ((here >> 1) & 1) ^ (i >> 1)
            bit2 = ((here >> 2) & 1) ^ half
            outer = jnp.where(k < 2, bit2 * 2 + bit1, bit1 * 2 + bit2)
            start = ((k // 2 * 4 + outer) * 2 + lax.rem(k, 2)) * share
            columns = pl.ds(pl.multiple_of(start, share), share)
            ref[bit0, :, columns] = values[:, i * share : (i + 1) * share]

    def hidden_step(j, carry):
        k, half = j // 2, lax.rem(j, 2)
        units = pl.ds(pl.multiple_of(half * per_step, per_step), per_step)
        expand = expand_ref[k, units, :]
        reduce = reduce_ref[k, units, :]
        value, slope = gelu_parts(contract_cols(normed_ref[...], expand) + bias_ref[j])
        value = value.astype(BF16)
        store_units(act_ref, k, half, value)
        result_ref[...] += times(value, reduce)
        grad = (contract_cols(out_low_ref[...], reduce) * slope).astype(BF16)
        store_units(pre_grad_ref, k, half, grad)
        bias_grad_ref[j] = jnp.sum(grad.astype(F32), axis=0, keepdims=True)
        hidden_grad_ref[...] += times(grad, expand)
        return carry

    lax.fori_loop(0, 2 * groups, hidden_step, 0)
    for copy in stores:
        copy.start()

    def back_step(i, carry):
        part = pl.ds(pl.multiple_of(i * ROW_STEP, ROW_STEP), ROW_STEP)
        res_part, gain_sum, shift_sum = norm_back(
            normal_ref[part, :], scale_ref[part, :], vectors_ref[1:2], hidden_grad_ref[part, :]
        )
        hidden_grad = cot_ref[part, :] + res_part
        hidden_grad_ref[part, :] = hidden_grad
        mix_ref[part, :] = hidden_grad.astype(BF16)
        sums_ref[1:2, :] += gain_sum[None]
        sums_ref[2:3, :] += shift_sum[None]
        sums_ref[3:4, :] += jnp.sum(hidden_grad, axis=0, keepdims=True)
        return carry

    lax.fori_loop(0, rows // ROW_STEP, back_step, 0)
    fold_rows(sums_ref, all_sums_ref)
    for k in range(groups):
        group = group_at(here_ref, k, groups)
        masked_grad = contract_cols(mix_ref[...], output_ref[k]) * mask
        second_grad_ref[k] = (masked_grad * conv_out(k)).astype(BF16)
        conv_grad = (masked_grad * second_ref[k].astype(F32)).astype(BF16)
        conv_grad_ref[group] = conv_grad
        products = conv_grad.astype(F32) * conv_ref[group].astype(F32)
        skip_grad_ref[k] = jnp.sum(products, axis=0, keepdims=True)
    for copy in stores:
        copy.wait()


def grad_shapes(groups, channels, width, split, parts):
    if split:
        return [((2, 2, 2, groups // 2 * parts, channels // 8, width), BF16)] * 2
    return [((groups * parts, channels, width), BF16), ((8, 128), BF16)]


def middle(
    here, long_out, conv_input, second, block_input, cotangent, vectors, small, bias, local, blocks
):
    rows, width = block_input.shape
    groups, _, channels = small.shape
    hidden = local[0].shape[0]
    grouped = ((groups, rows, channels), BF16)
    square = ((rows, width), BF16)
    wide = ((2, rows, groups * hidden // 2), BF16)
    outs = (
        [((rows, width), F32)] * 2
        + [grouped, grouped, square, wide, wide, square, square, square]
        + [((2 * groups, 1, hidden // 2), F32)]
        + [((8 * width // channels, channels), F32), ((groups, 1, channels), F32)]
    )
    return kernel_call(
        functools.partial(middle_kernel, len(blocks), len(blocks) == 8),
        "middle",
        outs,
        [SMEM_SPEC] + [VMEM_SPEC] * 8 + [ANY_SPEC] * (3 + len(blocks)),
        [
            pltpu.VMEM((groups, hidden, width), BF16),
            pltpu.VMEM((groups, hidden, width), BF16),
            pltpu.VMEM((groups, channels, width), BF16),
            pltpu.VMEM((rows, width), F32),
            pltpu.VMEM((rows, 1), F32),
            pltpu.VMEM((8, width), F32),
            pltpu.SemaphoreType.DMA((3,)),
            pltpu.VMEM(wide[0], BF16),
            pltpu.VMEM(wide[0], BF16),
            pltpu.VMEM((rows, width), BF16),
            pltpu.VMEM((rows, width), BF16),
            pltpu.SemaphoreType.DMA((4,)),
        ],
        20_000_000_000,
        48,
        62,
        (
            here,
            long_out,
            conv_input,
            second,
            block_input,
            cotangent,
            vectors,
            small,
            bias,
            *local,
            *blocks,
        ),
        copied=(5, 6, 7, 9),
    )


def leave_kernel(count, here_ref, *refs):
    (
        du_ref,
        conv_grad_ref,
        halo_gates_ref,
        halo_grads_ref,
        small_ref,
        vectors_ref,
        normed_ref,
        gated_ref,
        mix_ref,
        skip_grad_ref,
        bias_grad_ref,
        second_grad_any,
        gates_any,
        projected_any,
        input_any,
        hidden_grad_any,
        local_ref,
    ) = refs[:17]
    blocks = refs[17 : 17 + count]
    input_grad_ref, small_grad_ref, all_sums_ref, *weight_outs = refs[17 + count : 22 + count]
    low_ref, weight_ref, sums_ref, sem, *rest = refs[22 + count :]
    second_grad_ref, gates_ref, projected_ref, input_ref, hidden_grad_ref = rest[:5]
    sems, out_sems = rest[5:7]
    weight_grads = rest[7:]
    rows, width = input_ref.shape
    groups = small_ref.shape[0]
    channels = small_ref.shape[2]
    loads = [
        [
            pltpu.make_async_copy(source.at[k], target.at[k], sems.at[n, k])
            for n, (source, target) in enumerate(
                (
                    (second_grad_any, second_grad_ref),
                    (gates_any, gates_ref),
                    (projected_any, projected_ref),
                )
            )
        ]
        for k in range(groups)
    ]
    late_loads = [
        pltpu.make_async_copy(input_any, input_ref, sems.at[3, 0]),
        pltpu.make_async_copy(hidden_grad_any, hidden_grad_ref, sems.at[3, 1]),
    ]
    for copy in loads[0] + loads[1]:
        copy.start()
    start_input_weights(here_ref, local_ref, blocks, weight_ref, sem)
    for copy in loads[2] + loads[3] + late_loads:
        copy.start()
    row = lax.broadcasted_iota(jnp.int32, (rows + CHUNK, channels), 0)
    ends = (row >= rows) & (here_ref[1] == groups - 1)
    small_grad_ref[...] = jnp.zeros_like(small_grad_ref)

    def keep_grad(k, p, weight_grad):
        if count > 1:
            store_grad(weight_grads, k, k % 2 * 4 + p, here_ref[0], weight_grad)
        else:
            weight_grads[0][4 * k + p] = weight_grad.astype(BF16)

    for k in range(groups):
        nk = (k + 1) % groups
        for copy in loads[k]:
            copy.wait()

        def extended(values, halo):
            return jnp.concatenate([values, halo], axis=0).astype(F32)

        group = group_at(here_ref, k, groups)
        conv_grad = extended(conv_grad_ref[group], halo_grads_ref[0, group])
        skip = small_ref[k, 24:25, :]
        input_side = du_ref[group].astype(F32) + skip * conv_grad
        grads = (
            input_side * extended(gates_ref[k, 1], halo_gates_ref[nk, 1]),
            input_side * extended(gates_ref[k, 0], halo_gates_ref[nk, 0]),
            extended(second_grad_ref[k], halo_grads_ref[1, nk]),
        )
        for p, grad in enumerate(grads):
            grad = jnp.where(ends, 0.0, grad)
            small = small_ref[k, 8 * p : 8 * p + 8, :]
            low = (
                small[1:2] * grad[:rows]
                + small[2:3] * grad[1 : rows + 1]
                + small[3:4] * grad[2 : rows + 2]
            ).astype(BF16)
            low_ref[:, (3 * k + p) * channels : (3 * k + p + 1) * channels] = low
            keep_grad(k, p, contract_rows(low, normed_ref[...]))
            projected = projected_ref[k, p].astype(F32)
            own = grad[:rows]
            small_grad_ref[k, 8 * p : 8 * p + 1, :] = jnp.sum(
                low.astype(F32), axis=0, keepdims=True
            )
            for tap in range(3):
                delayed = projected[CHUNK - tap : rows + CHUNK - tap]
                small_grad_ref[k, 8 * p + 1 + tap : 8 * p + 2 + tap, :] = jnp.sum(
                    own * delayed, axis=0, keepdims=True
                )
            small_grad_ref[k, 8 * p + 4 : 8 * p + 5, :] = jnp.sum(own, axis=0, keepdims=True)
        gated = gated_ref[:, k * channels : (k + 1) * channels]
        keep_grad(k, 3, contract_rows(gated, mix_ref[...]))
        small_grad_ref[k, 24:25, :] = skip_grad_ref[k]
        per_half = bias_grad_ref.shape[2] // channels
        for n in range(2 * per_half):
            bias_row = bias_grad_ref[2 * k + n // per_half]
            first = n % per_half * channels
            small_grad_ref[k, 25 + n : 26 + n, :] = bias_row[:, first : first + channels]
        if count > 1 and k % 2 == 1:
            for n in range(2):
                pltpu.make_async_copy(
                    weight_grads[n].at[k // 2], weight_outs[n].at[k // 2], out_sems.at[n, k // 2]
                ).start()
    if count == 1:
        for n in range(2):
            pltpu.make_async_copy(weight_grads[n], weight_outs[n], out_sems.at[n, 0]).start()
    wait_whole(weight_ref, sem)
    input_grad_ref[...] = times(
        low_ref[...], weight_ref[...].reshape(groups * 3 * channels, width)
    )
    sums_ref[...] = jnp.zeros_like(sums_ref)
    for copy in late_loads:
        copy.wait()

    def back_step(i, carry):
        part = pl.ds(pl.multiple_of(i * ROW_STEP, ROW_STEP), ROW_STEP)
        normal, scale = norm_parts(input_ref[part, :])
        input_part, gain_sum, shift_sum = norm_back(
            normal, scale, vectors_ref[0:1], input_grad_ref[part, :]
        )
        input_grad_ref[part, :] = hidden_grad_ref[part, :] + input_part
        sums_ref[0:1, :] += gain_sum[None]
        sums_ref[1:2, :] += shift_sum[None]
        return carry

    lax.fori_loop(0, rows // ROW_STEP, back_step, 0)
    fold_rows(sums_ref, all_sums_ref)
    for n in range(2):
        if count > 1:
            for half in range(2):
                pltpu.make_async_copy(
                    weight_grads[n].at[half], weight_outs[n].at[half], out_sems.at[n, half]
                ).wait()
        else:
            pltpu.make_async_copy(weight_grads[n], weight_outs[n], out_sems.at[n, 0]).wait()


def leave(
    here,
    conv_input_grad,
    conv_grad,
    second_grad,
    gates,
    projected,
    halo_gates,
    halo_grads,
    small,
    block_input,
    hidden_grad,
    vectors,
    normed,
    gated,
    mix_low,
    skip_grad,
    bias_grad,
    local,
    blocks,
):
    rows, width = block_input.shape
    groups, _, channels = small.shape
    grads = grad_shapes(groups, channels, width, len(blocks) > 1, 4)
    outs = [
        ((rows, width), F32),
        ((groups, SMALL_ROWS, channels), F32),
        ((8 * width // channels, channels), F32),
        *grads,
    ]
    return pl.pallas_call(
        functools.partial(leave_kernel, len(blocks)),
        out_shape=tuple(jax.ShapeDtypeStruct(shape, dtype) for shape, dtype in outs),
        in_specs=[SMEM_SPEC] + [VMEM_SPEC] * 11 + [HBM_SPEC] * 5 + [ANY_SPEC] * (1 + len(blocks)),
        out_specs=(VMEM_SPEC,) * 3 + (HBM_SPEC,) * 2,
        scratch_shapes=[
            pltpu.VMEM((rows, 3 * groups * channels), BF16),
            pltpu.VMEM((groups, 3, channels, width), BF16),
            pltpu.VMEM((8, width), F32),
            pltpu.SemaphoreType.DMA,
            *[
                pltpu.VMEM(a.shape, a.dtype)
                for a in (second_grad, gates, projected, block_input, hidden_grad)
            ],
            pltpu.SemaphoreType.DMA((4, groups)),
            pltpu.SemaphoreType.DMA((2, 2)),
            *[pltpu.VMEM(shape, dtype) for shape, dtype in grads],
        ],
        compiler_params=pltpu.CompilerParams(vmem_limit_bytes=60 << 20),
        cost_estimate=pl.CostEstimate(
            flops=16_000_000_000, bytes_accessed=34 << 20, transcendentals=0
        ),
        name="leave",
    )(
        here,
        conv_input_grad,
        conv_grad,
        halo_gates,
        halo_grads,
        small,
        vectors,
        normed,
        gated,
        mix_low,
        skip_grad,
        bias_grad,
        second_grad,
        gates,
        projected,
        block_input,
        hidden_grad,
        local,
        *blocks,
    )


def per_device(
    block_input,
    lengths,
    mixer_gain,
    mixer_shift,
    input_weight,
    input_bias,
    conv_weight,
    conv_bias,
    enter_weight,
    enter_bias,
    middle_weight,
    middle_bias,
    inner_weight,
    inner_bias,
    frequency,
    filter_weight,
    skip_scale,
    output_weight,
    output_bias,
    feed_gain,
    feed_shift,
    expand_weight,
    expand_bias,
    reduce_weight,
    reduce_bias,
    cotangent,
):
    own_rows, width = block_input.shape
    channels = input_weight.shape[2]
    hidden = expand_weight.shape[1]
    mp_size = lax.axis_size("mp")
    dp_size = lax.axis_size("dp")
    mp_here = lax.axis_index("mp")
    dp_here = lax.axis_index("dp")
    seq_len = own_rows * mp_size
    split = dp_size == 8
    share = hidden // dp_size
    out_share = channels // dp_size
    here = jnp.stack([dp_here, mp_here, lengths[0]]).astype(jnp.int32)

    small_own = jnp.concatenate(
        [
            jnp.concatenate(
                [input_bias[:, None], conv_weight.transpose(1, 0, 2), conv_bias[:, None]]
                + [jnp.zeros((3, 3, channels), F32)],
                axis=1,
            ).reshape(24, channels),
            skip_scale[None],
            expand_bias.reshape(-1, channels),
        ]
    )
    small_own = jnp.pad(small_own, ((0, SMALL_ROWS - small_own.shape[0]), (0, 0)))

    def other_groups(values):
        return jnp.stack([shift_mp(values, k) for k in range(1, mp_size)])

    def turned_groups(stacked, start, sign):
        return jnp.concatenate(
            [
                lax.dynamic_slice_in_dim(stacked, (mp_here + sign * k) % mp_size, 1, 0)
                for k in range(start, mp_size)
            ]
        )

    features = position_features(seq_len, enter_weight.shape[0])
    columns = jnp.stack([enter_bias, middle_bias, inner_bias, frequency], axis=1)
    net_units = frequency.shape[0]
    net_shape = ((3, net_units, seq_len), F32)
    taps_low, *net_values = kernel_call(
        functools.partial(filter_kernel, width),
        "filter_taps",
        [((seq_len, channels), BF16)] + [net_shape] * 3,
        [SMEM_SPEC] + [VMEM_SPEC] * 6,
        [],
        4_000_000_000,
        6,
        32,
        (
            here,
            features,
            jnp.pad(enter_weight, ((0, FEATURE_ROWS - enter_weight.shape[0]), (0, 0))),
            middle_weight,
            inner_weight,
            columns,
            filter_weight,
        ),
    )
    small_rows = jnp.concatenate([small_own, block_input[-CHUNK:].reshape(-1, channels)])
    small_rows = jnp.stack([small_rows] + [shift_mp(small_rows, k) for k in range(1, mp_size)])
    small = small_rows[:, :SMALL_ROWS]
    halo = small_rows[1, SMALL_ROWS:].reshape(CHUNK, width)

    input_turned = input_weight.transpose(1, 2, 0)
    expand_turned = expand_weight.T
    if split:
        input_part = lax.dynamic_slice_in_dim(input_turned, dp_here * out_share, out_share, 1)
        input_pieces = after(other_groups(input_part), small_rows)
        input_blocks = split_blocks(input_pieces, 2, out_share // 2)
    else:
        input_blocks = [other_groups(input_turned)]
    tables = spectral_tables(seq_len)

    if split:
        expand_part = lax.dynamic_slice_in_dim(expand_turned, dp_here * share, share, 0)
        reduce_part = lax.dynamic_slice_in_dim(reduce_weight, dp_here * share, share, 0)
        output_part = lax.dynamic_slice_in_dim(output_weight, dp_here * out_share, out_share, 0)
        half = out_share // 2
        feed_part = jnp.concatenate(
            [expand_part, output_part[:half], reduce_part, output_part[half:]]
        )
        feed_groups = lax.all_gather(after(feed_part, input_pieces), "mp")
    else:
        feed_blocks = [other_groups(w) for w in (output_weight, expand_turned, reduce_weight)]

    mixer_vectors = jnp.stack([mixer_gain, mixer_shift])
    conv_input, second_gate, gates, projected, mixer_normed = enter(
        here,
        block_input,
        halo,
        mixer_vectors,
        small,
        input_turned,
        input_blocks,
    )
    halo_gates = shift_mp(gates[:, :, :CHUNK], -1)

    def exchange(values):
        return lax.all_to_all(values, "mp", 0, 0)

    arrived_input = exchange(conv_input)
    if split:
        feed_pieces = turned_groups(after(feed_groups, conv_input), 1, -1)
        halves = (feed_pieces[:, : share + half], feed_pieces[:, share + half :])
        pairs = [gather_start(part, n, arrived_input) for n, part in enumerate(halves)]
        arrived_input = after(arrived_input, *pairs)
    long_out, spec_u, spec_t = long_conv(tables, arrived_input, taps_low)
    long_out = after(exchange(long_out), halo_gates)
    if split:
        feed_blocks = [
            block for n, pair in enumerate(pairs) for block in gather_rest(pair, n, long_out)
        ]
    vectors = jnp.stack([output_bias, feed_gain, feed_shift, reduce_bias])
    bias = small[:, 25 : 25 + hidden // channels].reshape(2 * mp_size, 1, hidden // 2)
    (
        result,
        hidden_grad,
        conv_grad,
        second_grad,
        gated,
        activated,
        pre_grad,
        feed_normed,
        mix_low,
        out_low,
        bias_grad,
        feed_sums,
        skip_grad,
    ) = middle(
        here,
        long_out,
        conv_input,
        second_gate,
        block_input,
        cotangent,
        vectors,
        small,
        bias,
        (expand_turned, reduce_weight, output_weight),
        feed_blocks,
    )
    halo_grads = shift_mp(jnp.stack([conv_grad[:, :CHUNK], second_grad[:, :CHUNK]]), -1)
    arrived_grad = exchange(conv_grad)

    if split:
        pairs = ((activated, out_low), (pre_grad, feed_normed))
    else:
        def feed_grads(left, right):
            grads = [contract_rows(part, right).astype(BF16) for part in left]
            return own_group(jnp.concatenate(grads).reshape(mp_size, hidden, width))

        reduce_weight_grad = feed_grads(activated, out_low)
        expand_weight_grad = feed_grads(pre_grad, feed_normed).T

    arrived_grad = after(arrived_grad, halo_grads)
    conv_input_grad, taps_grad = long_conv_back(tables, arrived_grad, spec_u, spec_t)
    if split:
        late = [(after(u, taps_grad), right) for u, right in pairs]
        arrived = [
            swap_dp(contract_rows(u[1], right).astype(BF16), 0) for u, right in (pairs[0], late[1])
        ]
        pairs = late
        kept = [
            (contract_rows(u[0], right) + other.astype(F32)).astype(BF16)
            for (u, right), other in zip(pairs, arrived)
        ]
        held = [k.reshape(2, 2, 2, mp_size // 2, share, width) for k in kept]
        first_stages = [
            [jnp.stack([h[n, i] for h in held], axis=1) for i in range(2)] for n in range(2)
        ]
    conv_input_grad = exchange(conv_input_grad)
    if split:
        conv_input_grad = after(
            conv_input_grad, halo_grads, first_stages[0][1], first_stages[1][1]
        )
    input_grad, small_grad, mixer_sums, grads_kept, grads_away = leave(
        here,
        conv_input_grad,
        conv_grad,
        second_grad,
        gates,
        projected,
        halo_gates,
        halo_grads,
        small,
        block_input,
        hidden_grad,
        mixer_vectors,
        mixer_normed,
        gated,
        mix_low,
        skip_grad,
        bias_grad,
        input_turned,
        input_blocks,
    )
    if split:
        held = (grads_kept.astype(F32) + swap_dp(grads_away, 0).astype(F32)).astype(BF16)
        taps_grad = after(taps_grad, held)
    else:
        taps_grad = after(taps_grad, grads_kept)
    net_grads, filter_weight_grad = kernel_call(
        functools.partial(filter_back_kernel, width),
        "filter_back",
        [((net_units, 4 * net_units), F32), ((net_units, channels), F32)],
        [SMEM_SPEC] + [VMEM_SPEC] * 9,
        [pltpu.VMEM((net_units, seq_len), F32)],
        8_000_000_000,
        6,
        32,
        (
            here,
            features,
            middle_weight,
            inner_weight,
            columns,
            filter_weight,
            *net_values,
            taps_grad,
        ),
    )
    packed = [net_grads, feed_sums, mixer_sums, filter_weight_grad]
    packed.append(small_grad.reshape(-1, channels))
    ends = [sum(p.shape[0] for p in packed[:n]) for n in range(len(packed) + 1)]
    packed = jnp.concatenate(packed)
    def small_sums(summed):
        by_group = summed[ends[4] :].reshape(mp_size, SMALL_ROWS, channels)
        return sum_groups(
            [jnp.concatenate([summed[: ends[3]], by_group[k]]) for k in range(mp_size)]
        )

    if split:
        stages = [
            add_across(part, bit, small_grad) for part, bit in zip(first_stages, (2, 1))
        ]
        stages = [add_across(part, bit) for part, bit in zip(stages, (1, 2))]
        feed_grads = jnp.concatenate(stages, axis=1).transpose(1, 0, 2, 3)
        feed_grads = turned_groups(feed_grads, 0, -1).reshape(-1, width)
        feed_total = lax.psum_scatter(feed_grads, "mp", scatter_dimension=0, tiled=True)
        held = [add_across(held[0], 2, net_grads), add_across(held[1], 1, net_grads)]
        packed = after(packed, *held)
        held = [add_across(held[0], 1), add_across(held[1], 2)]
        feed_total = after(feed_total, *held)
        mine = jnp.concatenate(held).reshape(mp_size, 4, out_share, width)
        mine = turned_groups(mine, 0, -1).reshape(-1, width)
        input_total = lax.psum_scatter(mine, "mp", scatter_dimension=0, tiled=True)
        input_total = input_total.reshape(4, out_share, width)
        reduce_total, expand_total = feed_total[:share], feed_total[share:]
        summed = sum_dp(packed)
        blocks = []
        for n, total in enumerate((expand_total, reduce_total)):
            blocks.extend(gather_rest(gather_start(total.astype(BF16), n), n))
        expand_weight_grad, reduce_weight_grad = kernel_call(
            place_feed_kernel,
            "place_feed",
            [((width, hidden), F32), ((hidden, width), F32)],
            [SMEM_SPEC] + [VMEM_SPEC] * len(blocks),
            [],
            0,
            14,
            32,
            (here, *blocks),
        )
        input_total = after(input_total, expand_weight_grad)
        along_mp = small_sums(after(summed, input_total))
        blocks = split_blocks(input_total, 1, out_share // 2)
        input_weight_grad, output_weight_grad = kernel_call(
            place_input_kernel,
            "place_input",
            [((3, width, channels), F32), ((channels, width), F32)],
            [SMEM_SPEC] + [VMEM_SPEC] * len(blocks),
            [pltpu.VMEM((3, channels, width), F32)],
            0,
            8,
            24,
            (here, *blocks),
        )
        input_weight_grad = input_weight_grad.transpose(1, 0, 2)
    else:
        input_total = own_group(grads_kept.reshape(mp_size, 4, channels, width))
        input_weight_grad = input_total[:3].transpose(2, 0, 1)
        output_weight_grad = input_total[3]
        summed = sum_dp(packed)
        along_mp = small_sums(summed)

    everywhere, groups_sum = along_mp[: ends[3]], along_mp[ends[3] :]
    net = everywhere[: ends[1]]
    net_bias = net[:, 3 * net_units :].T
    feed_sums = unfold_rows(everywhere[ends[1] : ends[2]])
    mixer_sums = unfold_rows(everywhere[ends[2] : ends[3]])
    parts = groups_sum[:24].reshape(3, 8, channels)
    return (
        result,
        input_grad,
        mixer_sums[0],
        mixer_sums[1],
        input_weight_grad,
        parts[:, 0],
        parts[:, 1:4].transpose(1, 0, 2),
        parts[:, 4],
        net[: enter_weight.shape[0], :net_units],
        net_bias[0],
        net[:, net_units : 2 * net_units],
        net_bias[1],
        net[:, 2 * net_units : 3 * net_units],
        net_bias[2],
        net_bias[3],
        summed[ends[3] : ends[4]],
        groups_sum[24],
        output_weight_grad,
        feed_sums[3],
        feed_sums[1],
        feed_sums[2],
        expand_weight_grad,
        groups_sum[25 : 25 + hidden // channels].reshape(hidden),
        reduce_weight_grad,
        feed_sums[0],
    )


ROWS = P(("dp", "mp"), None)
FIRST = P("mp", None)
SECOND = P(None, "mp")
THIRD = P(None, None, "mp")


def solution(mesh):
    return jax.shard_map(
        per_device,
        mesh=mesh,
        in_specs=(
            ROWS, P("dp"), P(), P(), THIRD, SECOND, THIRD, SECOND,
            P(), P(), P(), P(), P(), P(), P(), SECOND,
            P("mp"), FIRST, P(), P(), P(), SECOND, P("mp"), FIRST, P(), ROWS,
        ),
        out_specs=(
            ROWS, ROWS, P(), P(), THIRD, SECOND, THIRD, SECOND,
            P(), P(), P(), P(), P(), P(), P(), SECOND,
            P("mp"), FIRST, P(), P(), P(), SECOND, P("mp"), FIRST, P(),
        ),
        check_vma=False,
    )
```

```python
import functools
import math

import jax
import jax.numpy as jnp
import ml_dtypes
import numpy as np
from jax import lax
from jax.experimental import pallas as pl
from jax.experimental.pallas import tpu as pltpu
from jax.sharding import PartitionSpec as P

HIGHEST_MODE = lax.Precision.HIGHEST
EPSILON = 1e-05
FIRST_FACTOR = 64
CHUNK = 16
F32 = jnp.float32
BF16 = jnp.bfloat16
VMEM_SPEC = pl.BlockSpec(memory_space=pltpu.VMEM)
SMEM_SPEC = pl.BlockSpec(memory_space=pltpu.SMEM)
ANY_SPEC = pl.BlockSpec(memory_space=pl.ANY)
HBM_SPEC = pl.BlockSpec(memory_space=pltpu.HBM)


def norm_parts(values_in):
    centred = values_in - jnp.mean(values_in, axis=-1, keepdims=True)
    variance = jnp.mean(centred * centred, axis=-1, keepdims=True)
    scale = lax.rsqrt(variance + EPSILON)
    return centred * scale, scale


def norm_back(normal, scale, gain, grad):
    inner = grad * gain
    part = scale * (
        inner
        - jnp.mean(inner, axis=-1, keepdims=True)
        - normal * jnp.mean(inner * normal, axis=-1, keepdims=True)
    )
    return part, jnp.sum(grad * normal, axis=0), jnp.sum(grad, axis=0)


FEATURE_ROWS = 40
TAP_STEP = 256


def position_features(total, emb_count):
    place = np.arange(total, dtype=np.float64)
    bands = (emb_count - 1) // 2
    freq_grid = 1e-4 + np.arange(bands) * ((bands - 1 - 1e-4) / (bands - 1))
    angles = 2.0 * math.pi / total * freq_grid[:, None] * place[None, :]
    rows = np.concatenate([place[None] / (total - 1), np.cos(angles), -np.sin(angles)])
    rows = np.pad(rows, ((0, FEATURE_ROWS - emb_count), (0, 0)))
    return jnp.asarray(rows.astype(np.float32))


def exact(left, right, left_dim, right_dim):
    dims = (((left_dim,), (right_dim,)), ((), ()))
    return lax.dot_general(
        left, right, dims, precision=HIGHEST_MODE, preferred_element_type=F32
    )


def decay_block(first_row, rows, channels, seq_len, channel_total, group):
    slowest = math.log(0.01) / 1.5
    fastest = math.log(0.01) / 0.3
    row = lax.broadcasted_iota(jnp.int32, (rows, channels), 0) + first_row
    channel = lax.broadcasted_iota(jnp.int32, (rows, channels), 1) + group * channels
    rates = jnp.abs(slowest + (fastest - slowest) * channel.astype(F32) / (channel_total - 1))
    return jnp.exp(-(row.astype(F32) / (seq_len - 1)) * rates)


def filter_kernel(
    channel_total, here_ref, features_ref, enter_ref, middle_ref, inner_ref, columns_ref, filter_ref, *outs
):
    taps_ref, value_ref, sine_ref, cosine_ref = outs
    seq_len, channels = taps_ref.shape
    frequency = columns_ref[:, 3:4]
    hidden = features_ref[...]
    for n, weight_ref in enumerate((enter_ref, middle_ref, inner_ref)):
        value = exact(weight_ref[...], hidden, 0, 0) + columns_ref[:, n : n + 1]
        value_ref[n] = value
        hidden = jnp.sin(frequency * value)
        sine_ref[n] = hidden
        cosine_ref[n] = jnp.cos(frequency * value)
    for start in range(0, seq_len, TAP_STEP):
        rows = slice(start, start + TAP_STEP)
        decay = decay_block(start, TAP_STEP, channels, seq_len, channel_total, here_ref[1])
        taps = exact(sine_ref[2, :, rows], filter_ref[...], 0, 0)
        taps_ref[rows, :] = (taps * decay).astype(BF16)


def filter_back_kernel(
    channel_total,
    here_ref,
    features_ref,
    middle_ref,
    inner_ref,
    columns_ref,
    filter_ref,
    value_ref,
    sine_ref,
    cosine_ref,
    grad_ref,
    packed_ref,
    filter_grad_ref,
    hidden_ref,
):
    seq_len, channels = grad_ref.shape
    units = filter_ref.shape[0]
    frequency = columns_ref[:, 3:4]
    filter_grad_ref[...] = jnp.zeros_like(filter_grad_ref)
    for start in range(0, seq_len, TAP_STEP):
        rows = slice(start, start + TAP_STEP)
        decay = decay_block(start, TAP_STEP, channels, seq_len, channel_total, here_ref[1])
        grad = grad_ref[rows, :] * decay
        filter_grad_ref[...] += exact(sine_ref[2, :, rows], grad, 1, 0)
        hidden_ref[:, rows] = exact(filter_ref[...], grad, 1, 1)
    packed_ref[...] = jnp.zeros_like(packed_ref)
    grad = hidden_ref[...]
    frequency_grad = jnp.zeros((units, 1), F32)
    for n in (2, 1, 0):
        inside = grad * cosine_ref[n]
        frequency_grad += jnp.sum(inside * value_ref[n], axis=1, keepdims=True)
        inside = inside * frequency
        packed_ref[:, 3 * units + n : 3 * units + n + 1] = jnp.sum(inside, axis=1, keepdims=True)
        below = features_ref[...] if n == 0 else sine_ref[n - 1]
        packed_ref[: below.shape[0], n * units : (n + 1) * units] = exact(below, inside, 1, 1)
        if n > 0:
            grad = exact((middle_ref, inner_ref)[n - 1][...], inside, 1, 0)
    packed_ref[:, 3 * units + 3 : 3 * units + 4] = frequency_grad


def spectral_tables(seq_len):
    total = 2 * seq_len
    count1 = FIRST_FACTOR
    count2 = total // count1
    half = count1 // 2
    slot = np.arange(half)
    t1 = np.arange(half)
    t2 = np.arange(count2)
    k2 = np.arange(count2)
    angle = 2 * np.pi * slot[:, None] * t1[None, :] / count1
    first = np.zeros((half, 2, half))
    first[:, 0] = np.cos(angle)
    first[:, 1] = -np.sin(angle)
    first[0, 1] = (-1.0) ** t1
    last = np.zeros((half, half, 2))
    last[:, :, 0] = np.cos(angle.T) / seq_len
    last[:, :, 1] = -np.sin(angle.T) / seq_len
    last[:, 0, 0] = 1.0 / total
    last[:, 0, 1] = (-1.0) ** t1 / total
    mid = np.zeros((half, 2, count2, 2, count2))
    back = np.zeros((half, 2, count2, 2, count2))
    for s in range(1, half):
        turn = np.exp(-2j * np.pi * t2[None, :] * (s / total + k2[:, None] / count2))
        mid[s, 0, :, 0] = turn.real
        mid[s, 0, :, 1] = -turn.imag
        mid[s, 1, :, 0] = turn.imag
        mid[s, 1, :, 1] = turn.real
        undo = np.conj(turn).T
        back[s, 0, :, 0] = undo.real
        back[s, 0, :, 1] = -undo.imag
        back[s, 1, :, 0] = undo.imag
        back[s, 1, :, 1] = undo.real
    h2 = count2 // 2
    turn = np.exp(-2j * np.pi * t2[None, :] * k2[:h2, None] / count2)
    mid[0, 0, :h2, 0] = turn.real
    mid[0, 1, :h2, 0] = turn.imag
    mid[0, 1, 0, 0] = (-1.0) ** t2
    back[0, 0, :, 0, :h2] = 2 * turn.real.T
    back[0, 0, :, 1, :h2] = 2 * turn.imag.T
    back[0, 0, :, 0, 0] = 1.0
    back[0, 0, :, 1, 0] = (-1.0) ** t2
    turn = np.exp(-2j * np.pi * t2[None, :] * (half / total + k2[:h2, None] / count2))
    mid[0, 0, h2:, 1] = turn.real
    mid[0, 1, h2:, 1] = turn.imag
    back[0, 1, :, 0, h2:] = 2 * turn.real.T
    back[0, 1, :, 1, h2:] = 2 * turn.imag.T
    unit = np.eye(CHUNK)
    tables = (
        np.kron(first.reshape(count1, half), unit),
        mid.reshape(half, 2 * count2, 2 * count2),
        back.reshape(half, 2 * count2, 2 * count2),
        np.kron(last.reshape(half, count1), unit),
    )
    return tuple(jnp.asarray(v.astype(np.float32).astype(ml_dtypes.bfloat16)) for v in tables)


def times(left, right):
    return jnp.dot(left, right, preferred_element_type=F32)


def stage_first(first_ref, x_ref, y_ref):
    count1, count2, cols = y_ref.shape
    for j in range(count2 // CHUNK):
        rows = slice(CHUNK * j, CHUNK * (j + 1))
        block = x_ref[:, rows, :].reshape(count1 // 2 * CHUNK, cols)
        y_ref[:, rows, :] = times(first_ref[...], block).reshape(count1, CHUNK, cols).astype(BF16)


def stage_last(last_ref, z_ref, out_ref):
    count1, count2, cols = z_ref.shape
    for j in range(count2 // CHUNK):
        rows = slice(CHUNK * j, CHUNK * (j + 1))
        block = z_ref[:, rows, :].reshape(count1 * CHUNK, cols)
        values = times(last_ref[...], block).reshape(count1 // 2, CHUNK, cols)
        out_ref[:, rows, :] = values.astype(out_ref.dtype)


def spectral_product(s, left_re, left_im, right_re, right_im, sign):
    both_re = left_re * right_re
    both_im = left_im * right_im
    row = lax.broadcasted_iota(jnp.int32, both_re.shape, 0)
    real_row = (row == 0) & (s == 0)
    out_re = jnp.where(real_row, both_re, both_re - sign * both_im)
    out_im = jnp.where(real_row, both_im, left_im * right_re + sign * left_re * right_im)
    return jnp.concatenate([out_re, out_im], axis=0).astype(BF16)


def conv_kernel(
    first_ref, mid_ref, back_ref, last_ref, u_ref, t_ref, out_ref, su_out, st_out, *refs
):
    y_ref, z_ref, su_ref, st_ref, sems = refs
    count1, count2, cols = y_ref.shape
    stage_first(first_ref, u_ref, y_ref)
    stage_first(first_ref, t_ref, z_ref)

    def slot_step(s, carry):
        pair = pl.ds(2 * s, 2)
        spec_u = times(mid_ref[s], y_ref[pair].reshape(2 * count2, cols))
        spec_t = times(mid_ref[s], z_ref[pair].reshape(2 * count2, cols))
        su_ref[pair] = spec_u.astype(BF16).reshape(2, count2, cols)
        st_ref[pair] = spec_t.astype(BF16).reshape(2, count2, cols)
        product = spectral_product(
            s, spec_u[:count2], spec_u[count2:], spec_t[:count2], spec_t[count2:], 1
        )
        z_ref[pair] = times(back_ref[s], product).astype(BF16).reshape(2, count2, cols)
        return carry

    lax.fori_loop(0, count1 // 2, slot_step, 0, unroll=2)
    stores = [
        pltpu.make_async_copy(su_ref, su_out, sems.at[0]),
        pltpu.make_async_copy(st_ref, st_out, sems.at[1]),
    ]
    for copy in stores:
        copy.start()
    stage_last(last_ref, z_ref, out_ref)
    for copy in stores:
        copy.wait()


def conv_back_kernel(
    first_ref, mid_ref, back_ref, last_ref, g_ref, su_any, st_any, *refs
):
    du_ref, dt_ref, y_ref, z_ref, x_ref, su_ref, st_ref, sems = refs
    count1, count2, cols = y_ref.shape
    loads = [
        pltpu.make_async_copy(su_any, su_ref, sems.at[0]),
        pltpu.make_async_copy(st_any, st_ref, sems.at[1]),
    ]
    for copy in loads:
        copy.start()
    stage_first(first_ref, g_ref, y_ref)

    for copy in loads:
        copy.wait()

    def slot_step(s, carry):
        pair = pl.ds(2 * s, 2)
        spec_g = times(mid_ref[s], y_ref[pair].reshape(2 * count2, cols))
        spec_u = su_ref[pair].astype(F32)
        spec_t = st_ref[pair].astype(F32)
        product = spectral_product(s, spec_g[:count2], spec_g[count2:], spec_t[0], spec_t[1], -1)
        y_ref[pair] = times(back_ref[s], product).astype(BF16).reshape(2, count2, cols)
        product = spectral_product(s, spec_g[:count2], spec_g[count2:], spec_u[0], spec_u[1], -1)
        z_ref[pair] = times(back_ref[s], product).astype(BF16).reshape(2, count2, cols)
        return carry

    lax.fori_loop(0, count1 // 2, slot_step, 0, unroll=2)
    stage_last(last_ref, y_ref, x_ref)
    stage_last(last_ref, z_ref, dt_ref)
    groups, rows, _ = du_ref.shape
    rows -= CHUNK
    step = count1 // 2 // groups
    for place in range(groups):
        block = x_ref[place * step : (place + 1) * step]
        du_ref[place, :rows, :] = block.reshape(rows, cols)
        du_ref[place, rows:, :] = x_ref[(place + 1) % groups * step, :CHUNK, :]


def kernel_call(kernel, name, outs, in_specs, scratch, flops, size, limit, args, copied=()):
    return pl.pallas_call(
        kernel,
        out_shape=tuple(jax.ShapeDtypeStruct(shape, dtype) for shape, dtype in outs),
        in_specs=in_specs,
        out_specs=tuple(HBM_SPEC if n in copied else VMEM_SPEC for n in range(len(outs))),
        scratch_shapes=scratch,
        compiler_params=pltpu.CompilerParams(vmem_limit_bytes=limit << 20),
        cost_estimate=pl.CostEstimate(flops=flops, bytes_accessed=size << 20, transcendentals=0),
        name=name,
    )(*args)


def long_conv(tables, signal, taps):
    seq_len, cols = taps.shape
    count1 = FIRST_FACTOR
    count2 = 2 * seq_len // count1
    timed = (count1 // 2, count2, cols)
    spectral = (count1, count2, cols)
    out, spec_u, spec_t = kernel_call(
        conv_kernel,
        "long_conv",
        [(timed, BF16), (spectral, BF16), (spectral, BF16)],
        [VMEM_SPEC] * 6,
        [pltpu.VMEM(spectral, BF16)] * 4 + [pltpu.SemaphoreType.DMA((2,))],
        9_000_000_000,
        14,
        40,
        (*tables, signal.reshape(timed), taps.reshape(timed)),
        copied=(1, 2),
    )
    return out.reshape(signal.shape), spec_u, spec_t


def long_conv_back(tables, grad, spec_u, spec_t):
    groups, rows, cols = grad.shape
    count1 = FIRST_FACTOR
    count2 = 2 * groups * rows // count1
    timed = (count1 // 2, count2, cols)
    spectral = (count1, count2, cols)
    grad_u, grad_t = kernel_call(
        conv_back_kernel,
        "long_conv_back",
        [((groups, rows + CHUNK, cols), BF16), (timed, F32)],
        [VMEM_SPEC] * 5 + [HBM_SPEC] * 2,
        [pltpu.VMEM(spectral, BF16)] * 2
        + [pltpu.VMEM(timed, BF16)]
        + [pltpu.VMEM(spectral, BF16)] * 2
        + [pltpu.SemaphoreType.DMA((2,))],
        9_000_000_000,
        14,
        40,
        (*tables, grad.reshape(timed), spec_u, spec_t),
    )
    return grad_u, grad_t.reshape(groups * rows, cols)


def shift_mp(values_in, count):
    size = lax.axis_size("mp")
    return lax.ppermute(values_in, "mp", [(i, (i + count) % size) for i in range(size)])


def swap_dp(values_in, bit):
    size = lax.axis_size("dp")
    return lax.ppermute(values_in, "dp", [(i, i ^ (1 << bit)) for i in range(size)])


def bit_orders():
    bits = lax.axis_size("dp").bit_length() - 1
    high = list(range(1, bits))
    return [0] + high, [0] + high[::-1]


def after(values_in, *others):
    return lax.optimization_barrier((values_in,) + others)[0]


def gather_offsets(half):
    first, second = ((4, 2), (2, 4))[half]
    return [(0, first), (second, first | second), (1, first | 1), (second | 1, first | second | 1)]


def gather_start(block, half, *beside):
    bit = bit_orders()[half][2]
    return jnp.stack([after(block, *beside) if beside else block, swap_dp(block, bit)])


def gather_rest(pair, half, *beside):
    others = swap_dp(pair, bit_orders()[half][1])
    if beside:
        others = after(others, *beside)
    return [pair, others, swap_dp(pair, 0), swap_dp(others, 0)]


def split_blocks(pieces, axis, rows, *beside):
    out = []
    for half in range(2):
        part = lax.slice_in_dim(pieces, half * rows, (half + 1) * rows, axis=axis)
        out.extend(gather_rest(gather_start(part, half), half, *beside))
    return out


def add_across(part, bit, *beside):
    keep = after(part[0], *beside) if beside else part[0]
    return (keep.astype(F32) + swap_dp(part[1], bit).astype(F32)).astype(BF16)


def sum_groups(mine):
    total = mine[0].astype(F32)
    for k in range(1, lax.axis_size("mp")):
        total = total + shift_mp(mine[k], -k).astype(F32)
    return total


def own_group(grads):
    return lax.psum(sum_groups(grads), "dp")


def each_block(here, blocks):
    for half in range(2):
        for n, offsets in enumerate(gather_offsets(half)):
            for i, offset in enumerate(offsets):
                yield blocks[4 * half + n].at[i], half, here ^ offset


def place_feed_kernel(here_ref, *refs):
    *blocks, expand_ref, reduce_ref = refs
    share = blocks[0].shape[1]
    for block, half, index in each_block(here_ref[0], blocks):
        place = pl.ds(pl.multiple_of(index * share, share), share)
        if half == 0:
            expand_ref[:, place] = block[...].astype(F32).T
        else:
            reduce_ref[place, :] = block[...].astype(F32)


def place_input_kernel(here_ref, *refs):
    *blocks, input_ref, output_ref, full_ref = refs
    rows = blocks[0].shape[2]
    parts = full_ref.shape[0]
    for block, half, index in each_block(here_ref[0], blocks):
        place = pl.ds(pl.multiple_of((index * 2 + half) * rows, rows), rows)
        full_ref[:, place, :] = block[:parts].astype(F32)
        output_ref[place, :] = block[parts].astype(F32)
    for p in range(parts):
        input_ref[p] = full_ref[p].T


def sum_dp(values_in):
    for bit in range(lax.axis_size("dp").bit_length() - 1):
        values_in = values_in + swap_dp(values_in, bit)
    return values_in


def contract_rows(left, right):
    return lax.dot_general(left, right, (((0,), (0,)), ((), ())), preferred_element_type=F32)


def contract_cols(left, right):
    return lax.dot_general(left, right, (((1,), (1,)), ((), ())), preferred_element_type=F32)


def gelu_parts(value):
    factor = math.sqrt(2.0 / math.pi)
    square = value * value
    tanh_part = jnp.tanh(factor * value * (1.0 + 0.044715 * square))
    half = 0.5 * (1.0 + tanh_part)
    slope = half + 0.5 * value * (1.0 - tanh_part * tanh_part) * (
        factor * (1.0 + 3.0 * 0.044715 * square)
    )
    return value * half, slope


ROW_STEP = 32
SMALL_ROWS = 32


def fold_rows(wide_ref, narrow_ref):
    channels = narrow_ref.shape[1]
    for i in range(wide_ref.shape[1] // channels):
        narrow_ref[8 * i : 8 * i + 8, :] = wide_ref[:, i * channels : (i + 1) * channels]


def unfold_rows(narrow):
    rows, channels = narrow.shape
    return narrow.reshape(rows // 8, 8, channels).transpose(1, 0, 2).reshape(8, -1)


def store_grad(refs, k, part, here, values):
    rows = values.shape[0] // 8
    for i in range(4):
        bit1, bit2 = (i & 1) ^ (here >> 1 & 1), (i >> 1) ^ (here >> 2)
        first, second = (bit2, bit1) if k < 2 else (bit1, bit2)
        pair = [values[(2 * i + n) * rows : (2 * i + n + 1) * rows].astype(BF16) for n in range(2)]
        even = here & 1 == 0
        refs[0][k // 2, first, second, part] = jnp.where(even, pair[0], pair[1])
        refs[1][k // 2, first, second, part] = jnp.where(even, pair[1], pair[0])


def start_input_weights(here_ref, local, blocks, weight_ref, sem):
    others = pl.ds(1, weight_ref.shape[0] - 1)
    pltpu.make_async_copy(local, weight_ref.at[0], sem).start()
    if len(blocks) == 1:
        pltpu.make_async_copy(blocks[0], weight_ref.at[others], sem).start()
        return
    rows = blocks[0].shape[3]
    for block, half, index in each_block(here_ref[0], blocks):
        start = pl.multiple_of((index * 2 + half) * rows, rows)
        pltpu.make_async_copy(block, weight_ref.at[others, :, pl.ds(start, rows)], sem).start()


def group_at(here_ref, k, groups):
    return lax.rem(here_ref[1] + (groups - k), groups)


def wait_whole(ref, sem):
    pltpu.make_async_copy(ref, ref, sem).wait()


def enter_kernel(count, here_ref, input_ref, halo_ref, vectors_ref, small_ref, local_ref, *refs):
    blocks = refs[:count]
    conv_input_ref, second_ref, gates_ref, projected_ref, normed_ref = refs[count : count + 5]
    weight_ref, rows_ref, sem = refs[count + 5 :]
    rows = input_ref.shape[0]
    groups, _, channels = conv_input_ref.shape
    start_input_weights(here_ref, local_ref, blocks, weight_ref, sem)

    def normed(values):
        return (norm_parts(values)[0] * vectors_ref[0:1] + vectors_ref[1:2]).astype(BF16)

    rows_ref[:CHUNK, :] = normed(halo_ref[...])

    def norm_step(i, carry):
        start = pl.multiple_of(i * ROW_STEP, ROW_STEP)
        values = normed(input_ref[pl.ds(start, ROW_STEP), :])
        normed_ref[pl.ds(start, ROW_STEP), :] = values
        rows_ref[pl.ds(start + CHUNK, ROW_STEP), :] = values
        return carry

    lax.fori_loop(0, rows // ROW_STEP, norm_step, 0)
    wait_whole(weight_ref, sem)
    row = lax.broadcasted_iota(jnp.int32, (rows + CHUNK, channels), 0)
    begins = (row < CHUNK) & (here_ref[1] == 0)
    for k in range(groups):
        mixed = []
        for p in range(3):
            small = small_ref[k, 8 * p : 8 * p + 8, :]
            values = contract_cols(rows_ref[...], weight_ref[k, p]) + small[0:1]
            values = jnp.where(begins, 0.0, values)
            projected_ref[k, p] = values.astype(BF16)
            mixed.append(
                small[1:2] * values[CHUNK:]
                + small[2:3] * values[CHUNK - 1 : -1]
                + small[3:4] * values[CHUNK - 2 : -2]
                + small[4:5]
            )
        group = group_at(here_ref, k, groups)
        conv_input_ref[group] = (mixed[1] * mixed[0]).astype(BF16)
        gates_ref[k, 0] = mixed[0].astype(BF16)
        gates_ref[k, 1] = mixed[1].astype(BF16)
        second_ref[k] = mixed[2].astype(BF16)


def enter(here, block_input, halo, vectors, small, local, blocks):
    rows, width = block_input.shape
    parts, channels, _ = local.shape
    groups = small.shape[0]
    outs = [
        ((groups, rows, channels), BF16),
        ((groups, rows, channels), BF16),
        ((groups, 2, rows, channels), BF16),
        ((groups, parts, rows + CHUNK, channels), BF16),
        ((rows, width), BF16),
    ]
    return kernel_call(
        functools.partial(enter_kernel, len(blocks)),
        "enter",
        outs,
        [SMEM_SPEC] + [VMEM_SPEC] * 4 + [ANY_SPEC] * (1 + len(blocks)),
        [
            pltpu.VMEM((groups, parts, channels, width), BF16),
            pltpu.VMEM((rows + CHUNK, width), BF16),
            pltpu.SemaphoreType.DMA,
        ],
        2 * rows * width * parts * groups * channels,
        16,
        40,
        (here, block_input, halo, vectors, small, local, *blocks),
    )


def middle_kernel(count, sorted_units, here_ref, *refs):
    long_ref, conv_ref, second_ref, input_ref, cot_ref, vectors_ref, small_ref, bias_ref = refs[:8]
    expand_local, reduce_local, output_local = refs[8:11]
    blocks = refs[11 : 11 + count]
    (
        result_ref,
        hidden_grad_ref,
        conv_grad_ref,
        second_grad_ref,
        gated_ref,
        act_ref,
        pre_grad_ref,
        normed_ref,
        mix_ref,
        out_low_ref,
        bias_grad_ref,
        all_sums_ref,
        skip_grad_ref,
    ) = refs[11 + count : 24 + count]
    expand_ref, reduce_ref, output_ref, normal_ref, scale_ref, sums_ref, sems = refs[
        24 + count : 31 + count
    ]
    early_outs = (act_ref, pre_grad_ref, normed_ref, out_low_ref)
    act_ref, pre_grad_ref, normed_ref, out_low_ref, out_sems = refs[31 + count :]
    stores = [
        pltpu.make_async_copy(source, target, out_sems.at[n])
        for n, (source, target) in enumerate(
            zip((act_ref, pre_grad_ref, normed_ref, out_low_ref), early_outs)
        )
    ]
    rows, width = input_ref.shape
    groups, hidden, _ = expand_ref.shape
    channels = output_ref.shape[1]
    others = pl.ds(1, groups - 1)
    here = here_ref[0]

    pltpu.make_async_copy(output_local, output_ref.at[0], sems.at[0]).start()
    pltpu.make_async_copy(expand_local, expand_ref.at[0], sems.at[1]).start()
    pltpu.make_async_copy(reduce_local, reduce_ref.at[0], sems.at[2]).start()
    if sorted_units:
        share = hidden // 8
        half_share = channels // 16
        for block, half, index in each_block(here, blocks):
            ref = (expand_ref, reduce_ref)[half]
            start = pl.multiple_of((index * 2 + half) * half_share, half_share)
            pltpu.make_async_copy(
                block.at[:, pl.ds(share, half_share)],
                output_ref.at[others, pl.ds(start, half_share)],
                sems.at[0],
            ).start()
            start = pl.multiple_of(index * share, share)
            pltpu.make_async_copy(
                block.at[:, pl.ds(0, share)],
                ref.at[others, pl.ds(start, share)],
                sems.at[1 + half],
            ).start()
    else:
        for n, (block, ref) in enumerate(zip(blocks, (output_ref, expand_ref, reduce_ref))):
            pltpu.make_async_copy(block, ref.at[others], sems.at[n]).start()

    position = here_ref[1] * rows + lax.broadcasted_iota(jnp.int32, (rows, channels), 0)
    mask = jnp.where(position < here_ref[2], 1.0, 0.0)

    def conv_out(k):
        skip = small_ref[k, 24:25, :]
        group = group_at(here_ref, k, groups)
        return long_ref[group].astype(F32) + skip * conv_ref[group].astype(F32)

    for k in range(groups):
        gated = mask * second_ref[k].astype(F32) * conv_out(k)
        gated_ref[:, k * channels : (k + 1) * channels] = gated.astype(BF16)
    wait_whole(output_ref, sems.at[0])
    mixed = times(gated_ref[...], output_ref[...].reshape(groups * channels, width))
    result_ref[...] = input_ref[...] + mixed + vectors_ref[0:1]
    sums_ref[...] = jnp.zeros_like(sums_ref)

    def norm_step(i, carry):
        part = pl.ds(pl.multiple_of(i * ROW_STEP, ROW_STEP), ROW_STEP)
        values = result_ref[part, :]
        normal, scale = norm_parts(values)
        normal_ref[part, :] = normal
        scale_ref[part, :] = scale
        normed_ref[part, :] = (normal * vectors_ref[1:2] + vectors_ref[2:3]).astype(BF16)
        cot = cot_ref[part, :]
        out_low_ref[part, :] = cot.astype(BF16)
        result_ref[part, :] = values + vectors_ref[3:4]
        hidden_grad_ref[part, :] = jnp.zeros_like(cot)
        sums_ref[0:1, :] += jnp.sum(cot, axis=0, keepdims=True)
        return carry

    lax.fori_loop(0, rows // ROW_STEP, norm_step, 0)
    wait_whole(expand_ref, sems.at[1])
    wait_whole(reduce_ref, sems.at[2])
    per_step = hidden // 2

    def store_units(ref, k, half, values):
        if not sorted_units:
            start = pl.multiple_of((lax.rem(k, 2) * 2 + half) * per_step, per_step)
            ref[k // 2, :, pl.ds(start, per_step)] = values
            return
        share = hidden // 8
        for i in range(4):
            bit0 = (here & 1) ^ (i & 1)
            bit1 = ((here >> 1) & 1) ^ (i >> 1)
            bit2 = ((here >> 2) & 1) ^ half
            outer = jnp.where(k < 2, bit2 * 2 + bit1, bit1 * 2 + bit2)
            start = ((k // 2 * 4 + outer) * 2 + lax.rem(k, 2)) * share
            columns = pl.ds(pl.multiple_of(start, share), share)
            ref[bit0, :, columns] = values[:, i * share : (i + 1) * share]

    def hidden_step(j, carry):
        k, half = j // 2, lax.rem(j, 2)
        units = pl.ds(pl.multiple_of(half * per_step, per_step), per_step)
        expand = expand_ref[k, units, :]
        reduce = reduce_ref[k, units, :]
        value, slope = gelu_parts(contract_cols(normed_ref[...], expand) + bias_ref[j])
        value = value.astype(BF16)
        store_units(act_ref, k, half, value)
        result_ref[...] += times(value, reduce)
        grad = (contract_cols(out_low_ref[...], reduce) * slope).astype(BF16)
        store_units(pre_grad_ref, k, half, grad)
        bias_grad_ref[j] = jnp.sum(grad.astype(F32), axis=0, keepdims=True)
        hidden_grad_ref[...] += times(grad, expand)
        return carry

    lax.fori_loop(0, 2 * groups, hidden_step, 0)
    for copy in stores:
        copy.start()

    def back_step(i, carry):
        part = pl.ds(pl.multiple_of(i * ROW_STEP, ROW_STEP), ROW_STEP)
        res_part, gain_sum, shift_sum = norm_back(
            normal_ref[part, :], scale_ref[part, :], vectors_ref[1:2], hidden_grad_ref[part, :]
        )
        hidden_grad = cot_ref[part, :] + res_part
        hidden_grad_ref[part, :] = hidden_grad
        mix_ref[part, :] = hidden_grad.astype(BF16)
        sums_ref[1:2, :] += gain_sum[None]
        sums_ref[2:3, :] += shift_sum[None]
        sums_ref[3:4, :] += jnp.sum(hidden_grad, axis=0, keepdims=True)
        return carry

    lax.fori_loop(0, rows // ROW_STEP, back_step, 0)
    fold_rows(sums_ref, all_sums_ref)
    for k in range(groups):
        group = group_at(here_ref, k, groups)
        masked_grad = contract_cols(mix_ref[...], output_ref[k]) * mask
        second_grad_ref[k] = (masked_grad * conv_out(k)).astype(BF16)
        conv_grad = (masked_grad * second_ref[k].astype(F32)).astype(BF16)
        conv_grad_ref[group] = conv_grad
        products = conv_grad.astype(F32) * conv_ref[group].astype(F32)
        skip_grad_ref[k] = jnp.sum(products, axis=0, keepdims=True)
    for copy in stores:
        copy.wait()


def grad_shapes(groups, channels, width, split, parts):
    if split:
        return [((2, 2, 2, groups // 2 * parts, channels // 8, width), BF16)] * 2
    return [((groups * parts, channels, width), BF16), ((8, 128), BF16)]


def middle(
    here, long_out, conv_input, second, block_input, cotangent, vectors, small, bias, local, blocks
):
    rows, width = block_input.shape
    groups, _, channels = small.shape
    hidden = local[0].shape[0]
    grouped = ((groups, rows, channels), BF16)
    square = ((rows, width), BF16)
    wide = ((2, rows, groups * hidden // 2), BF16)
    outs = (
        [((rows, width), F32)] * 2
        + [grouped, grouped, square, wide, wide, square, square, square]
        + [((2 * groups, 1, hidden // 2), F32)]
        + [((8 * width // channels, channels), F32), ((groups, 1, channels), F32)]
    )
    return kernel_call(
        functools.partial(middle_kernel, len(blocks), len(blocks) == 8),
        "middle",
        outs,
        [SMEM_SPEC] + [VMEM_SPEC] * 8 + [ANY_SPEC] * (3 + len(blocks)),
        [
            pltpu.VMEM((groups, hidden, width), BF16),
            pltpu.VMEM((groups, hidden, width), BF16),
            pltpu.VMEM((groups, channels, width), BF16),
            pltpu.VMEM((rows, width), F32),
            pltpu.VMEM((rows, 1), F32),
            pltpu.VMEM((8, width), F32),
            pltpu.SemaphoreType.DMA((3,)),
            pltpu.VMEM(wide[0], BF16),
            pltpu.VMEM(wide[0], BF16),
            pltpu.VMEM((rows, width), BF16),
            pltpu.VMEM((rows, width), BF16),
            pltpu.SemaphoreType.DMA((4,)),
        ],
        20_000_000_000,
        48,
        62,
        (
            here,
            long_out,
            conv_input,
            second,
            block_input,
            cotangent,
            vectors,
            small,
            bias,
            *local,
            *blocks,
        ),
        copied=(5, 6, 7, 9),
    )


def leave_kernel(count, here_ref, *refs):
    (
        du_ref,
        conv_grad_ref,
        halo_gates_ref,
        halo_grads_ref,
        small_ref,
        vectors_ref,
        normed_ref,
        gated_ref,
        mix_ref,
        skip_grad_ref,
        bias_grad_ref,
        second_grad_any,
        gates_any,
        projected_any,
        input_any,
        hidden_grad_any,
        local_ref,
    ) = refs[:17]
    blocks = refs[17 : 17 + count]
    input_grad_ref, small_grad_ref, all_sums_ref, *weight_outs = refs[17 + count : 22 + count]
    low_ref, weight_ref, sums_ref, sem, *rest = refs[22 + count :]
    second_grad_ref, gates_ref, projected_ref, input_ref, hidden_grad_ref = rest[:5]
    sems, out_sems = rest[5:7]
    weight_grads = rest[7:]
    rows, width = input_ref.shape
    groups = small_ref.shape[0]
    channels = small_ref.shape[2]
    loads = [
        [
            pltpu.make_async_copy(source.at[k], target.at[k], sems.at[n, k])
            for n, (source, target) in enumerate(
                (
                    (second_grad_any, second_grad_ref),
                    (gates_any, gates_ref),
                    (projected_any, projected_ref),
                )
            )
        ]
        for k in range(groups)
    ]
    late_loads = [
        pltpu.make_async_copy(input_any, input_ref, sems.at[3, 0]),
        pltpu.make_async_copy(hidden_grad_any, hidden_grad_ref, sems.at[3, 1]),
    ]
    for copy in loads[0] + loads[1]:
        copy.start()
    start_input_weights(here_ref, local_ref, blocks, weight_ref, sem)
    for copy in loads[2] + loads[3] + late_loads:
        copy.start()
    row = lax.broadcasted_iota(jnp.int32, (rows + CHUNK, channels), 0)
    ends = (row >= rows) & (here_ref[1] == groups - 1)
    small_grad_ref[...] = jnp.zeros_like(small_grad_ref)

    def keep_grad(k, p, weight_grad):
        if count > 1:
            store_grad(weight_grads, k, k % 2 * 4 + p, here_ref[0], weight_grad)
        else:
            weight_grads[0][4 * k + p] = weight_grad.astype(BF16)

    for k in range(groups):
        nk = (k + 1) % groups
        for copy in loads[k]:
            copy.wait()

        def extended(values, halo):
            return jnp.concatenate([values, halo], axis=0).astype(F32)

        group = group_at(here_ref, k, groups)
        conv_grad = extended(conv_grad_ref[group], halo_grads_ref[0, group])
        skip = small_ref[k, 24:25, :]
        input_side = du_ref[group].astype(F32) + skip * conv_grad
        grads = (
            input_side * extended(gates_ref[k, 1], halo_gates_ref[nk, 1]),
            input_side * extended(gates_ref[k, 0], halo_gates_ref[nk, 0]),
            extended(second_grad_ref[k], halo_grads_ref[1, nk]),
        )
        for p, grad in enumerate(grads):
            grad = jnp.where(ends, 0.0, grad)
            small = small_ref[k, 8 * p : 8 * p + 8, :]
            low = (
                small[1:2] * grad[:rows]
                + small[2:3] * grad[1 : rows + 1]
                + small[3:4] * grad[2 : rows + 2]
            ).astype(BF16)
            low_ref[:, (3 * k + p) * channels : (3 * k + p + 1) * channels] = low
            keep_grad(k, p, contract_rows(low, normed_ref[...]))
            projected = projected_ref[k, p].astype(F32)
            own = grad[:rows]
            small_grad_ref[k, 8 * p : 8 * p + 1, :] = jnp.sum(
                low.astype(F32), axis=0, keepdims=True
            )
            for tap in range(3):
                delayed = projected[CHUNK - tap : rows + CHUNK - tap]
                small_grad_ref[k, 8 * p + 1 + tap : 8 * p + 2 + tap, :] = jnp.sum(
                    own * delayed, axis=0, keepdims=True
                )
            small_grad_ref[k, 8 * p + 4 : 8 * p + 5, :] = jnp.sum(own, axis=0, keepdims=True)
        gated = gated_ref[:, k * channels : (k + 1) * channels]
        keep_grad(k, 3, contract_rows(gated, mix_ref[...]))
        small_grad_ref[k, 24:25, :] = skip_grad_ref[k]
        per_half = bias_grad_ref.shape[2] // channels
        for n in range(2 * per_half):
            bias_row = bias_grad_ref[2 * k + n // per_half]
            first = n % per_half * channels
            small_grad_ref[k, 25 + n : 26 + n, :] = bias_row[:, first : first + channels]
        if count > 1 and k % 2 == 1:
            for n in range(2):
                pltpu.make_async_copy(
                    weight_grads[n].at[k // 2], weight_outs[n].at[k // 2], out_sems.at[n, k // 2]
                ).start()
    if count == 1:
        for n in range(2):
            pltpu.make_async_copy(weight_grads[n], weight_outs[n], out_sems.at[n, 0]).start()
    wait_whole(weight_ref, sem)
    input_grad_ref[...] = times(
        low_ref[...], weight_ref[...].reshape(groups * 3 * channels, width)
    )
    sums_ref[...] = jnp.zeros_like(sums_ref)
    for copy in late_loads:
        copy.wait()

    def back_step(i, carry):
        part = pl.ds(pl.multiple_of(i * ROW_STEP, ROW_STEP), ROW_STEP)
        normal, scale = norm_parts(input_ref[part, :])
        input_part, gain_sum, shift_sum = norm_back(
            normal, scale, vectors_ref[0:1], input_grad_ref[part, :]
        )
        input_grad_ref[part, :] = hidden_grad_ref[part, :] + input_part
        sums_ref[0:1, :] += gain_sum[None]
        sums_ref[1:2, :] += shift_sum[None]
        return carry

    lax.fori_loop(0, rows // ROW_STEP, back_step, 0)
    fold_rows(sums_ref, all_sums_ref)
    for n in range(2):
        if count > 1:
            for half in range(2):
                pltpu.make_async_copy(
                    weight_grads[n].at[half], weight_outs[n].at[half], out_sems.at[n, half]
                ).wait()
        else:
            pltpu.make_async_copy(weight_grads[n], weight_outs[n], out_sems.at[n, 0]).wait()


def leave(
    here,
    conv_input_grad,
    conv_grad,
    second_grad,
    gates,
    projected,
    halo_gates,
    halo_grads,
    small,
    block_input,
    hidden_grad,
    vectors,
    normed,
    gated,
    mix_low,
    skip_grad,
    bias_grad,
    local,
    blocks,
):
    rows, width = block_input.shape
    groups, _, channels = small.shape
    grads = grad_shapes(groups, channels, width, len(blocks) > 1, 4)
    outs = [
        ((rows, width), F32),
        ((groups, SMALL_ROWS, channels), F32),
        ((8 * width // channels, channels), F32),
        *grads,
    ]
    return pl.pallas_call(
        functools.partial(leave_kernel, len(blocks)),
        out_shape=tuple(jax.ShapeDtypeStruct(shape, dtype) for shape, dtype in outs),
        in_specs=[SMEM_SPEC] + [VMEM_SPEC] * 11 + [HBM_SPEC] * 5 + [ANY_SPEC] * (1 + len(blocks)),
        out_specs=(VMEM_SPEC,) * 3 + (HBM_SPEC,) * 2,
        scratch_shapes=[
            pltpu.VMEM((rows, 3 * groups * channels), BF16),
            pltpu.VMEM((groups, 3, channels, width), BF16),
            pltpu.VMEM((8, width), F32),
            pltpu.SemaphoreType.DMA,
            *[
                pltpu.VMEM(a.shape, a.dtype)
                for a in (second_grad, gates, projected, block_input, hidden_grad)
            ],
            pltpu.SemaphoreType.DMA((4, groups)),
            pltpu.SemaphoreType.DMA((2, 2)),
            *[pltpu.VMEM(shape, dtype) for shape, dtype in grads],
        ],
        compiler_params=pltpu.CompilerParams(vmem_limit_bytes=60 << 20),
        cost_estimate=pl.CostEstimate(
            flops=16_000_000_000, bytes_accessed=34 << 20, transcendentals=0
        ),
        name="leave",
    )(
        here,
        conv_input_grad,
        conv_grad,
        halo_gates,
        halo_grads,
        small,
        vectors,
        normed,
        gated,
        mix_low,
        skip_grad,
        bias_grad,
        second_grad,
        gates,
        projected,
        block_input,
        hidden_grad,
        local,
        *blocks,
    )


def per_device(
    block_input,
    lengths,
    mixer_gain,
    mixer_shift,
    input_weight,
    input_bias,
    conv_weight,
    conv_bias,
    enter_weight,
    enter_bias,
    middle_weight,
    middle_bias,
    inner_weight,
    inner_bias,
    frequency,
    filter_weight,
    skip_scale,
    output_weight,
    output_bias,
    feed_gain,
    feed_shift,
    expand_weight,
    expand_bias,
    reduce_weight,
    reduce_bias,
    cotangent,
):
    own_rows, width = block_input.shape
    channels = input_weight.shape[2]
    hidden = expand_weight.shape[1]
    mp_size = lax.axis_size("mp")
    dp_size = lax.axis_size("dp")
    mp_here = lax.axis_index("mp")
    dp_here = lax.axis_index("dp")
    seq_len = own_rows * mp_size
    split = dp_size == 8
    share = hidden // dp_size
    out_share = channels // dp_size
    here = jnp.stack([dp_here, mp_here, lengths[0]]).astype(jnp.int32)

    small_own = jnp.concatenate(
        [
            jnp.concatenate(
                [input_bias[:, None], conv_weight.transpose(1, 0, 2), conv_bias[:, None]]
                + [jnp.zeros((3, 3, channels), F32)],
                axis=1,
            ).reshape(24, channels),
            skip_scale[None],
            expand_bias.reshape(-1, channels),
        ]
    )
    small_own = jnp.pad(small_own, ((0, SMALL_ROWS - small_own.shape[0]), (0, 0)))

    def other_groups(values):
        return jnp.stack([shift_mp(values, k) for k in range(1, mp_size)])

    def turned_groups(stacked, start, sign):
        return jnp.concatenate(
            [
                lax.dynamic_slice_in_dim(stacked, (mp_here + sign * k) % mp_size, 1, 0)
                for k in range(start, mp_size)
            ]
        )

    features = position_features(seq_len, enter_weight.shape[0])
    columns = jnp.stack([enter_bias, middle_bias, inner_bias, frequency], axis=1)
    net_units = frequency.shape[0]
    net_shape = ((3, net_units, seq_len), F32)
    taps_low, *net_values = kernel_call(
        functools.partial(filter_kernel, width),
        "filter_taps",
        [((seq_len, channels), BF16)] + [net_shape] * 3,
        [SMEM_SPEC] + [VMEM_SPEC] * 6,
        [],
        4_000_000_000,
        6,
        32,
        (
            here,
            features,
            jnp.pad(enter_weight, ((0, FEATURE_ROWS - enter_weight.shape[0]), (0, 0))),
            middle_weight,
            inner_weight,
            columns,
            filter_weight,
        ),
    )
    small_rows = jnp.concatenate([small_own, block_input[-CHUNK:].reshape(-1, channels)])
    small_rows = jnp.stack([small_rows] + [shift_mp(small_rows, k) for k in range(1, mp_size)])
    small = small_rows[:, :SMALL_ROWS]
    halo = small_rows[1, SMALL_ROWS:].reshape(CHUNK, width)

    input_turned = input_weight.transpose(1, 2, 0)
    expand_turned = expand_weight.T
    if split:
        input_part = lax.dynamic_slice_in_dim(input_turned, dp_here * out_share, out_share, 1)
        input_pieces = after(other_groups(input_part), small_rows)
        input_blocks = split_blocks(input_pieces, 2, out_share // 2)
    else:
        input_blocks = [other_groups(input_turned)]
    tables = spectral_tables(seq_len)

    if split:
        expand_part = lax.dynamic_slice_in_dim(expand_turned, dp_here * share, share, 0)
        reduce_part = lax.dynamic_slice_in_dim(reduce_weight, dp_here * share, share, 0)
        output_part = lax.dynamic_slice_in_dim(output_weight, dp_here * out_share, out_share, 0)
        half = out_share // 2
        feed_part = jnp.concatenate(
            [expand_part, output_part[:half], reduce_part, output_part[half:]]
        )
        feed_groups = lax.all_gather(after(feed_part, input_pieces), "mp")
    else:
        feed_blocks = [other_groups(w) for w in (output_weight, expand_turned, reduce_weight)]

    mixer_vectors = jnp.stack([mixer_gain, mixer_shift])
    conv_input, second_gate, gates, projected, mixer_normed = enter(
        here,
        block_input,
        halo,
        mixer_vectors,
        small,
        input_turned,
        input_blocks,
    )
    halo_gates = shift_mp(gates[:, :, :CHUNK], -1)

    def exchange(values):
        return lax.all_to_all(values, "mp", 0, 0)

    arrived_input = exchange(conv_input)
    if split:
        feed_pieces = turned_groups(after(feed_groups, conv_input), 1, -1)
        halves = (feed_pieces[:, : share + half], feed_pieces[:, share + half :])
        pairs = [gather_start(part, n, arrived_input) for n, part in enumerate(halves)]
        arrived_input = after(arrived_input, *pairs)
    long_out, spec_u, spec_t = long_conv(tables, arrived_input, taps_low)
    long_out = after(exchange(long_out), halo_gates)
    if split:
        feed_blocks = [
            block for n, pair in enumerate(pairs) for block in gather_rest(pair, n, long_out)
        ]
    vectors = jnp.stack([output_bias, feed_gain, feed_shift, reduce_bias])
    bias = small[:, 25 : 25 + hidden // channels].reshape(2 * mp_size, 1, hidden // 2)
    (
        result,
        hidden_grad,
        conv_grad,
        second_grad,
        gated,
        activated,
        pre_grad,
        feed_normed,
        mix_low,
        out_low,
        bias_grad,
        feed_sums,
        skip_grad,
    ) = middle(
        here,
        long_out,
        conv_input,
        second_gate,
        block_input,
        cotangent,
        vectors,
        small,
        bias,
        (expand_turned, reduce_weight, output_weight),
        feed_blocks,
    )
    halo_grads = shift_mp(jnp.stack([conv_grad[:, :CHUNK], second_grad[:, :CHUNK]]), -1)
    arrived_grad = exchange(conv_grad)

    if split:
        pairs = ((activated, out_low), (pre_grad, feed_normed))
    else:
        def feed_grads(left, right):
            grads = [contract_rows(part, right).astype(BF16) for part in left]
            return own_group(jnp.concatenate(grads).reshape(mp_size, hidden, width))

        reduce_weight_grad = feed_grads(activated, out_low)
        expand_weight_grad = feed_grads(pre_grad, feed_normed).T

    arrived_grad = after(arrived_grad, halo_grads)
    conv_input_grad, taps_grad = long_conv_back(tables, arrived_grad, spec_u, spec_t)
    if split:
        late = [(after(u, taps_grad), right) for u, right in pairs]
        arrived = [
            swap_dp(contract_rows(u[1], right).astype(BF16), 0) for u, right in (pairs[0], late[1])
        ]
        pairs = late
        kept = [
            (contract_rows(u[0], right) + other.astype(F32)).astype(BF16)
            for (u, right), other in zip(pairs, arrived)
        ]
        held = [k.reshape(2, 2, 2, mp_size // 2, share, width) for k in kept]
        first_stages = [
            [jnp.stack([h[n, i] for h in held], axis=1) for i in range(2)] for n in range(2)
        ]
    conv_input_grad = exchange(conv_input_grad)
    if split:
        conv_input_grad = after(
            conv_input_grad, halo_grads, first_stages[0][1], first_stages[1][1]
        )
    input_grad, small_grad, mixer_sums, grads_kept, grads_away = leave(
        here,
        conv_input_grad,
        conv_grad,
        second_grad,
        gates,
        projected,
        halo_gates,
        halo_grads,
        small,
        block_input,
        hidden_grad,
        mixer_vectors,
        mixer_normed,
        gated,
        mix_low,
        skip_grad,
        bias_grad,
        input_turned,
        input_blocks,
    )
    if split:
        held = (grads_kept.astype(F32) + swap_dp(grads_away, 0).astype(F32)).astype(BF16)
        taps_grad = after(taps_grad, held)
    else:
        taps_grad = after(taps_grad, grads_kept)
    net_grads, filter_weight_grad = kernel_call(
        functools.partial(filter_back_kernel, width),
        "filter_back",
        [((net_units, 4 * net_units), F32), ((net_units, channels), F32)],
        [SMEM_SPEC] + [VMEM_SPEC] * 9,
        [pltpu.VMEM((net_units, seq_len), F32)],
        8_000_000_000,
        6,
        32,
        (
            here,
            features,
            middle_weight,
            inner_weight,
            columns,
            filter_weight,
            *net_values,
            taps_grad,
        ),
    )
    packed = [net_grads, feed_sums, mixer_sums, filter_weight_grad]
    packed.append(small_grad.reshape(-1, channels))
    ends = [sum(p.shape[0] for p in packed[:n]) for n in range(len(packed) + 1)]
    packed = jnp.concatenate(packed)
    def small_sums(summed):
        by_group = summed[ends[4] :].reshape(mp_size, SMALL_ROWS, channels)
        return sum_groups(
            [jnp.concatenate([summed[: ends[3]], by_group[k]]) for k in range(mp_size)]
        )

    if split:
        stages = [
            add_across(part, bit, small_grad) for part, bit in zip(first_stages, (2, 1))
        ]
        stages = [add_across(part, bit) for part, bit in zip(stages, (1, 2))]
        feed_grads = jnp.concatenate(stages, axis=1).transpose(1, 0, 2, 3)
        feed_grads = turned_groups(feed_grads, 0, -1).reshape(-1, width)
        feed_total = lax.psum_scatter(feed_grads, "mp", scatter_dimension=0, tiled=True)
        held = [add_across(held[0], 2, net_grads), add_across(held[1], 1, net_grads)]
        packed = after(packed, *held)
        held = [add_across(held[0], 1), add_across(held[1], 2)]
        feed_total = after(feed_total, *held)
        mine = jnp.concatenate(held).reshape(mp_size, 4, out_share, width)
        mine = turned_groups(mine, 0, -1).reshape(-1, width)
        input_total = lax.psum_scatter(mine, "mp", scatter_dimension=0, tiled=True)
        input_total = input_total.reshape(4, out_share, width)
        reduce_total, expand_total = feed_total[:share], feed_total[share:]
        summed = sum_dp(packed)
        blocks = []
        for n, total in enumerate((expand_total, reduce_total)):
            blocks.extend(gather_rest(gather_start(total.astype(BF16), n), n))
        expand_weight_grad, reduce_weight_grad = kernel_call(
            place_feed_kernel,
            "place_feed",
            [((width, hidden), F32), ((hidden, width), F32)],
            [SMEM_SPEC] + [VMEM_SPEC] * len(blocks),
            [],
            0,
            14,
            32,
            (here, *blocks),
        )
        input_total = after(input_total, expand_weight_grad)
        along_mp = small_sums(after(summed, input_total))
        blocks = split_blocks(input_total, 1, out_share // 2, along_mp)
        input_weight_grad, output_weight_grad = kernel_call(
            place_input_kernel,
            "place_input",
            [((3, width, channels), F32), ((channels, width), F32)],
            [SMEM_SPEC] + [VMEM_SPEC] * len(blocks),
            [pltpu.VMEM((3, channels, width), F32)],
            0,
            8,
            24,
            (here, *blocks),
        )
        input_weight_grad = input_weight_grad.transpose(1, 0, 2)
    else:
        input_total = own_group(grads_kept.reshape(mp_size, 4, channels, width))
        input_weight_grad = input_total[:3].transpose(2, 0, 1)
        output_weight_grad = input_total[3]
        summed = sum_dp(packed)
        along_mp = small_sums(summed)

    everywhere, groups_sum = along_mp[: ends[3]], along_mp[ends[3] :]
    net = everywhere[: ends[1]]
    net_bias = net[:, 3 * net_units :].T
    feed_sums = unfold_rows(everywhere[ends[1] : ends[2]])
    mixer_sums = unfold_rows(everywhere[ends[2] : ends[3]])
    parts = groups_sum[:24].reshape(3, 8, channels)
    return (
        result,
        input_grad,
        mixer_sums[0],
        mixer_sums[1],
        input_weight_grad,
        parts[:, 0],
        parts[:, 1:4].transpose(1, 0, 2),
        parts[:, 4],
        net[: enter_weight.shape[0], :net_units],
        net_bias[0],
        net[:, net_units : 2 * net_units],
        net_bias[1],
        net[:, 2 * net_units : 3 * net_units],
        net_bias[2],
        net_bias[3],
        summed[ends[3] : ends[4]],
        groups_sum[24],
        output_weight_grad,
        feed_sums[3],
        feed_sums[1],
        feed_sums[2],
        expand_weight_grad,
        groups_sum[25 : 25 + hidden // channels].reshape(hidden),
        reduce_weight_grad,
        feed_sums[0],
    )


ROWS = P(("dp", "mp"), None)
FIRST = P("mp", None)
SECOND = P(None, "mp")
THIRD = P(None, None, "mp")


def solution(mesh):
    return jax.shard_map(
        per_device,
        mesh=mesh,
        in_specs=(
            ROWS, P("dp"), P(), P(), THIRD, SECOND, THIRD, SECOND,
            P(), P(), P(), P(), P(), P(), P(), SECOND,
            P("mp"), FIRST, P(), P(), P(), SECOND, P("mp"), FIRST, P(), ROWS,
        ),
        out_specs=(
            ROWS, ROWS, P(), P(), THIRD, SECOND, THIRD, SECOND,
            P(), P(), P(), P(), P(), P(), P(), SECOND,
            P("mp"), FIRST, P(), P(), P(), SECOND, P("mp"), FIRST, P(),
        ),
        check_vma=False,
    )
```
